32 devices in a mesh: blk: 4 (over x, core), uly: 2 (over y), batch: 4 (over z).
Axes of the slice: x: 2, y: 2, z: 4, core: 2. Of those that a mesh axis runs over, the one named last changes fastest.
Arguments:
- queries: bfloat16 [4096, 1024], P(('batch', 'blk', 'uly')), parts along dimension 0, may hold values from -10 to 10
- keys: bfloat16 [4096, 1024], P(('batch', 'blk', 'uly')), parts along dimension 0, may hold values from -10 to 10
- values: bfloat16 [4096, 1024], P(('batch', 'blk', 'uly')), parts along dimension 0, may hold values from -6 to 6
- out_grad: bfloat16 [4096, 1024], P(('batch', 'blk', 'uly')), parts along dimension 0, may hold values from -16 to 16
- block_mask: int32 [32, 8], P('batch'), parts along dimension 0, may hold values from 0 to 1, as said below
Outputs:
- query_grad: bfloat16 [4096, 1024], P(('batch', 'blk', 'uly')), parts along dimension 0
- key_grad: bfloat16 [4096, 1024], P(('batch', 'blk', 'uly')), parts along dimension 0
- value_grad: bfloat16 [4096, 1024], P(('batch', 'blk', 'uly')), parts along dimension 0
The draws below stay inside these ranges and needn't reach their ends.
There are 4 independent parts, one for each index of `batch`. The reference program is written for one: setup_inputs(seed, part) draws one part's arguments, and reference() takes and returns one part's arrays. A program takes and returns all parts, laid end to end along the dimension named above; each array names one. Nothing has to cross between parts.
Inputs may be any that keep to these rules, and one draw needn't show every extreme that they name: block_mask[a, b] is 1 for every two blocks a, b of the same cell (cell c holds tokens c * 256 to (c + 1) * 256 - 1); for blocks of different cells it is 1 only where the two cells are neighbours on the closed chain of 4 cells (cell c beside cells c - 1 and c + 1 modulo 4), and 0 for all other pairs.
All inputs are finite; a program needn't handle non-finite values.
Results may differ from the reference program's by a relative error of at most 0.0096.
Values may be sent and summed in bfloat16 or wider, within the bound.
No kernel may reach another device: no remote copies, remote signals or barrier semaphores. Data moves between devices by JAX's collectives and lax.ppermute only.
A program may use at most 64 MiB of HBM per device.

```python
import math
import jax
import jax.numpy as jnp
from jax import lax

HEADS = 8
HEAD_DIM = 128
HD = 1024
GENES = 256
CELLS = 4
TOKENS = 1024


def draw_queries(key, part):
    base_key = jax.random.fold_in(key, 1)
    base = jnp.clip(1.5 * jax.random.normal(base_key, (TOKENS, HEADS * HEAD_DIM), jnp.float32), -9.0, 9.0)
    return base.astype(jnp.bfloat16)


def draw_keys(key, part):
    base_key = jax.random.fold_in(key, 2)
    base = jnp.clip(jax.random.normal(base_key, (TOKENS, HEADS * HEAD_DIM), jnp.float32), -6.0, 6.0)
    return base.astype(jnp.bfloat16)


def draw_block_mask(key, part):
    count = TOKENS // 128
    per_cell = GENES // 128
    blocks = jnp.arange(count, dtype=jnp.int32)
    owner = blocks // per_cell
    inside = blocks % per_cell
    levels = jax.random.randint(jax.random.fold_in(key, 11), (CELLS, 2), 1, 9)
    coins = jax.random.randint(jax.random.fold_in(key, 12), (count, count), 0, 16)
    query_cell = owner[:, None]
    key_cell = owner[None, :]
    right = key_cell == (query_cell + 1) % CELLS
    left = key_cell == (query_cell - 1 + CELLS) % CELLS
    level = jnp.where(right, levels[owner, 0][:, None], levels[owner, 1][:, None])
    cross = (right | left) & (coins < level)
    forced = right & (inside[:, None] == per_cell - 1) & (inside[None, :] == 0)
    if per_cell > 1:
        forced = forced | left & (inside[:, None] == 0) & (inside[None, :] == per_cell - 1)
    same = query_cell == key_cell
    return (same | cross | forced).astype(jnp.int32)


def level_of(rng, shape, split, least, top_value):
    factor_of = 1.0
    for dim, blocks in split:
        heights = jax.random.uniform(jax.random.fold_in(jax.random.fold_in(rng, 6), dim), (blocks,), jnp.float32, least / len(split), top_value / len(split))
        factor_of = factor_of * jnp.repeat(jnp.exp(heights), shape[dim] // blocks).reshape((-1,) + (1,) * (len(shape) - 1 - dim))
    return factor_of


def scatter_about(own_key, dims, width, reach, split=(), kind=jnp.bfloat16):
    factor_of = level_of(own_key, dims, split, -0.22, 0.18) if split else 1.0
    values = jax.random.normal(own_key, dims, jnp.float32) * width * factor_of
    return jnp.minimum(jnp.maximum(values, -reach), reach).astype(kind)


def setup_inputs(seed: int = 0, part: int = 0) -> dict:
    key_of = jax.random.split(jax.random.key(seed), 6)
    part_keys = jax.random.split(jax.random.fold_in(key_of[5], part), 6)
    return {
        "queries": draw_queries(jax.random.fold_in(jax.random.fold_in(key_of[5], part), 71), part),
        "keys": draw_keys(jax.random.fold_in(jax.random.fold_in(key_of[5], part), 71), part),
        "values": scatter_about(part_keys[2], (TOKENS, HD), 1.0, 6.0, ((0, 8),)),
        "out_grad": scatter_about(part_keys[3], (TOKENS, HD), 4.0, 16.0, ((0, 8),)),
        "block_mask": draw_block_mask(jax.random.fold_in(jax.random.fold_in(key_of[5], part), 71), part),
    }


def band_cells(x, axis):
    return jnp.concatenate([jnp.roll(x, 1, axis=0), x, jnp.roll(x, -1, axis=0)], axis=axis)

def widen(mask_blocks):
    return jnp.repeat(jnp.repeat(mask_blocks, 128, axis=1), 128, axis=2)

def reference(queries, keys, values, out_grad, block_mask):
    per_cell = GENES // 128
    scale = 1.0 / math.sqrt(HEAD_DIM)

    def cells(x):
        return x.reshape(CELLS, GENES, HEADS, HEAD_DIM)
    q_cells = cells(queries)
    k_cells = cells(keys)
    v_cells = cells(values)
    g_cells = cells(out_grad)
    grid = (block_mask > 0).reshape(CELLS, per_cell, CELLS, per_cell)
    base = jnp.arange(CELLS, dtype=jnp.int32)
    near = (base[:, None] + jnp.array([-1, 0, 1], dtype=jnp.int32)[None, :]) % CELLS
    row_blocks = grid[base[:, None], :, near, :]
    row_blocks = jnp.transpose(row_blocks, (0, 2, 1, 3)).reshape(CELLS, per_cell, 3 * per_cell)
    row_mask = widen(row_blocks)
    col_blocks = grid[near, :, base[:, None], :].reshape(CELLS, 3 * per_cell, per_cell)
    col_mask = widen(col_blocks)

    def query_side(items):
        q_cell, k_band, v_band, g_cell, mask = items
        scores = jnp.einsum('qhd,khd->hqk', q_cell.astype(jnp.float32), k_band.astype(jnp.float32)) * scale
        scores = jnp.where(mask[None], scores, -1e+30)
        top = lax.optimization_barrier(jnp.max(scores, axis=-1, keepdims=True))
        total = lax.optimization_barrier(jnp.sum(jnp.where(mask[None], jnp.exp(scores - top), 0.0), axis=-1, keepdims=True))
        lse = top + jnp.log(total)
        probs = jnp.where(mask[None], jnp.exp(scores - lse), 0.0)
        dprobs = jnp.einsum('qhd,khd->hqk', g_cell.astype(jnp.float32), v_band.astype(jnp.float32))
        delta = lax.optimization_barrier(jnp.sum(probs * dprobs, axis=-1, keepdims=True))
        dscores = lax.optimization_barrier((probs * (dprobs - delta)).astype(jnp.bfloat16))
        grad = jnp.einsum('hqk,khd->qhd', dscores.astype(jnp.float32), k_band.astype(jnp.float32)) * scale
        return (grad.astype(jnp.bfloat16), lse[..., 0], delta[..., 0])
    q_grad, lse_all, delta_all = lax.map(query_side, (q_cells, band_cells(k_cells, 1), band_cells(v_cells, 1), g_cells, row_mask))

    def key_side(items):
        q_band, g_band, lse_band, delta_band, k_cell, v_cell, mask = items
        scores = jnp.einsum('qhd,khd->hqk', q_band.astype(jnp.float32), k_cell.astype(jnp.float32)) * scale
        probs = jnp.where(mask[None], jnp.exp(scores - lse_band[..., None]), 0.0)
        dprobs = jnp.einsum('qhd,khd->hqk', g_band.astype(jnp.float32), v_cell.astype(jnp.float32))
        dscores = lax.optimization_barrier((probs * (dprobs - delta_band[..., None])).astype(jnp.bfloat16))
        probs_low = lax.optimization_barrier(probs.astype(jnp.bfloat16))
        k_grad = jnp.einsum('hqk,qhd->khd', dscores.astype(jnp.float32), q_band.astype(jnp.float32)) * scale
        v_grad = jnp.einsum('hqk,qhd->khd', probs_low.astype(jnp.float32), g_band.astype(jnp.float32))
        return (k_grad.astype(jnp.bfloat16), v_grad.astype(jnp.bfloat16))
    k_grad, v_grad = lax.map(key_side, (band_cells(q_cells, 1), band_cells(g_cells, 1), band_cells(lse_all, 2), band_cells(delta_all, 2), k_cells, v_cells, col_mask))
    shape = (TOKENS, HEADS * HEAD_DIM)
    return (q_grad.reshape(shape), k_grad.reshape(shape), v_grad.reshape(shape))
```

```python
import math

import jax
import jax.numpy as jnp
from jax import lax
from jax.experimental import pallas as pl
from jax.experimental.pallas import tpu as pltpu
from jax.sharding import PartitionSpec as P

HEAD_DIM = 128
GROUP = ("blk", "uly")
ORDER = (5, 7, 4, 6, 1, 3, 2)


def padded(block, sides, width):
    for axis, dim in sides:
        count = lax.axis_size(axis)
        forward = [(i, i + 1) for i in range(count - 1)]
        forward.append((count - 1, 0))
        backward = [(target, source) for source, target in forward]
        low = lax.ppermute(
            lax.slice_in_dim(block, block.shape[dim] - width, None, axis=dim), axis, forward
        )
        high = lax.ppermute(lax.slice_in_dim(block, 0, width, axis=dim), axis, backward)
        block = jnp.concatenate([low, block, high], axis=dim)
    return block


def passed_along(block, axis, distance):
    devices = range(lax.axis_size(axis))
    route = [((i - distance) % len(devices), i) for i in devices]
    return lax.ppermute(block, axis, route)


def times_t(left, right):
    return lax.dot_general(
        left, right, (((1,), (1,)), ((), ())), preferred_element_type=jnp.float32
    )


def t_times(left, right):
    return lax.dot_general(
        left, right, (((0,), (0,)), ((), ())), preferred_element_type=jnp.float32
    )


def widen_blocks(mask_blocks):
    return jnp.repeat(jnp.repeat(mask_blocks > 0, 128, axis=0), 128, axis=1)


def by_cells(queries, keys, values, out_grad, block_mask):
    local_q, local_k, local_v, local_g = (
        lax.all_to_all(queries, "uly", split_axis=1, concat_axis=0, tiled=True),
        lax.all_to_all(keys, "uly", split_axis=1, concat_axis=0, tiled=True),
        lax.all_to_all(values, "uly", split_axis=1, concat_axis=0, tiled=True),
        lax.all_to_all(out_grad, "uly", split_axis=1, concat_axis=0, tiled=True),
    )
    genes = local_q.shape[0]
    heads_here = local_q.shape[1] // HEAD_DIM
    scale = 1.0 / math.sqrt(HEAD_DIM)
    cells = lax.axis_size("blk")
    here = lax.axis_index("blk")
    per_cell = genes // 128
    near = (here + jnp.array([-1, 0, 1], dtype=jnp.int32) + cells) % cells
    mask_rows = lax.dynamic_slice_in_dim(block_mask, here * per_cell, per_cell, 0).reshape(
        per_cell, cells, per_cell
    )
    row_mask = widen_blocks(jnp.take(mask_rows, near, axis=1).reshape(per_cell, 3 * per_cell))
    pairs = jnp.stack([local_k, local_v], axis=1)
    band = padded(pairs, (("blk", 0),), genes)
    q_grads = []
    k_parts = []
    v_parts = []
    for head in range(heads_here):
        lower = head * HEAD_DIM
        upper = lower + HEAD_DIM
        q_head = local_q[:, lower:upper]
        g_head = local_g[:, lower:upper]
        k_band = band[:, 0, lower:upper]
        v_band = band[:, 1, lower:upper]
        scores = jnp.where(row_mask, times_t(q_head, k_band) * scale, -1e30)
        top = jnp.max(scores, axis=1, keepdims=True)
        total = jnp.sum(jnp.where(row_mask, jnp.exp(scores - top), 0.0), axis=1, keepdims=True)
        lse = top + jnp.log(total)
        probs = jnp.where(row_mask, jnp.exp(scores - lse), 0.0)
        dprobs = times_t(g_head, v_band)
        delta = jnp.sum(probs * dprobs, axis=1, keepdims=True)
        dscores = (probs * (dprobs - delta)).astype(jnp.bfloat16)
        q_grads.append(
            (jnp.dot(dscores, k_band, preferred_element_type=jnp.float32) * scale).astype(
                jnp.bfloat16
            )
        )
        k_parts.append(t_times(dscores, q_head))
        v_parts.append(t_times(probs.astype(jnp.bfloat16), g_head))
    query_grad = jnp.concatenate(q_grads, axis=1)
    partial_terms = jnp.stack(
        [jnp.concatenate(k_parts, axis=1), jnp.concatenate(v_parts, axis=1)], axis=1
    )
    from_next = passed_along(partial_terms[:genes].astype(jnp.bfloat16), "blk", -1).astype(
        jnp.float32
    )
    from_prior = passed_along(partial_terms[2 * genes :].astype(jnp.bfloat16), "blk", 1).astype(
        jnp.float32
    )
    summed = partial_terms[genes : 2 * genes] + from_next + from_prior
    key_grad = (summed[:, 0] * scale).astype(jnp.bfloat16)
    value_grad = summed[:, 1].astype(jnp.bfloat16)
    return (
        lax.all_to_all(query_grad, "uly", split_axis=0, concat_axis=1, tiled=True),
        lax.all_to_all(key_grad, "uly", split_axis=0, concat_axis=1, tiled=True),
        lax.all_to_all(value_grad, "uly", split_axis=0, concat_axis=1, tiled=True),
    )


def flat_index(axes):
    index = 0
    for axis in axes:
        index = index * lax.axis_size(axis) + lax.axis_index(axis)
    return index


def exchange(block, distance):
    devices = lax.axis_size(GROUP)
    return lax.ppermute(block, GROUP, [(i, i ^ distance) for i in range(devices)])


def head_columns(head):
    return pl.ds(pl.multiple_of(head * HEAD_DIM, HEAD_DIM), HEAD_DIM)


def pack_kernel(here_ref, *refs):
    arrays, slabs = refs[:4], refs[4:]
    for distance, slab in enumerate(slabs):
        columns = head_columns(here_ref[0] ^ distance)
        for n, array in enumerate(arrays):
            slab[:, n * HEAD_DIM : (n + 1) * HEAD_DIM] = array[:, columns]


def unpack_kernel(here_ref, *refs):
    slabs, arrays = refs[:-3], refs[-3:]
    for distance, slab in enumerate(slabs):
        columns = head_columns(here_ref[0] ^ distance)
        for n, array in enumerate(arrays):
            array[:, columns] = slab[:, n * HEAD_DIM : (n + 1) * HEAD_DIM]


def attention_kernel(here_ref, mask_ref, *refs):
    count = len(refs) // 2
    slabs, outs = refs[:count], refs[count:]
    scale = 1.0 / math.sqrt(HEAD_DIM)
    here = here_ref[0]
    cells = count // 2

    def cell(c, n):
        columns = slice(n * HEAD_DIM, (n + 1) * HEAD_DIM)
        return jnp.concatenate([slabs[2 * c][:, columns], slabs[2 * c + 1][:, columns]], axis=0)

    q = [cell(c, 0) for c in range(cells)]
    k = [cell(c, 1) for c in range(cells)]
    v = [cell(c, 2) for c in range(cells)]
    g = [cell(c, 3) for c in range(cells)]
    k_turned = [block.T for block in k]
    dk = [None] * cells
    dv = [None] * cells
    rows = q[0].shape[0]
    half = rows // 2
    lane = lax.broadcasted_iota(jnp.int32, (1, rows), 1)

    def add(total, term):
        return term if total is None else total + term

    for c in range(cells):
        near = [c, c ^ 1, c ^ 3]
        scores = [times_t(k[n], q[c]) for n in near]
        allowed = []
        for n in near:
            for a in range(2):
                key_block = here ^ (2 * n + a)
                low = mask_ref[here ^ (2 * c), key_block]
                high = mask_ref[here ^ (2 * c + 1), key_block]
                allowed.append(jnp.where(lane < half, low, high) > 0)
        top = jnp.full((1, rows), -1e30, jnp.float32)
        for t in range(3):
            for a in range(2):
                block = scores[t][a * half : (a + 1) * half]
                top = jnp.maximum(
                    top, jnp.where(allowed[2 * t + a], jnp.max(block, axis=0, keepdims=True), -1e30)
                )
        factor = scale * math.log2(math.e)
        top = top * factor
        exps = []
        total = jnp.zeros((1, rows), jnp.float32)
        for t in range(3):
            parts = []
            for a in range(2):
                block = scores[t][a * half : (a + 1) * half]
                shift = jnp.where(allowed[2 * t + a], top, 1e30)
                parts.append(jnp.exp2(block * factor - shift))
            part = jnp.concatenate(parts, axis=0)
            total = total + jnp.sum(part, axis=0, keepdims=True)
            exps.append(part)
        inverse = 1.0 / total
        probs = [part * inverse for part in exps]
        dprobs = [times_t(v[n], g[c]) for n in near]
        delta = jnp.zeros((1, rows), jnp.float32)
        for t in range(3):
            delta = delta + jnp.sum(probs[t] * dprobs[t], axis=0, keepdims=True)
        dq = None
        for t, n in enumerate(near):
            low = probs[t].astype(jnp.bfloat16)
            dscores = (probs[t] * (dprobs[t] - delta)).astype(jnp.bfloat16)
            dv[n] = add(dv[n], jnp.dot(low, g[c], preferred_element_type=jnp.float32))
            dk[n] = add(dk[n], jnp.dot(dscores, q[c], preferred_element_type=jnp.float32))
            dq = add(dq, jnp.dot(k_turned[n], dscores, preferred_element_type=jnp.float32))
        dq = (dq * scale).T.astype(jnp.bfloat16)
        for a in range(2):
            outs[2 * c + a][:, :HEAD_DIM] = dq[a * half : (a + 1) * half]
    for c in range(cells):
        dk_low = (dk[c] * scale).astype(jnp.bfloat16)
        dv_low = dv[c].astype(jnp.bfloat16)
        for a in range(2):
            outs[2 * c + a][:, HEAD_DIM : 2 * HEAD_DIM] = dk_low[a * half : (a + 1) * half]
            outs[2 * c + a][:, 2 * HEAD_DIM :] = dv_low[a * half : (a + 1) * half]


SMEM = pl.BlockSpec(memory_space=pltpu.SMEM)
VMEM = pl.BlockSpec(memory_space=pltpu.VMEM)


def by_heads(queries, keys, values, out_grad, block_mask):
    devices = lax.axis_size(GROUP)
    tokens = queries.shape[0]
    here = flat_index(GROUP).astype(jnp.int32).reshape(1)
    slab = jax.ShapeDtypeStruct((tokens, 4 * HEAD_DIM), jnp.bfloat16)
    out_slab = jax.ShapeDtypeStruct((tokens, 3 * HEAD_DIM), jnp.bfloat16)
    sent = pl.pallas_call(
        pack_kernel,
        out_shape=[slab] * devices,
        in_specs=[SMEM] + [VMEM] * 4,
        out_specs=[VMEM] * devices,
        name="pack",
    )(here, queries, keys, values, out_grad)
    order = ORDER
    got = [sent[0]] + [None] * (devices - 1)
    for distance in order:
        got[distance] = exchange(sent[distance], distance)
    grads = pl.pallas_call(
        attention_kernel,
        out_shape=[out_slab] * devices,
        in_specs=[SMEM, SMEM] + [VMEM] * devices,
        out_specs=[VMEM] * devices,
        compiler_params=pltpu.CompilerParams(vmem_limit_bytes=40 * 1024 * 1024),
        name="attention",
    )(here, block_mask, *got)
    back = [grads[0]] + [None] * (devices - 1)
    for distance in order:
        back[distance] = exchange(grads[distance], distance)
    return pl.pallas_call(
        unpack_kernel,
        out_shape=[jax.ShapeDtypeStruct(queries.shape, queries.dtype)] * 3,
        in_specs=[SMEM] + [VMEM] * devices,
        out_specs=[VMEM] * 3,
        name="unpack",
    )(here, *back)


def local(queries, keys, values, out_grad, block_mask):
    heads = queries.shape[1] // HEAD_DIM
    cells, halves = lax.axis_size("blk"), lax.axis_size("uly")
    if (cells, halves) == (4, 2) and heads == cells * halves and queries.shape[0] == 128:
        return by_heads(queries, keys, values, out_grad, block_mask)
    return by_cells(queries, keys, values, out_grad, block_mask)


def solution(mesh):
    return jax.shard_map(
        local,
        mesh=mesh,
        in_specs=(
            P(("batch", "blk", "uly"), None),
            P(("batch", "blk", "uly"), None),
            P(("batch", "blk", "uly"), None),
            P(("batch", "blk", "uly"), None),
            P("batch", None),
        ),
        out_specs=(
            P(("batch", "blk", "uly"), None),
            P(("batch", "blk", "uly"), None),
            P(("batch", "blk", "uly"), None),
        ),
        check_vma=False,
    )
```

```python
import functools
import math

import jax
import jax.numpy as jnp
from jax import lax
from jax.experimental import pallas as pl
from jax.experimental.pallas import tpu as pltpu
from jax.sharding import PartitionSpec as P

HEAD_DIM = 128
MIB = 1024 * 1024
GROUP = ("blk", "uly")
ORDER = (5, 7, 4, 6, 1, 3, 2)


def padded(block, sides, width):
    for axis, dim in sides:
        count = lax.axis_size(axis)
        forward = [(i, i + 1) for i in range(count - 1)]
        forward.append((count - 1, 0))
        backward = [(target, source) for source, target in forward]
        low = lax.ppermute(
            lax.slice_in_dim(block, block.shape[dim] - width, None, axis=dim), axis, forward
        )
        high = lax.ppermute(lax.slice_in_dim(block, 0, width, axis=dim), axis, backward)
        block = jnp.concatenate([low, block, high], axis=dim)
    return block


def passed_along(block, axis, distance):
    devices = range(lax.axis_size(axis))
    route = [((i - distance) % len(devices), i) for i in devices]
    return lax.ppermute(block, axis, route)


def times_t(left, right):
    return lax.dot_general(
        left, right, (((1,), (1,)), ((), ())), preferred_element_type=jnp.float32
    )


def t_times(left, right):
    return lax.dot_general(
        left, right, (((0,), (0,)), ((), ())), preferred_element_type=jnp.float32
    )


def widen_blocks(mask_blocks):
    return jnp.repeat(jnp.repeat(mask_blocks > 0, 128, axis=0), 128, axis=1)


def by_cells(queries, keys, values, out_grad, block_mask):
    local_q, local_k, local_v, local_g = (
        lax.all_to_all(queries, "uly", split_axis=1, concat_axis=0, tiled=True),
        lax.all_to_all(keys, "uly", split_axis=1, concat_axis=0, tiled=True),
        lax.all_to_all(values, "uly", split_axis=1, concat_axis=0, tiled=True),
        lax.all_to_all(out_grad, "uly", split_axis=1, concat_axis=0, tiled=True),
    )
    genes = local_q.shape[0]
    heads_here = local_q.shape[1] // HEAD_DIM
    scale = 1.0 / math.sqrt(HEAD_DIM)
    cells = lax.axis_size("blk")
    here = lax.axis_index("blk")
    per_cell = genes // 128
    near = (here + jnp.array([-1, 0, 1], dtype=jnp.int32) + cells) % cells
    mask_rows = lax.dynamic_slice_in_dim(block_mask, here * per_cell, per_cell, 0).reshape(
        per_cell, cells, per_cell
    )
    row_mask = widen_blocks(jnp.take(mask_rows, near, axis=1).reshape(per_cell, 3 * per_cell))
    pairs = jnp.stack([local_k, local_v], axis=1)
    band = padded(pairs, (("blk", 0),), genes)
    q_grads = []
    k_parts = []
    v_parts = []
    for head in range(heads_here):
        lower = head * HEAD_DIM
        upper = lower + HEAD_DIM
        q_head = local_q[:, lower:upper]
        g_head = local_g[:, lower:upper]
        k_band = band[:, 0, lower:upper]
        v_band = band[:, 1, lower:upper]
        scores = jnp.where(row_mask, times_t(q_head, k_band) * scale, -1e30)
        top = jnp.max(scores, axis=1, keepdims=True)
        total = jnp.sum(jnp.where(row_mask, jnp.exp(scores - top), 0.0), axis=1, keepdims=True)
        lse = top + jnp.log(total)
        probs = jnp.where(row_mask, jnp.exp(scores - lse), 0.0)
        dprobs = times_t(g_head, v_band)
        delta = jnp.sum(probs * dprobs, axis=1, keepdims=True)
        dscores = (probs * (dprobs - delta)).astype(jnp.bfloat16)
        q_grads.append(
            (jnp.dot(dscores, k_band, preferred_element_type=jnp.float32) * scale).astype(
                jnp.bfloat16
            )
        )
        k_parts.append(t_times(dscores, q_head))
        v_parts.append(t_times(probs.astype(jnp.bfloat16), g_head))
    query_grad = jnp.concatenate(q_grads, axis=1)
    partial_terms = jnp.stack(
        [jnp.concatenate(k_parts, axis=1), jnp.concatenate(v_parts, axis=1)], axis=1
    )
    from_next = passed_along(partial_terms[:genes].astype(jnp.bfloat16), "blk", -1).astype(
        jnp.float32
    )
    from_prior = passed_along(partial_terms[2 * genes :].astype(jnp.bfloat16), "blk", 1).astype(
        jnp.float32
    )
    summed = partial_terms[genes : 2 * genes] + from_next + from_prior
    key_grad = (summed[:, 0] * scale).astype(jnp.bfloat16)
    value_grad = summed[:, 1].astype(jnp.bfloat16)
    return (
        lax.all_to_all(query_grad, "uly", split_axis=0, concat_axis=1, tiled=True),
        lax.all_to_all(key_grad, "uly", split_axis=0, concat_axis=1, tiled=True),
        lax.all_to_all(value_grad, "uly", split_axis=0, concat_axis=1, tiled=True),
    )


def flat_index(axes):
    index = 0
    for axis in axes:
        index = index * lax.axis_size(axis) + lax.axis_index(axis)
    return index


def exchange(block, distance):
    devices = lax.axis_size(GROUP)
    return lax.ppermute(block, GROUP, [(i, i ^ distance) for i in range(devices)])


def head_columns(head):
    return pl.ds(pl.multiple_of(head * HEAD_DIM, HEAD_DIM), HEAD_DIM)


def pack_kernel(distances, *refs):
    arrays, slabs, sems = refs[:4], refs[4:-1], refs[-1]
    here = flat_index(GROUP)
    copies = []
    for i, (distance, slab) in enumerate(zip(distances, slabs)):
        columns = head_columns(here ^ distance)
        for n, array in enumerate(arrays):
            into = slab.at[:, n * HEAD_DIM : (n + 1) * HEAD_DIM]
            copies.append(pltpu.make_async_copy(array.at[:, columns], into, sems.at[i, n]))
    for copy in copies:
        copy.start()
    for copy in copies:
        copy.wait()


def unpack_kernel(distances, *refs):
    slabs, arrays, sems = refs[:-4], refs[-4:-1], refs[-1]
    here = flat_index(GROUP)
    copies = []
    for i, (distance, slab) in enumerate(zip(distances, slabs)):
        columns = head_columns(here ^ distance)
        for n, array in enumerate(arrays):
            part = slab.at[:, n * HEAD_DIM : (n + 1) * HEAD_DIM]
            copies.append(pltpu.make_async_copy(part, array.at[:, columns], sems.at[i, n]))
    for copy in copies:
        copy.start()
    for copy in copies:
        copy.wait()


def attention_kernel(order, mask_ref, *refs):
    count = len(order)
    slabs = [refs[order.index(distance)] for distance in range(count)]
    outs = [refs[count + order.index(distance)] for distance in range(count)]
    scale = 1.0 / math.sqrt(HEAD_DIM)
    here = flat_index(GROUP)
    cells = count // 2

    def cell(c, n):
        columns = slice(n * HEAD_DIM, (n + 1) * HEAD_DIM)
        return jnp.concatenate([slabs[2 * c][:, columns], slabs[2 * c + 1][:, columns]], axis=0)

    q = [cell(c, 0) for c in range(cells)]
    k = [cell(c, 1) for c in range(cells)]
    v = [cell(c, 2) for c in range(cells)]
    g = [cell(c, 3) for c in range(cells)]
    k_turned = [block.T for block in k]
    dk = [None] * cells
    dv = [None] * cells
    rows = q[0].shape[0]
    half = rows // 2
    lane = lax.broadcasted_iota(jnp.int32, (1, rows), 1)

    def add(total, term):
        return term if total is None else total + term

    for c in range(cells):
        near = [c, c ^ 1, c ^ 3]
        scores = [times_t(k[n], q[c]) for n in near]
        allowed = []
        for n in near:
            for a in range(2):
                key_block = here ^ (2 * n + a)
                low = mask_ref[here ^ (2 * c), key_block]
                high = mask_ref[here ^ (2 * c + 1), key_block]
                allowed.append(jnp.where(lane < half, low, high) > 0)
        top = jnp.full((1, rows), -1e30, jnp.float32)
        for t in range(3):
            for a in range(2):
                block = scores[t][a * half : (a + 1) * half]
                top = jnp.maximum(
                    top, jnp.where(allowed[2 * t + a], jnp.max(block, axis=0, keepdims=True), -1e30)
                )
        factor = scale * math.log2(math.e)
        top = top * factor
        exps = []
        total = jnp.zeros((1, rows), jnp.float32)
        for t in range(3):
            parts = []
            for a in range(2):
                block = scores[t][a * half : (a + 1) * half]
                shift = jnp.where(allowed[2 * t + a], top, 1e30)
                parts.append(jnp.exp2(block * factor - shift))
            part = jnp.concatenate(parts, axis=0)
            total = total + jnp.sum(part, axis=0, keepdims=True)
            exps.append(part)
        inverse = 1.0 / total
        probs = [part * inverse for part in exps]
        dprobs = [times_t(v[n], g[c]) for n in near]
        delta = jnp.zeros((1, rows), jnp.float32)
        for t in range(3):
            delta = delta + jnp.sum(probs[t] * dprobs[t], axis=0, keepdims=True)
        dq = None
        for t, n in enumerate(near):
            low = probs[t].astype(jnp.bfloat16)
            dscores = (probs[t] * (dprobs[t] - delta)).astype(jnp.bfloat16)
            dv[n] = add(dv[n], jnp.dot(low, g[c], preferred_element_type=jnp.float32))
            dk[n] = add(dk[n], jnp.dot(dscores, q[c], preferred_element_type=jnp.float32))
            dq = add(dq, jnp.dot(k_turned[n], dscores, preferred_element_type=jnp.float32))
        dq = (dq * scale).T.astype(jnp.bfloat16)
        for a in range(2):
            outs[2 * c + a][:, :HEAD_DIM] = dq[a * half : (a + 1) * half]
    for c in range(cells):
        dk_low = (dk[c] * scale).astype(jnp.bfloat16)
        dv_low = dv[c].astype(jnp.bfloat16)
        for a in range(2):
            outs[2 * c + a][:, HEAD_DIM : 2 * HEAD_DIM] = dk_low[a * half : (a + 1) * half]
            outs[2 * c + a][:, 2 * HEAD_DIM :] = dv_low[a * half : (a + 1) * half]


SMEM = pl.BlockSpec(memory_space=pltpu.SMEM)
VMEM = pl.BlockSpec(memory_space=pltpu.VMEM)
ANY = pl.BlockSpec(memory_space=pl.ANY)


def pack(arrays, distances, name):
    tokens = arrays[0].shape[0]
    return pl.pallas_call(
        functools.partial(pack_kernel, distances),
        out_shape=[jax.ShapeDtypeStruct((tokens, 4 * HEAD_DIM), jnp.bfloat16)] * len(distances),
        in_specs=[ANY] * 4,
        out_specs=[ANY] * len(distances),
        scratch_shapes=[pltpu.SemaphoreType.DMA((len(distances), 4))],
        compiler_params=pltpu.CompilerParams(vmem_limit_bytes=MIB),
        name=name,
    )(*arrays)


def by_heads(queries, keys, values, out_grad, block_mask):
    devices = lax.axis_size(GROUP)
    tokens = queries.shape[0]
    arrays = [
        pltpu.with_memory_space_constraint(array, pltpu.HBM)
        for array in (queries, keys, values, out_grad)
    ]
    sent = {}
    for distances, name in ((ORDER[:2], "pack_first"), (ORDER[2:] + (0,), "pack_rest")):
        sent.update(zip(distances, pack(arrays, distances, name)))
    order = ORDER + (0,)
    got = [exchange(sent[distance], distance) for distance in ORDER] + [sent[0]]
    grads = pl.pallas_call(
        functools.partial(attention_kernel, order),
        out_shape=[jax.ShapeDtypeStruct((tokens, 3 * HEAD_DIM), jnp.bfloat16)] * devices,
        in_specs=[SMEM] + [VMEM] * devices,
        out_specs=[VMEM] * devices,
        compiler_params=pltpu.CompilerParams(vmem_limit_bytes=40 * MIB),
        name="attention",
    )(block_mask, *got)
    back = [exchange(grad, distance) for grad, distance in zip(grads, ORDER)] + [grads[-1]]
    return pl.pallas_call(
        functools.partial(unpack_kernel, order),
        out_shape=[jax.ShapeDtypeStruct(queries.shape, queries.dtype)] * 3,
        in_specs=[ANY] * devices,
        out_specs=[ANY] * 3,
        scratch_shapes=[pltpu.SemaphoreType.DMA((devices, 3))],
        compiler_params=pltpu.CompilerParams(vmem_limit_bytes=MIB),
        name="unpack",
    )(*back)


def local(queries, keys, values, out_grad, block_mask):
    heads = queries.shape[1] // HEAD_DIM
    cells, halves = lax.axis_size("blk"), lax.axis_size("uly")
    if (cells, halves) == (4, 2) and heads == cells * halves and queries.shape[0] == 128:
        return by_heads(queries, keys, values, out_grad, block_mask)
    return by_cells(queries, keys, values, out_grad, block_mask)


def solution(mesh):
    return jax.shard_map(
        local,
        mesh=mesh,
        in_specs=(
            P(("batch", "blk", "uly"), None),
            P(("batch", "blk", "uly"), None),
            P(("batch", "blk", "uly"), None),
            P(("batch", "blk", "uly"), None),
            P("batch", None),
        ),
        out_specs=(
            P(("batch", "blk", "uly"), None),
            P(("batch", "blk", "uly"), None),
            P(("batch", "blk", "uly"), None),
        ),
        check_vma=False,
    )
```

```python
import functools
import math

import jax
import jax.numpy as jnp
from jax import lax
from jax.experimental import pallas as pl
from jax.experimental.pallas import tpu as pltpu
from jax.sharding import PartitionSpec as P

HEAD_DIM = 128
MIB = 1024 * 1024
GROUP = ("blk", "uly")


def padded(block, sides, width):
    for axis, dim in sides:
        count = lax.axis_size(axis)
        forward = [(i, i + 1) for i in range(count - 1)]
        forward.append((count - 1, 0))
        backward = [(target, source) for source, target in forward]
        low = lax.ppermute(
            lax.slice_in_dim(block, block.shape[dim] - width, None, axis=dim), axis, forward
        )
        high = lax.ppermute(lax.slice_in_dim(block, 0, width, axis=dim), axis, backward)
        block = jnp.concatenate([low, block, high], axis=dim)
    return block


def passed_along(block, axis, distance):
    devices = range(lax.axis_size(axis))
    route = [((i - distance) % len(devices), i) for i in devices]
    return lax.ppermute(block, axis, route)


def times_t(left, right):
    return lax.dot_general(
        left, right, (((1,), (1,)), ((), ())), preferred_element_type=jnp.float32
    )


def t_times(left, right):
    return lax.dot_general(
        left, right, (((0,), (0,)), ((), ())), preferred_element_type=jnp.float32
    )


def widen_blocks(mask_blocks):
    return jnp.repeat(jnp.repeat(mask_blocks > 0, 128, axis=0), 128, axis=1)


def by_cells(queries, keys, values, out_grad, block_mask):
    local_q, local_k, local_v, local_g = (
        lax.all_to_all(queries, "uly", split_axis=1, concat_axis=0, tiled=True),
        lax.all_to_all(keys, "uly", split_axis=1, concat_axis=0, tiled=True),
        lax.all_to_all(values, "uly", split_axis=1, concat_axis=0, tiled=True),
        lax.all_to_all(out_grad, "uly", split_axis=1, concat_axis=0, tiled=True),
    )
    genes = local_q.shape[0]
    heads_here = local_q.shape[1] // HEAD_DIM
    scale = 1.0 / math.sqrt(HEAD_DIM)
    cells = lax.axis_size("blk")
    here = lax.axis_index("blk")
    per_cell = genes // 128
    near = (here + jnp.array([-1, 0, 1], dtype=jnp.int32) + cells) % cells
    mask_rows = lax.dynamic_slice_in_dim(block_mask, here * per_cell, per_cell, 0).reshape(
        per_cell, cells, per_cell
    )
    row_mask = widen_blocks(jnp.take(mask_rows, near, axis=1).reshape(per_cell, 3 * per_cell))
    pairs = jnp.stack([local_k, local_v], axis=1)
    band = padded(pairs, (("blk", 0),), genes)
    q_grads = []
    k_parts = []
    v_parts = []
    for head in range(heads_here):
        lower = head * HEAD_DIM
        upper = lower + HEAD_DIM
        q_head = local_q[:, lower:upper]
        g_head = local_g[:, lower:upper]
        k_band = band[:, 0, lower:upper]
        v_band = band[:, 1, lower:upper]
        scores = jnp.where(row_mask, times_t(q_head, k_band) * scale, -1e30)
        top = jnp.max(scores, axis=1, keepdims=True)
        total = jnp.sum(jnp.where(row_mask, jnp.exp(scores - top), 0.0), axis=1, keepdims=True)
        lse = top + jnp.log(total)
        probs = jnp.where(row_mask, jnp.exp(scores - lse), 0.0)
        dprobs = times_t(g_head, v_band)
        delta = jnp.sum(probs * dprobs, axis=1, keepdims=True)
        dscores = (probs * (dprobs - delta)).astype(jnp.bfloat16)
        q_grads.append(
            (jnp.dot(dscores, k_band, preferred_element_type=jnp.float32) * scale).astype(
                jnp.bfloat16
            )
        )
        k_parts.append(t_times(dscores, q_head))
        v_parts.append(t_times(probs.astype(jnp.bfloat16), g_head))
    query_grad = jnp.concatenate(q_grads, axis=1)
    partial_terms = jnp.stack(
        [jnp.concatenate(k_parts, axis=1), jnp.concatenate(v_parts, axis=1)], axis=1
    )
    from_next = passed_along(partial_terms[:genes].astype(jnp.bfloat16), "blk", -1).astype(
        jnp.float32
    )
    from_prior = passed_along(partial_terms[2 * genes :].astype(jnp.bfloat16), "blk", 1).astype(
        jnp.float32
    )
    summed = partial_terms[genes : 2 * genes] + from_next + from_prior
    key_grad = (summed[:, 0] * scale).astype(jnp.bfloat16)
    value_grad = summed[:, 1].astype(jnp.bfloat16)
    return (
        lax.all_to_all(query_grad, "uly", split_axis=0, concat_axis=1, tiled=True),
        lax.all_to_all(key_grad, "uly", split_axis=0, concat_axis=1, tiled=True),
        lax.all_to_all(value_grad, "uly", split_axis=0, concat_axis=1, tiled=True),
    )


def flat_index(axes):
    index = 0
    for axis in axes:
        index = index * lax.axis_size(axis) + lax.axis_index(axis)
    return index


def same_core(here):
    return (here >> 1) & 1


def even_places(here):
    return (here ^ (here >> 1) ^ (here >> 2)) & 1


def hop(first, second=None, chooser=same_core):
    if second is None:
        return lambda here: first
    return lambda here: first + (second - first) * chooser(here)


STAY = hop(0)
CORE = hop(2)
FAR = hop(5)
FAR_CORE = hop(7)
SIDE = hop(4, 1)
OTHER_SIDE = hop(1, 4)
SIDE_CORE = hop(6, 3, even_places)
OTHER_SIDE_CORE = hop(3, 6, even_places)

INWARD = (SIDE, FAR_CORE, OTHER_SIDE, SIDE_CORE, OTHER_SIDE_CORE, CORE, FAR)
OUTWARD = (SIDE, FAR, FAR_CORE, OTHER_SIDE, SIDE_CORE, OTHER_SIDE_CORE, CORE)
FIRST = 2
EARLY = 2
LATE = 5
DONE = 0
AFTER = {6: 1}
EXPONENT = math.log2(math.e) / math.sqrt(HEAD_DIM)


def exchange(block, distance):
    places = range(lax.axis_size(GROUP))
    return lax.ppermute(block, GROUP, [(i, i ^ distance(i)) for i in places])


def part(ref, n):
    return ref.at[:, n * HEAD_DIM : (n + 1) * HEAD_DIM]


def head_of(ref, head):
    return ref.at[:, pl.ds(pl.multiple_of(head * HEAD_DIM, HEAD_DIM), HEAD_DIM)]


def run(copies):
    for copy in copies:
        copy.start()
    for copy in copies:
        copy.wait()


def pack_kernel(distances, *refs):
    count = len(distances)
    extras = (len(refs) - 1 - count - 4) // 2
    sources, outs, sems = refs[: 4 + extras], refs[4 + extras : -1], refs[-1]
    here = flat_index(GROUP)
    pairs = list(zip(sources[4:], outs[count:]))
    for distance, slab in zip(distances, outs):
        for n, array in enumerate(sources[:4]):
            pairs.append((head_of(array, here ^ distance(here)), part(slab, n)))
    run([pltpu.make_async_copy(*pair, sems.at[n]) for n, pair in enumerate(pairs)])


def unpack_kernel(distances, *refs):
    slabs, arrays, sems = refs[: len(distances)], refs[-4:-1], refs[-1]
    here = flat_index(GROUP)
    pairs = []
    for distance, slab in zip(distances, slabs):
        for n, array in enumerate(arrays):
            pairs.append((part(slab, n), head_of(array, here ^ distance(here))))
    run([pltpu.make_async_copy(*pair, sems.at[n]) for n, pair in enumerate(pairs)])


def near_cells(c):
    return (c, c ^ 1, c ^ 3)


def key_places(c):
    return [2 * n + a for n in near_cells(c) for a in range(2)]


def blocks_of(value):
    return [value[r : r + 128] for r in range(0, value.shape[0], 128)]


def seen_by(mask_ref, here, key, queries):
    flags = [jnp.full((1, 128), mask_ref[here ^ query, here ^ key]) for query in queries]
    return jnp.concatenate(flags, axis=1) > 0


def weights(scores, seen, top):
    return [
        jnp.exp2(block * EXPONENT - jnp.where(flag, top, 1e30)) for block, flag in zip(scores, seen)
    ]


def top_of(scores, seen):
    top = jnp.full((1, scores[0].shape[1]), -1e30, jnp.float32)
    for block, flag in zip(scores, seen):
        top = jnp.maximum(top, jnp.where(flag, jnp.max(block, axis=0, keepdims=True), -1e30))
    return top * EXPONENT


def sum_of(blocks):
    total = blocks[0]
    for block in blocks[1:]:
        total = total + block
    return jnp.sum(total, axis=0, keepdims=True)


def query_grad(keys, dscores):
    low = (t_times(keys, dscores) * (1.0 / math.sqrt(HEAD_DIM))).T.astype(jnp.bfloat16)
    return low.reshape(-1, 128, HEAD_DIM)


def early_kernel(distances, mask_ref, *refs):
    slabs, outs = refs[:-6], refs[-6:]
    stack_ref, exps_ref, dprobs_ref, stats_ref, done_ref, query_ref = outs
    here = flat_index(GROUP)
    for distance, slab in zip(distances, slabs):
        stack_ref[distance(here)] = slab[...]

    def take(places, n):
        columns = slice(n * HEAD_DIM, (n + 1) * HEAD_DIM)
        return jnp.concatenate([stack_ref[place, :, columns] for place in places], axis=0)

    cells = stack_ref.shape[0] // 2
    present = [[p for p in (2 * c, 2 * c + 1) if p != LATE] for c in range(cells)]
    for c in range(cells):
        q, g = take(present[c], 0), take(present[c], 3)
        width = q.shape[0]
        keys = [place for place in key_places(c) if place != LATE]
        scores = [b for n in near_cells(c) for b in blocks_of(times_t(take(present[n], 1), q))]
        dprobs = [b for n in near_cells(c) for b in blocks_of(times_t(take(present[n], 2), g))]
        seen = [seen_by(mask_ref, here, key, present[c]) for key in keys]
        top = top_of(scores, seen)
        exps = weights(scores, seen, top)
        total = sum_of(exps)
        product = sum_of([e * d for e, d in zip(exps, dprobs)])
        if LATE not in key_places(c):
            inverse = 1.0 / total
            delta = product * inverse
            terms = []
            for n, (weight, term) in enumerate(zip(exps, dprobs)):
                probs = weight * inverse
                terms.append((probs * (term - delta)).astype(jnp.bfloat16))
                done_ref[0, 128 * n : 128 * (n + 1)] = probs.astype(jnp.bfloat16)
                done_ref[1, 128 * n : 128 * (n + 1)] = terms[n]
            query_ref[...] = query_grad(take(key_places(c), 1), jnp.concatenate(terms, axis=0))
            continue
        for key, weight, term in zip(keys, exps, dprobs):
            row = 128 * key_places(c).index(key)
            exps_ref[c, row : row + 128, :width] = weight
            dprobs_ref[c, row : row + 128, :width] = term
        stats_ref[c, 0:1, :width] = top
        stats_ref[c, 1:2, :width] = total
        stats_ref[c, 2:3, :width] = product


def late_kernel(distances, mask_ref, slab, *refs):
    stack_ref, exps_ref, dprobs_ref, stats_ref, done_ref, query_ref = refs[:6]
    outs, out_ref = refs[6:-1], refs[-1]
    here = flat_index(GROUP)
    fixed = [distance(here) for distance in distances]
    fixed = {place: out for place, out in zip(fixed, outs) if isinstance(place, int)}
    scale = 1.0 / math.sqrt(HEAD_DIM)
    cells = stack_ref.shape[0] // 2

    def take(places, n):
        columns = slice(n * HEAD_DIM, (n + 1) * HEAD_DIM)
        parts = [slab[:, columns] if p == LATE else stack_ref[p, :, columns] for p in places]
        return jnp.concatenate(parts, axis=0)

    def whole(n):
        return [take((2 * c, 2 * c + 1), n) for c in range(cells)]

    q, k, v, g = (whole(n) for n in range(4))

    units = [(c, (2 * c, 2 * c + 1)) for c in range(cells) if c not in (DONE, LATE // 2)]
    units = [(LATE // 2, (place,)) for place in (LATE - 1, LATE)] + units
    fresh = [[p for p in key_places(c) if LATE in (p, *queries)] for c, queries in units]
    scores, dprobs, exps, inverse, delta, early_inverse = ([None] * len(units) for _ in range(6))
    for u, (c, queries) in enumerate(units):
        groups = [(LATE,)] if LATE not in queries else [(2 * n, 2 * n + 1) for n in near_cells(c)]
        groups = groups if fresh[u] else []
        mine_q, mine_g = take(queries, 0), take(queries, 3)
        scores[u] = [b for keys in groups for b in blocks_of(times_t(take(keys, 1), mine_q))]
        dprobs[u] = [b for keys in groups for b in blocks_of(times_t(take(keys, 2), mine_g))]
    seen = [[seen_by(mask_ref, here, p, unit[1]) for p in keys] for unit, keys in zip(units, fresh)]
    tops = [top_of(blocks, flags) if blocks else None for blocks, flags in zip(scores, seen)]
    for u, (c, queries) in enumerate(units):
        early = LATE not in queries
        if early:
            top, total, product = (
                stats_ref[c, n : n + 1, : 128 * len(queries)] for n in range(3)
            )
        shrink = None
        if fresh[u]:
            new_top = jnp.maximum(top, tops[u]) if early else tops[u]
            exps[u] = weights(scores[u], seen[u], new_top)
            new_total = sum_of(exps[u])
            new_product = sum_of([e * d for e, d in zip(exps[u], dprobs[u])])
            if early:
                shrink = jnp.exp2(top - new_top)
                new_total = new_total + total * shrink
                new_product = new_product + product * shrink
            total, product = new_total, new_product
        inverse[u] = 1.0 / total
        delta[u] = product * inverse[u]
        early_inverse[u] = inverse[u] if shrink is None else inverse[u] * shrink

    def finished(u):
        c, queries = units[u]
        probs_low, dscores = [], []
        for n, key in enumerate(key_places(c)):
            if key in fresh[u]:
                index = fresh[u].index(key)
                probs, term = exps[u][index] * inverse[u], dprobs[u][index]
            else:
                place = (c, slice(128 * n, 128 * (n + 1)), slice(0, 128 * len(queries)))
                probs, term = exps_ref[place] * early_inverse[u], dprobs_ref[place]
            probs_low.append(probs.astype(jnp.bfloat16))
            dscores.append((probs * (term - delta[u])).astype(jnp.bfloat16))
        return probs_low, dscores

    def put(n, c, value):
        low = value.astype(jnp.bfloat16).reshape(2, 128, HEAD_DIM)
        for place in (2 * c, 2 * c + 1):
            out = fixed.get(place, out_ref.at[place])
            out[:, n * HEAD_DIM : (n + 1) * HEAD_DIM] = low[place - 2 * c]

    def joined(blocks, c, axis):
        return jnp.concatenate([blocks[n] for n in near_cells(c)], axis=axis)

    probs_low = [{} for _ in range(cells)]
    dscores = [{} for _ in range(cells)]

    def rows_of(c):
        if c == DONE:
            pair = [blocks_of(done_ref[n]) for n in range(2)]
        elif LATE // 2 == c:
            sides = zip(finished(0), finished(1))
            pair = [
                [jnp.concatenate(both, axis=1) for both in zip(left, right)] for left, right in sides
            ]
        else:
            pair = finished(units.index((c, (2 * c, 2 * c + 1))))
        for t, n in enumerate(near_cells(c)):
            probs_low[n][c] = jnp.concatenate(pair[0][2 * t : 2 * t + 2], axis=0)
            dscores[n][c] = jnp.concatenate(pair[1][2 * t : 2 * t + 2], axis=0)

    def put_value_grad(c):
        low = joined(probs_low[c], c, 1)
        put(2, c, jnp.dot(low, joined(g, c, 0), preferred_element_type=jnp.float32))

    def put_key_grad(c):
        low = joined(dscores[c], c, 1)
        put(1, c, jnp.dot(low, joined(q, c, 0), preferred_element_type=jnp.float32) * scale)

    def put_query_grad(c):
        if c == DONE:
            put(0, c, query_ref[...])
            return
        terms = jnp.concatenate([dscores[n][c] for n in near_cells(c)], axis=0)
        put(0, c, query_grad(joined(k, c, 0), terms))

    rows_of(2)
    rows_of(1)
    rows_of(3)
    rows_of(0)
    put_value_grad(0)
    put_value_grad(1)
    put_value_grad(2)
    put_value_grad(3)
    put_key_grad(0)
    put_key_grad(1)
    put_key_grad(2)
    put_key_grad(3)
    put_query_grad(0)
    put_query_grad(1)
    put_query_grad(2)
    put_query_grad(3)
    for distance, out in zip(distances, outs):
        if not isinstance(distance(here), int):
            out[...] = out_ref[distance(here)]


SMEM = pl.BlockSpec(memory_space=pltpu.SMEM)
VMEM = pl.BlockSpec(memory_space=pltpu.VMEM)
ANY = pl.BlockSpec(memory_space=pl.ANY)


def slab_shape(tokens, parts):
    return jax.ShapeDtypeStruct((tokens, parts * HEAD_DIM), jnp.bfloat16)


def pack(arrays, distances, name, *extras):
    tokens = arrays[0].shape[0]
    count = len(distances)
    outs = [slab_shape(tokens, 4)] * count
    outs += [jax.ShapeDtypeStruct(extra.shape, extra.dtype) for extra in extras]
    return pl.pallas_call(
        functools.partial(pack_kernel, distances),
        out_shape=outs,
        in_specs=[ANY] * (4 + len(extras)),
        out_specs=[ANY] * len(outs),
        scratch_shapes=[pltpu.SemaphoreType.DMA((4 * count + len(extras),))],
        compiler_params=pltpu.CompilerParams(vmem_limit_bytes=MIB),
        name=name,
    )(*arrays, *extras)


def unpack(whole, distances, slabs, name, *arrays):
    count = len(distances)
    return pl.pallas_call(
        functools.partial(unpack_kernel, distances),
        out_shape=[whole] * 3,
        in_specs=[ANY] * (count + len(arrays)),
        out_specs=[ANY] * 3,
        scratch_shapes=[pltpu.SemaphoreType.DMA((3 * count,))],
        compiler_params=pltpu.CompilerParams(vmem_limit_bytes=MIB),
        input_output_aliases={count + n: n for n in range(len(arrays))},
        name=name,
    )(*slabs, *arrays)


def by_heads(queries, keys, values, out_grad, block_mask):
    devices = lax.axis_size(GROUP)
    cells = lax.axis_size("blk")
    tokens = queries.shape[0]
    *arrays, block_mask = [
        pltpu.with_memory_space_constraint(array, pltpu.HBM)
        for array in (queries, keys, values, out_grad, block_mask)
    ]
    sent = pack(arrays, INWARD[:FIRST], "pack_first")
    arrays, sent = lax.optimization_barrier((arrays, sent))
    *rest, own, block_mask = pack(arrays, INWARD[FIRST:] + (STAY,), "pack_rest", block_mask)
    got = list(sent) + rest
    for n, distance in enumerate(INWARD):
        if n in AFTER:
            got[n], got[AFTER[n]] = lax.optimization_barrier((got[n], got[AFTER[n]]))
        got[n] = exchange(got[n], distance)
    pairs = jax.ShapeDtypeStruct((cells, 6 * tokens, 2 * tokens), jnp.float32)
    partial = pl.pallas_call(
        functools.partial(early_kernel, INWARD[:-1] + (STAY,)),
        out_shape=[
            jax.ShapeDtypeStruct((devices, tokens, 4 * HEAD_DIM), jnp.bfloat16),
            pairs,
            pairs,
            jax.ShapeDtypeStruct((cells, 8, 2 * tokens), jnp.float32),
            jax.ShapeDtypeStruct((2, 6 * tokens, 2 * tokens), jnp.bfloat16),
            jax.ShapeDtypeStruct((2, tokens, HEAD_DIM), jnp.bfloat16),
        ],
        in_specs=[SMEM] + [VMEM] * (devices - 1),
        out_specs=[VMEM] * 6,
        compiler_params=pltpu.CompilerParams(vmem_limit_bytes=24 * MIB),
        name="early",
    )(block_mask, *got[:-1], own)
    distances = OUTWARD + (STAY,)
    grads = pl.pallas_call(
        functools.partial(late_kernel, distances),
        out_shape=[slab_shape(tokens, 3)] * devices,
        in_specs=[SMEM] + [VMEM] * 7,
        out_specs=[VMEM] * devices,
        scratch_shapes=[pltpu.VMEM((devices, tokens, 3 * HEAD_DIM), jnp.bfloat16)],
        compiler_params=pltpu.CompilerParams(vmem_limit_bytes=24 * MIB),
        name="late",
    )(block_mask, got[-1], *partial)
    back = [exchange(grad, distance) for grad, distance in zip(grads, OUTWARD)] + [grads[-1]]
    whole = jax.ShapeDtypeStruct(queries.shape, queries.dtype)
    grads = unpack(whole, distances[-1:] + distances[:EARLY], back[-1:] + back[:EARLY], "unpack")
    return unpack(whole, distances[EARLY:-1], back[EARLY:-1], "unpack_last", *grads)


def local(queries, keys, values, out_grad, block_mask):
    heads = queries.shape[1] // HEAD_DIM
    cells, halves = lax.axis_size("blk"), lax.axis_size("uly")
    if (cells, halves) == (4, 2) and heads == cells * halves and queries.shape[0] == 128:
        return by_heads(queries, keys, values, out_grad, block_mask)
    return by_cells(queries, keys, values, out_grad, block_mask)


def solution(mesh):
    return jax.shard_map(
        local,
        mesh=mesh,
        in_specs=(
            P(("batch", "blk", "uly"), None),
            P(("batch", "blk", "uly"), None),
            P(("batch", "blk", "uly"), None),
            P(("batch", "blk", "uly"), None),
            P("batch", None),
        ),
        out_specs=(
            P(("batch", "blk", "uly"), None),
            P(("batch", "blk", "uly"), None),
            P(("batch", "blk", "uly"), None),
        ),
        check_vma=False,
    )
```

```python
import functools
import math

import jax
import jax.numpy as jnp
from jax import lax
from jax.experimental import pallas as pl
from jax.experimental.pallas import tpu as pltpu
from jax.sharding import PartitionSpec as P

HEAD_DIM = 128
MIB = 1024 * 1024
GROUP = ("blk", "uly")


def padded(block, sides, width):
    for axis, dim in sides:
        count = lax.axis_size(axis)
        forward = [(i, i + 1) for i in range(count - 1)]
        forward.append((count - 1, 0))
        backward = [(target, source) for source, target in forward]
        low = lax.ppermute(
            lax.slice_in_dim(block, block.shape[dim] - width, None, axis=dim), axis, forward
        )
        high = lax.ppermute(lax.slice_in_dim(block, 0, width, axis=dim), axis, backward)
        block = jnp.concatenate([low, block, high], axis=dim)
    return block


def passed_along(block, axis, distance):
    devices = range(lax.axis_size(axis))
    route = [((i - distance) % len(devices), i) for i in devices]
    return lax.ppermute(block, axis, route)


def times_t(left, right):
    return lax.dot_general(
        left, right, (((1,), (1,)), ((), ())), preferred_element_type=jnp.float32
    )


def t_times(left, right):
    return lax.dot_general(
        left, right, (((0,), (0,)), ((), ())), preferred_element_type=jnp.float32
    )


def widen_blocks(mask_blocks):
    return jnp.repeat(jnp.repeat(mask_blocks > 0, 128, axis=0), 128, axis=1)


def by_cells(queries, keys, values, out_grad, block_mask):
    local_q, local_k, local_v, local_g = (
        lax.all_to_all(queries, "uly", split_axis=1, concat_axis=0, tiled=True),
        lax.all_to_all(keys, "uly", split_axis=1, concat_axis=0, tiled=True),
        lax.all_to_all(values, "uly", split_axis=1, concat_axis=0, tiled=True),
        lax.all_to_all(out_grad, "uly", split_axis=1, concat_axis=0, tiled=True),
    )
    genes = local_q.shape[0]
    heads_here = local_q.shape[1] // HEAD_DIM
    scale = 1.0 / math.sqrt(HEAD_DIM)
    cells = lax.axis_size("blk")
    here = lax.axis_index("blk")
    per_cell = genes // 128
    near = (here + jnp.array([-1, 0, 1], dtype=jnp.int32) + cells) % cells
    mask_rows = lax.dynamic_slice_in_dim(block_mask, here * per_cell, per_cell, 0).reshape(
        per_cell, cells, per_cell
    )
    row_mask = widen_blocks(jnp.take(mask_rows, near, axis=1).reshape(per_cell, 3 * per_cell))
    pairs = jnp.stack([local_k, local_v], axis=1)
    band = padded(pairs, (("blk", 0),), genes)
    q_grads = []
    k_parts = []
    v_parts = []
    for head in range(heads_here):
        lower = head * HEAD_DIM
        upper = lower + HEAD_DIM
        q_head = local_q[:, lower:upper]
        g_head = local_g[:, lower:upper]
        k_band = band[:, 0, lower:upper]
        v_band = band[:, 1, lower:upper]
        scores = jnp.where(row_mask, times_t(q_head, k_band) * scale, -1e30)
        top = jnp.max(scores, axis=1, keepdims=True)
        total = jnp.sum(jnp.where(row_mask, jnp.exp(scores - top), 0.0), axis=1, keepdims=True)
        lse = top + jnp.log(total)
        probs = jnp.where(row_mask, jnp.exp(scores - lse), 0.0)
        dprobs = times_t(g_head, v_band)
        delta = jnp.sum(probs * dprobs, axis=1, keepdims=True)
        dscores = (probs * (dprobs - delta)).astype(jnp.bfloat16)
        q_grads.append(
            (jnp.dot(dscores, k_band, preferred_element_type=jnp.float32) * scale).astype(
                jnp.bfloat16
            )
        )
        k_parts.append(t_times(dscores, q_head))
        v_parts.append(t_times(probs.astype(jnp.bfloat16), g_head))
    query_grad = jnp.concatenate(q_grads, axis=1)
    partial_terms = jnp.stack(
        [jnp.concatenate(k_parts, axis=1), jnp.concatenate(v_parts, axis=1)], axis=1
    )
    from_next = passed_along(partial_terms[:genes].astype(jnp.bfloat16), "blk", -1).astype(
        jnp.float32
    )
    from_prior = passed_along(partial_terms[2 * genes :].astype(jnp.bfloat16), "blk", 1).astype(
        jnp.float32
    )
    summed = partial_terms[genes : 2 * genes] + from_next + from_prior
    key_grad = (summed[:, 0] * scale).astype(jnp.bfloat16)
    value_grad = summed[:, 1].astype(jnp.bfloat16)
    return (
        lax.all_to_all(query_grad, "uly", split_axis=0, concat_axis=1, tiled=True),
        lax.all_to_all(key_grad, "uly", split_axis=0, concat_axis=1, tiled=True),
        lax.all_to_all(value_grad, "uly", split_axis=0, concat_axis=1, tiled=True),
    )


def flat_index(axes):
    index = 0
    for axis in axes:
        index = index * lax.axis_size(axis) + lax.axis_index(axis)
    return index


def same_core(here):
    return (here >> 1) & 1


def even_places(here):
    return (here ^ (here >> 1) ^ (here >> 2)) & 1


def hop(first, second=None, chooser=same_core):
    if second is None:
        return lambda here: first
    return lambda here: first + (second - first) * chooser(here)


STAY = hop(0)
CORE = hop(2)
FAR = hop(5)
FAR_CORE = hop(7)
SIDE = hop(4, 1)
OTHER_SIDE = hop(1, 4)
SIDE_CORE = hop(6, 3, even_places)
OTHER_SIDE_CORE = hop(3, 6, even_places)

INWARD = (SIDE, FAR_CORE, OTHER_SIDE, SIDE_CORE, OTHER_SIDE_CORE, FAR, CORE)
OUTWARD = (SIDE, FAR, FAR_CORE, OTHER_SIDE, SIDE_CORE, OTHER_SIDE_CORE, CORE)
FIRST = 2
EARLY = 2
LATE = 5
DONE = 0
AFTER = {5: 0, 6: 1}
EXPONENT = math.log2(math.e) / math.sqrt(HEAD_DIM)


def exchange(block, distance):
    places = range(lax.axis_size(GROUP))
    return lax.ppermute(block, GROUP, [(i, i ^ distance(i)) for i in places])


def part(ref, n):
    return ref.at[:, n * HEAD_DIM : (n + 1) * HEAD_DIM]


def head_of(ref, head):
    return ref.at[:, pl.ds(pl.multiple_of(head * HEAD_DIM, HEAD_DIM), HEAD_DIM)]


def run(copies):
    for copy in copies:
        copy.start()
    for copy in copies:
        copy.wait()


def pack_kernel(distances, *refs):
    count = len(distances)
    extras = (len(refs) - 1 - count - 4) // 2
    sources, outs, sems = refs[: 4 + extras], refs[4 + extras : -1], refs[-1]
    here = flat_index(GROUP)
    pairs = list(zip(sources[4:], outs[count:]))
    for distance, slab in zip(distances, outs):
        for n, array in enumerate(sources[:4]):
            pairs.append((head_of(array, here ^ distance(here)), part(slab, n)))
    run([pltpu.make_async_copy(*pair, sems.at[n]) for n, pair in enumerate(pairs)])


def unpack_kernel(distances, *refs):
    slabs, arrays, sems = refs[: len(distances)], refs[-4:-1], refs[-1]
    here = flat_index(GROUP)
    pairs = []
    for distance, slab in zip(distances, slabs):
        for n, array in enumerate(arrays):
            pairs.append((part(slab, n), head_of(array, here ^ distance(here))))
    run([pltpu.make_async_copy(*pair, sems.at[n]) for n, pair in enumerate(pairs)])


def near_cells(c):
    return (c, c ^ 1, c ^ 3)


def key_places(c):
    return [2 * n + a for n in near_cells(c) for a in range(2)]


def blocks_of(value):
    return [value[r : r + 128] for r in range(0, value.shape[0], 128)]


def seen_by(mask_ref, here, key, queries):
    flags = [jnp.full((1, 128), mask_ref[here ^ query, here ^ key]) for query in queries]
    return jnp.concatenate(flags, axis=1) > 0


def weights(scores, seen, top):
    return [
        jnp.exp2(block * EXPONENT - jnp.where(flag, top, 1e30)) for block, flag in zip(scores, seen)
    ]


def top_of(scores, seen):
    top = jnp.full((1, scores[0].shape[1]), -1e30, jnp.float32)
    for block, flag in zip(scores, seen):
        top = jnp.maximum(top, jnp.where(flag, jnp.max(block, axis=0, keepdims=True), -1e30))
    return top * EXPONENT


def sum_of(blocks):
    total = blocks[0]
    for block in blocks[1:]:
        total = total + block
    return jnp.sum(total, axis=0, keepdims=True)


def query_grad(keys, dscores):
    low = (t_times(keys, dscores) * (1.0 / math.sqrt(HEAD_DIM))).T.astype(jnp.bfloat16)
    return low.reshape(-1, 128, HEAD_DIM)


def early_kernel(distances, mask_ref, *refs):
    slabs, outs = refs[:-7], refs[-7:]
    stack_ref, exps_ref, dprobs_ref, stats_ref, seen_ref, done_ref, query_ref = outs
    here = flat_index(GROUP)
    for distance, slab in zip(distances, slabs):
        stack_ref[distance(here)] = slab[...]

    def take(places, n):
        columns = slice(n * HEAD_DIM, (n + 1) * HEAD_DIM)
        return jnp.concatenate([stack_ref[place, :, columns] for place in places], axis=0)

    cells = stack_ref.shape[0] // 2
    present = [[p for p in (2 * c, 2 * c + 1) if p != LATE] for c in range(cells)]
    for c in range(cells):
        q, g = take(present[c], 0), take(present[c], 3)
        width = q.shape[0]
        keys = [place for place in key_places(c) if place != LATE]
        scores = [b for n in near_cells(c) for b in blocks_of(times_t(take(present[n], 1), q))]
        dprobs = [b for n in near_cells(c) for b in blocks_of(times_t(take(present[n], 2), g))]
        seen = [seen_by(mask_ref, here, key, present[c]) for key in keys]
        top = top_of(scores, seen)
        exps = weights(scores, seen, top)
        total = sum_of(exps)
        product = sum_of([e * d for e, d in zip(exps, dprobs)])
        if c == DONE:
            inverse = 1.0 / total
            delta = product * inverse
            terms = []
            for n, (weight, term) in enumerate(zip(exps, dprobs)):
                probs = weight * inverse
                terms.append((probs * (term - delta)).astype(jnp.bfloat16))
                done_ref[0, 128 * n : 128 * (n + 1)] = probs.astype(jnp.bfloat16)
                done_ref[1, 128 * n : 128 * (n + 1)] = terms[n]
            query_ref[...] = query_grad(take(key_places(c), 1), jnp.concatenate(terms, axis=0))
            continue
        for key, weight, term in zip(keys, exps, dprobs):
            row = 128 * key_places(c).index(key)
            exps_ref[c, row : row + 128, :width] = weight
            dprobs_ref[c, row : row + 128, :width] = term
        stats_ref[c, 0:1, :width] = top
        stats_ref[c, 1:2, :width] = total
        stats_ref[c, 2:3, :width] = product
        for n, key in enumerate(key_places(c)):
            flags = seen_by(mask_ref, here, key, (2 * c, 2 * c + 1))
            seen_ref[c, n : n + 1] = flags.astype(jnp.float32)


def late_kernel(distances, slab, *refs):
    stack_ref, exps_ref, dprobs_ref, stats_ref, seen_ref, done_ref, query_ref = refs[:7]
    outs, out_ref = refs[7:-1], refs[-1]
    here = flat_index(GROUP)
    fixed = [distance(here) for distance in distances]
    fixed = {place: out for place, out in zip(fixed, outs) if isinstance(place, int)}
    scale = 1.0 / math.sqrt(HEAD_DIM)
    cells = stack_ref.shape[0] // 2

    def take(places, n):
        columns = slice(n * HEAD_DIM, (n + 1) * HEAD_DIM)
        parts = [slab[:, columns] if p == LATE else stack_ref[p, :, columns] for p in places]
        return jnp.concatenate(parts, axis=0)

    def whole(n):
        return [take((2 * c, 2 * c + 1), n) for c in range(cells)]

    q, k, v, g = (whole(n) for n in range(4))

    units = [(c, (2 * c, 2 * c + 1)) for c in range(cells) if c not in (DONE, LATE // 2)]
    units = [(LATE // 2, (place,)) for place in (LATE - 1, LATE)] + units
    fresh = [[p for p in key_places(c) if LATE in (p, *queries)] for c, queries in units]
    scores, dprobs, exps, inverse, delta, early_inverse = ([None] * len(units) for _ in range(6))
    for u, (c, queries) in enumerate(units):
        groups = [(LATE,)] if LATE not in queries else [(2 * n, 2 * n + 1) for n in near_cells(c)]
        groups = groups if fresh[u] else []
        mine_q, mine_g = take(queries, 0), take(queries, 3)
        scores[u] = [b for keys in groups for b in blocks_of(times_t(take(keys, 1), mine_q))]
        dprobs[u] = [b for keys in groups for b in blocks_of(times_t(take(keys, 2), mine_g))]
    seen = []
    for (c, queries), keys in zip(units, fresh):
        first = 128 * (queries[0] - 2 * c)
        columns = slice(first, first + 128 * len(queries))
        rows = [key_places(c).index(key) for key in keys]
        seen.append([seen_ref[c, n : n + 1, columns] > 0 for n in rows])
    tops = [top_of(blocks, flags) if blocks else None for blocks, flags in zip(scores, seen)]
    for u, (c, queries) in enumerate(units):
        early = LATE not in queries
        if early:
            top, total, product = (
                stats_ref[c, n : n + 1, : 128 * len(queries)] for n in range(3)
            )
        shrink = None
        if fresh[u]:
            new_top = jnp.maximum(top, tops[u]) if early else tops[u]
            exps[u] = weights(scores[u], seen[u], new_top)
            new_total = sum_of(exps[u])
            new_product = sum_of([e * d for e, d in zip(exps[u], dprobs[u])])
            if early:
                shrink = jnp.exp2(top - new_top)
                new_total = new_total + total * shrink
                new_product = new_product + product * shrink
            total, product = new_total, new_product
        inverse[u] = 1.0 / total
        delta[u] = product * inverse[u]
        early_inverse[u] = inverse[u] if shrink is None else inverse[u] * shrink

    def finished(u):
        c, queries = units[u]
        probs_low, dscores = [], []
        for n, key in enumerate(key_places(c)):
            if key in fresh[u]:
                index = fresh[u].index(key)
                probs, term = exps[u][index] * inverse[u], dprobs[u][index]
            else:
                place = (c, slice(128 * n, 128 * (n + 1)), slice(0, 128 * len(queries)))
                probs, term = exps_ref[place] * early_inverse[u], dprobs_ref[place]
            probs_low.append(probs.astype(jnp.bfloat16))
            dscores.append((probs * (term - delta[u])).astype(jnp.bfloat16))
        return probs_low, dscores

    def put(n, c, value):
        low = value.astype(jnp.bfloat16).reshape(2, 128, HEAD_DIM)
        for place in (2 * c, 2 * c + 1):
            out = fixed.get(place, out_ref.at[place])
            out[:, n * HEAD_DIM : (n + 1) * HEAD_DIM] = low[place - 2 * c]

    def joined(blocks, c, axis):
        return jnp.concatenate([blocks[n] for n in near_cells(c)], axis=axis)

    probs_low = [{} for _ in range(cells)]
    dscores = [{} for _ in range(cells)]

    def rows_of(c):
        if c == DONE:
            pair = [blocks_of(done_ref[n]) for n in range(2)]
        elif LATE // 2 == c:
            sides = zip(finished(0), finished(1))
            pair = [
                [jnp.concatenate(both, axis=1) for both in zip(left, right)] for left, right in sides
            ]
        else:
            pair = finished(units.index((c, (2 * c, 2 * c + 1))))
        for t, n in enumerate(near_cells(c)):
            probs_low[n][c] = jnp.concatenate(pair[0][2 * t : 2 * t + 2], axis=0)
            dscores[n][c] = jnp.concatenate(pair[1][2 * t : 2 * t + 2], axis=0)

    def put_value_grad(c):
        low = joined(probs_low[c], c, 1)
        put(2, c, jnp.dot(low, joined(g, c, 0), preferred_element_type=jnp.float32))

    def put_key_grad(c):
        low = joined(dscores[c], c, 1)
        put(1, c, jnp.dot(low, joined(q, c, 0), preferred_element_type=jnp.float32) * scale)

    def put_query_grad(c):
        if c == DONE:
            put(0, c, query_ref[...])
            return
        terms = jnp.concatenate([dscores[n][c] for n in near_cells(c)], axis=0)
        put(0, c, query_grad(joined(k, c, 0), terms))

    rows_of(2)
    rows_of(1)
    rows_of(3)
    rows_of(0)
    put_value_grad(0)
    put_value_grad(1)
    put_value_grad(2)
    put_value_grad(3)
    put_key_grad(0)
    put_key_grad(1)
    put_key_grad(2)
    put_key_grad(3)
    put_query_grad(0)
    put_query_grad(1)
    put_query_grad(2)
    put_query_grad(3)
    for distance, out in zip(distances, outs):
        if not isinstance(distance(here), int):
            out[...] = out_ref[distance(here)]


SMEM = pl.BlockSpec(memory_space=pltpu.SMEM)
VMEM = pl.BlockSpec(memory_space=pltpu.VMEM)
ANY = pl.BlockSpec(memory_space=pl.ANY)


def slab_shape(tokens, parts):
    return jax.ShapeDtypeStruct((tokens, parts * HEAD_DIM), jnp.bfloat16)


def pack(arrays, distances, name, *extras):
    tokens = arrays[0].shape[0]
    count = len(distances)
    outs = [slab_shape(tokens, 4)] * count
    outs += [jax.ShapeDtypeStruct(extra.shape, extra.dtype) for extra in extras]
    return pl.pallas_call(
        functools.partial(pack_kernel, distances),
        out_shape=outs,
        in_specs=[ANY] * (4 + len(extras)),
        out_specs=[ANY] * len(outs),
        scratch_shapes=[pltpu.SemaphoreType.DMA((4 * count + len(extras),))],
        compiler_params=pltpu.CompilerParams(vmem_limit_bytes=MIB),
        name=name,
    )(*arrays, *extras)


def unpack(whole, distances, slabs, name, *arrays):
    count = len(distances)
    return pl.pallas_call(
        functools.partial(unpack_kernel, distances),
        out_shape=[whole] * 3,
        in_specs=[ANY] * (count + len(arrays)),
        out_specs=[ANY] * 3,
        scratch_shapes=[pltpu.SemaphoreType.DMA((3 * count,))],
        compiler_params=pltpu.CompilerParams(vmem_limit_bytes=MIB),
        input_output_aliases={count + n: n for n in range(len(arrays))},
        name=name,
    )(*slabs, *arrays)


def by_heads(queries, keys, values, out_grad, block_mask):
    devices = lax.axis_size(GROUP)
    cells = lax.axis_size("blk")
    tokens = queries.shape[0]
    *arrays, block_mask = [
        pltpu.with_memory_space_constraint(array, pltpu.HBM)
        for array in (queries, keys, values, out_grad, block_mask)
    ]
    sent = pack(arrays, INWARD[:FIRST], "pack_first")
    arrays, sent = lax.optimization_barrier((arrays, sent))
    *rest, own, block_mask = pack(arrays, INWARD[FIRST:] + (STAY,), "pack_rest", block_mask)
    got = list(sent) + rest
    for n, distance in enumerate(INWARD):
        if n in AFTER:
            got[n], got[AFTER[n]] = lax.optimization_barrier((got[n], got[AFTER[n]]))
        got[n] = exchange(got[n], distance)
    soon = [n for n, distance in enumerate(INWARD) if distance is not FAR]
    pairs = jax.ShapeDtypeStruct((cells, 6 * tokens, 2 * tokens), jnp.float32)
    partial = pl.pallas_call(
        functools.partial(early_kernel, [INWARD[n] for n in soon] + [STAY]),
        out_shape=[
            jax.ShapeDtypeStruct((devices, tokens, 4 * HEAD_DIM), jnp.bfloat16),
            pairs,
            pairs,
            jax.ShapeDtypeStruct((cells, 8, 2 * tokens), jnp.float32),
            jax.ShapeDtypeStruct((cells, 8, 2 * tokens), jnp.float32),
            jax.ShapeDtypeStruct((2, 6 * tokens, 2 * tokens), jnp.bfloat16),
            jax.ShapeDtypeStruct((2, tokens, HEAD_DIM), jnp.bfloat16),
        ],
        in_specs=[SMEM] + [VMEM] * (devices - 1),
        out_specs=[VMEM] * 7,
        compiler_params=pltpu.CompilerParams(vmem_limit_bytes=24 * MIB),
        name="early",
    )(block_mask, *[got[n] for n in soon], own)
    distances = OUTWARD + (STAY,)
    grads = pl.pallas_call(
        functools.partial(late_kernel, distances),
        out_shape=[slab_shape(tokens, 3)] * devices,
        in_specs=[VMEM] * 8,
        out_specs=[VMEM] * devices,
        scratch_shapes=[pltpu.VMEM((devices, tokens, 3 * HEAD_DIM), jnp.bfloat16)],
        compiler_params=pltpu.CompilerParams(vmem_limit_bytes=24 * MIB),
        name="late",
    )(got[INWARD.index(FAR)], *partial)
    back = [exchange(grad, distance) for grad, distance in zip(grads, OUTWARD)] + [grads[-1]]
    whole = jax.ShapeDtypeStruct(queries.shape, queries.dtype)
    grads = unpack(whole, distances[-1:] + distances[:EARLY], back[-1:] + back[:EARLY], "unpack")
    return unpack(whole, distances[EARLY:-1], back[EARLY:-1], "unpack_last", *grads)


def local(queries, keys, values, out_grad, block_mask):
    heads = queries.shape[1] // HEAD_DIM
    cells, halves = lax.axis_size("blk"), lax.axis_size("uly")
    if (cells, halves) == (4, 2) and heads == cells * halves and queries.shape[0] == 128:
        return by_heads(queries, keys, values, out_grad, block_mask)
    return by_cells(queries, keys, values, out_grad, block_mask)


def solution(mesh):
    return jax.shard_map(
        local,
        mesh=mesh,
        in_specs=(
            P(("batch", "blk", "uly"), None),
            P(("batch", "blk", "uly"), None),
            P(("batch", "blk", "uly"), None),
            P(("batch", "blk", "uly"), None),
            P("batch", None),
        ),
        out_specs=(
            P(("batch", "blk", "uly"), None),
            P(("batch", "blk", "uly"), None),
            P(("batch", "blk", "uly"), None),
        ),
        check_vma=False,
    )
```

```python
import functools
import math

import jax
import jax.numpy as jnp
from jax import lax
from jax.experimental import pallas as pl
from jax.experimental.pallas import tpu as pltpu
from jax.sharding import PartitionSpec as P

HEAD_DIM = 128
MIB = 1024 * 1024
GROUP = ("blk", "uly")


def padded(block, sides, width):
    for axis, dim in sides:
        count = lax.axis_size(axis)
        forward = [(i, i + 1) for i in range(count - 1)]
        forward.append((count - 1, 0))
        backward = [(target, source) for source, target in forward]
        low = lax.ppermute(
            lax.slice_in_dim(block, block.shape[dim] - width, None, axis=dim), axis, forward
        )
        high = lax.ppermute(lax.slice_in_dim(block, 0, width, axis=dim), axis, backward)
        block = jnp.concatenate([low, block, high], axis=dim)
    return block


def passed_along(block, axis, distance):
    devices = range(lax.axis_size(axis))
    route = [((i - distance) % len(devices), i) for i in devices]
    return lax.ppermute(block, axis, route)


def times_t(left, right):
    return lax.dot_general(
        left, right, (((1,), (1,)), ((), ())), preferred_element_type=jnp.float32
    )


def t_times(left, right):
    return lax.dot_general(
        left, right, (((0,), (0,)), ((), ())), preferred_element_type=jnp.float32
    )


def widen_blocks(mask_blocks):
    return jnp.repeat(jnp.repeat(mask_blocks > 0, 128, axis=0), 128, axis=1)


def by_cells(queries, keys, values, out_grad, block_mask):
    local_q, local_k, local_v, local_g = (
        lax.all_to_all(queries, "uly", split_axis=1, concat_axis=0, tiled=True),
        lax.all_to_all(keys, "uly", split_axis=1, concat_axis=0, tiled=True),
        lax.all_to_all(values, "uly", split_axis=1, concat_axis=0, tiled=True),
        lax.all_to_all(out_grad, "uly", split_axis=1, concat_axis=0, tiled=True),
    )
    genes = local_q.shape[0]
    heads_here = local_q.shape[1] // HEAD_DIM
    scale = 1.0 / math.sqrt(HEAD_DIM)
    cells = lax.axis_size("blk")
    here = lax.axis_index("blk")
    per_cell = genes // 128
    near = (here + jnp.array([-1, 0, 1], dtype=jnp.int32) + cells) % cells
    mask_rows = lax.dynamic_slice_in_dim(block_mask, here * per_cell, per_cell, 0).reshape(
        per_cell, cells, per_cell
    )
    row_mask = widen_blocks(jnp.take(mask_rows, near, axis=1).reshape(per_cell, 3 * per_cell))
    pairs = jnp.stack([local_k, local_v], axis=1)
    band = padded(pairs, (("blk", 0),), genes)
    q_grads = []
    k_parts = []
    v_parts = []
    for head in range(heads_here):
        lower = head * HEAD_DIM
        upper = lower + HEAD_DIM
        q_head = local_q[:, lower:upper]
        g_head = local_g[:, lower:upper]
        k_band = band[:, 0, lower:upper]
        v_band = band[:, 1, lower:upper]
        scores = jnp.where(row_mask, times_t(q_head, k_band) * scale, -1e30)
        top = jnp.max(scores, axis=1, keepdims=True)
        total = jnp.sum(jnp.where(row_mask, jnp.exp(scores - top), 0.0), axis=1, keepdims=True)
        lse = top + jnp.log(total)
        probs = jnp.where(row_mask, jnp.exp(scores - lse), 0.0)
        dprobs = times_t(g_head, v_band)
        delta = jnp.sum(probs * dprobs, axis=1, keepdims=True)
        dscores = (probs * (dprobs - delta)).astype(jnp.bfloat16)
        q_grads.append(
            (jnp.dot(dscores, k_band, preferred_element_type=jnp.float32) * scale).astype(
                jnp.bfloat16
            )
        )
        k_parts.append(t_times(dscores, q_head))
        v_parts.append(t_times(probs.astype(jnp.bfloat16), g_head))
    query_grad = jnp.concatenate(q_grads, axis=1)
    partial_terms = jnp.stack(
        [jnp.concatenate(k_parts, axis=1), jnp.concatenate(v_parts, axis=1)], axis=1
    )
    from_next = passed_along(partial_terms[:genes].astype(jnp.bfloat16), "blk", -1).astype(
        jnp.float32
    )
    from_prior = passed_along(partial_terms[2 * genes :].astype(jnp.bfloat16), "blk", 1).astype(
        jnp.float32
    )
    summed = partial_terms[genes : 2 * genes] + from_next + from_prior
    key_grad = (summed[:, 0] * scale).astype(jnp.bfloat16)
    value_grad = summed[:, 1].astype(jnp.bfloat16)
    return (
        lax.all_to_all(query_grad, "uly", split_axis=0, concat_axis=1, tiled=True),
        lax.all_to_all(key_grad, "uly", split_axis=0, concat_axis=1, tiled=True),
        lax.all_to_all(value_grad, "uly", split_axis=0, concat_axis=1, tiled=True),
    )


def flat_index(axes):
    index = 0
    for axis in axes:
        index = index * lax.axis_size(axis) + lax.axis_index(axis)
    return index


def same_core(here):
    return (here >> 1) & 1


def even_places(here):
    return (here ^ (here >> 1) ^ (here >> 2)) & 1


def hop(first, second=None, chooser=same_core):
    if second is None:
        return lambda here: first
    return lambda here: first + (second - first) * chooser(here)


STAY = hop(0)
CORE = hop(2)
FAR = hop(5)
FAR_CORE = hop(7)
SIDE = hop(4, 1)
OTHER_SIDE = hop(1, 4)
SIDE_CORE = hop(6, 3, even_places)
OTHER_SIDE_CORE = hop(3, 6, even_places)

INWARD = (FAR_CORE, SIDE, CORE, OTHER_SIDE, SIDE_CORE, FAR, OTHER_SIDE_CORE)
OUTWARD = (FAR, FAR_CORE, SIDE, OTHER_SIDE, SIDE_CORE, OTHER_SIDE_CORE, CORE)
FIRST = 2
EARLY = 2
LATE = 5
DONE = 0
AFTER = {}
EXPONENT = math.log2(math.e) / math.sqrt(HEAD_DIM)


def exchange(block, distance):
    places = range(lax.axis_size(GROUP))
    return lax.ppermute(block, GROUP, [(i, i ^ distance(i)) for i in places])


def part(ref, n):
    return ref.at[:, n * HEAD_DIM : (n + 1) * HEAD_DIM]


def head_of(ref, head):
    return ref.at[:, pl.ds(pl.multiple_of(head * HEAD_DIM, HEAD_DIM), HEAD_DIM)]


def run(copies):
    for copy in copies:
        copy.start()
    for copy in copies:
        copy.wait()


def pack_kernel(distances, *refs):
    count = len(distances)
    extras = (len(refs) - 1 - count - 4) // 2
    sources, outs, sems = refs[: 4 + extras], refs[4 + extras : -1], refs[-1]
    here = flat_index(GROUP)
    pairs = list(zip(sources[4:], outs[count:]))
    for distance, slab in zip(distances, outs):
        for n, array in enumerate(sources[:4]):
            pairs.append((head_of(array, here ^ distance(here)), part(slab, n)))
    run([pltpu.make_async_copy(*pair, sems.at[n]) for n, pair in enumerate(pairs)])


def unpack_kernel(distances, *refs):
    slabs, arrays, sems = refs[: len(distances)], refs[-4:-1], refs[-1]
    here = flat_index(GROUP)
    pairs = []
    for distance, slab in zip(distances, slabs):
        for n, array in enumerate(arrays):
            pairs.append((part(slab, n), head_of(array, here ^ distance(here))))
    run([pltpu.make_async_copy(*pair, sems.at[n]) for n, pair in enumerate(pairs)])


def near_cells(c):
    return (c, c ^ 1, c ^ 3)


def key_places(c):
    return [2 * n + a for n in near_cells(c) for a in range(2)]


def blocks_of(value):
    return [value[r : r + 128] for r in range(0, value.shape[0], 128)]


def seen_by(mask_ref, here, key, queries):
    flags = [jnp.full((1, 128), mask_ref[here ^ query, here ^ key]) for query in queries]
    return jnp.concatenate(flags, axis=1) > 0


def weights(scores, seen, top):
    return [
        jnp.exp2(block * EXPONENT - jnp.where(flag, top, 1e30)) for block, flag in zip(scores, seen)
    ]


def top_of(scores, seen):
    top = jnp.full((1, scores[0].shape[1]), -1e30, jnp.float32)
    for block, flag in zip(scores, seen):
        top = jnp.maximum(top, jnp.where(flag, jnp.max(block, axis=0, keepdims=True), -1e30))
    return top * EXPONENT


def sum_of(blocks):
    total = blocks[0]
    for block in blocks[1:]:
        total = total + block
    return jnp.sum(total, axis=0, keepdims=True)


def query_grad(keys, dscores):
    low = (t_times(keys, dscores) * (1.0 / math.sqrt(HEAD_DIM))).T.astype(jnp.bfloat16)
    return low.reshape(-1, 128, HEAD_DIM)


def early_kernel(distances, mask_ref, *refs):
    slabs, outs = refs[:-7], refs[-7:]
    stack_ref, exps_ref, dprobs_ref, stats_ref, seen_ref, done_ref, query_ref = outs
    here = flat_index(GROUP)
    for distance, slab in zip(distances, slabs):
        stack_ref[distance(here)] = slab[...]

    def take(places, n):
        columns = slice(n * HEAD_DIM, (n + 1) * HEAD_DIM)
        return jnp.concatenate([stack_ref[place, :, columns] for place in places], axis=0)

    cells = stack_ref.shape[0] // 2
    present = [[p for p in (2 * c, 2 * c + 1) if p != LATE] for c in range(cells)]
    for c in range(cells):
        q, g = take(present[c], 0), take(present[c], 3)
        width = q.shape[0]
        keys = [place for place in key_places(c) if place != LATE]
        scores = [b for n in near_cells(c) for b in blocks_of(times_t(take(present[n], 1), q))]
        dprobs = [b for n in near_cells(c) for b in blocks_of(times_t(take(present[n], 2), g))]
        seen = [seen_by(mask_ref, here, key, present[c]) for key in keys]
        top = top_of(scores, seen)
        exps = weights(scores, seen, top)
        total = sum_of(exps)
        product = sum_of([e * d for e, d in zip(exps, dprobs)])
        if c == DONE:
            inverse = 1.0 / total
            delta = product * inverse
            terms = []
            for n, (weight, term) in enumerate(zip(exps, dprobs)):
                probs = weight * inverse
                terms.append((probs * (term - delta)).astype(jnp.bfloat16))
                done_ref[0, 128 * n : 128 * (n + 1)] = probs.astype(jnp.bfloat16)
                done_ref[1, 128 * n : 128 * (n + 1)] = terms[n]
            query_ref[...] = query_grad(take(key_places(c), 1), jnp.concatenate(terms, axis=0))
            continue
        for key, weight, term in zip(keys, exps, dprobs):
            row = 128 * key_places(c).index(key)
            exps_ref[c, row : row + 128, :width] = weight
            dprobs_ref[c, row : row + 128, :width] = term
        stats_ref[c, 0:1, :width] = top
        stats_ref[c, 1:2, :width] = total
        stats_ref[c, 2:3, :width] = product
        for n, key in enumerate(key_places(c)):
            flags = seen_by(mask_ref, here, key, (2 * c, 2 * c + 1))
            seen_ref[c, n : n + 1] = flags.astype(jnp.float32)


def late_kernel(distances, slab, *refs):
    stack_ref, exps_ref, dprobs_ref, stats_ref, seen_ref, done_ref, query_ref = refs[:7]
    outs, out_ref = refs[7:-1], refs[-1]
    here = flat_index(GROUP)
    fixed = [distance(here) for distance in distances]
    fixed = {place: out for place, out in zip(fixed, outs) if isinstance(place, int)}
    scale = 1.0 / math.sqrt(HEAD_DIM)
    cells = stack_ref.shape[0] // 2

    def take(places, n):
        columns = slice(n * HEAD_DIM, (n + 1) * HEAD_DIM)
        parts = [slab[:, columns] if p == LATE else stack_ref[p, :, columns] for p in places]
        return jnp.concatenate(parts, axis=0)

    def whole(n):
        return [take((2 * c, 2 * c + 1), n) for c in range(cells)]

    q, k, v, g = (whole(n) for n in range(4))

    units = [(c, (2 * c, 2 * c + 1)) for c in range(cells) if c not in (DONE, LATE // 2)]
    units = [(LATE // 2, (place,)) for place in (LATE - 1, LATE)] + units
    fresh = [[p for p in key_places(c) if LATE in (p, *queries)] for c, queries in units]
    scores, dprobs, exps, inverse, delta, early_inverse = ([None] * len(units) for _ in range(6))
    for u, (c, queries) in enumerate(units):
        groups = [(LATE,)] if LATE not in queries else [(2 * n, 2 * n + 1) for n in near_cells(c)]
        groups = groups if fresh[u] else []
        mine_q, mine_g = take(queries, 0), take(queries, 3)
        scores[u] = [b for keys in groups for b in blocks_of(times_t(take(keys, 1), mine_q))]
        dprobs[u] = [b for keys in groups for b in blocks_of(times_t(take(keys, 2), mine_g))]
    seen = []
    for (c, queries), keys in zip(units, fresh):
        first = 128 * (queries[0] - 2 * c)
        columns = slice(first, first + 128 * len(queries))
        rows = [key_places(c).index(key) for key in keys]
        seen.append([seen_ref[c, n : n + 1, columns] > 0 for n in rows])
    tops = [top_of(blocks, flags) if blocks else None for blocks, flags in zip(scores, seen)]
    for u, (c, queries) in enumerate(units):
        early = LATE not in queries
        if early:
            top, total, product = (
                stats_ref[c, n : n + 1, : 128 * len(queries)] for n in range(3)
            )
        shrink = None
        if fresh[u]:
            new_top = jnp.maximum(top, tops[u]) if early else tops[u]
            exps[u] = weights(scores[u], seen[u], new_top)
            new_total = sum_of(exps[u])
            new_product = sum_of([e * d for e, d in zip(exps[u], dprobs[u])])
            if early:
                shrink = jnp.exp2(top - new_top)
                new_total = new_total + total * shrink
                new_product = new_product + product * shrink
            total, product = new_total, new_product
        inverse[u] = 1.0 / total
        delta[u] = product * inverse[u]
        early_inverse[u] = inverse[u] if shrink is None else inverse[u] * shrink

    def finished(u):
        c, queries = units[u]
        probs_low, dscores = [], []
        for n, key in enumerate(key_places(c)):
            if key in fresh[u]:
                index = fresh[u].index(key)
                probs, term = exps[u][index] * inverse[u], dprobs[u][index]
            else:
                place = (c, slice(128 * n, 128 * (n + 1)), slice(0, 128 * len(queries)))
                probs, term = exps_ref[place] * early_inverse[u], dprobs_ref[place]
            probs_low.append(probs.astype(jnp.bfloat16))
            dscores.append((probs * (term - delta[u])).astype(jnp.bfloat16))
        return probs_low, dscores

    def put(n, c, value):
        low = value.astype(jnp.bfloat16).reshape(2, 128, HEAD_DIM)
        for place in (2 * c, 2 * c + 1):
            out = fixed.get(place, out_ref.at[place])
            out[:, n * HEAD_DIM : (n + 1) * HEAD_DIM] = low[place - 2 * c]

    def joined(blocks, c, axis):
        return jnp.concatenate([blocks[n] for n in near_cells(c)], axis=axis)

    probs_low = [{} for _ in range(cells)]
    dscores = [{} for _ in range(cells)]

    def rows_of(c):
        if c == DONE:
            pair = [blocks_of(done_ref[n]) for n in range(2)]
        elif LATE // 2 == c:
            sides = zip(finished(0), finished(1))
            pair = [
                [jnp.concatenate(both, axis=1) for both in zip(left, right)] for left, right in sides
            ]
        else:
            pair = finished(units.index((c, (2 * c, 2 * c + 1))))
        for t, n in enumerate(near_cells(c)):
            probs_low[n][c] = jnp.concatenate(pair[0][2 * t : 2 * t + 2], axis=0)
            dscores[n][c] = jnp.concatenate(pair[1][2 * t : 2 * t + 2], axis=0)

    def put_value_grad(c):
        low = joined(probs_low[c], c, 1)
        put(2, c, jnp.dot(low, joined(g, c, 0), preferred_element_type=jnp.float32))

    def put_key_grad(c):
        low = joined(dscores[c], c, 1)
        put(1, c, jnp.dot(low, joined(q, c, 0), preferred_element_type=jnp.float32) * scale)

    def put_query_grad(c):
        if c == DONE:
            put(0, c, query_ref[...])
            return
        terms = jnp.concatenate([dscores[n][c] for n in near_cells(c)], axis=0)
        put(0, c, query_grad(joined(k, c, 0), terms))

    rows_of(2)
    rows_of(1)
    rows_of(3)
    rows_of(0)
    put_value_grad(0)
    put_value_grad(1)
    put_value_grad(2)
    put_value_grad(3)
    put_key_grad(0)
    put_key_grad(1)
    put_key_grad(2)
    put_key_grad(3)
    put_query_grad(0)
    put_query_grad(1)
    put_query_grad(2)
    put_query_grad(3)
    for distance, out in zip(distances, outs):
        if not isinstance(distance(here), int):
            out[...] = out_ref[distance(here)]


SMEM = pl.BlockSpec(memory_space=pltpu.SMEM)
VMEM = pl.BlockSpec(memory_space=pltpu.VMEM)
ANY = pl.BlockSpec(memory_space=pl.ANY)


def slab_shape(tokens, parts):
    return jax.ShapeDtypeStruct((tokens, parts * HEAD_DIM), jnp.bfloat16)


def pack(arrays, distances, name, *extras):
    tokens = arrays[0].shape[0]
    count = len(distances)
    outs = [slab_shape(tokens, 4)] * count
    outs += [jax.ShapeDtypeStruct(extra.shape, extra.dtype) for extra in extras]
    return pl.pallas_call(
        functools.partial(pack_kernel, distances),
        out_shape=outs,
        in_specs=[ANY] * (4 + len(extras)),
        out_specs=[ANY] * len(outs),
        scratch_shapes=[pltpu.SemaphoreType.DMA((4 * count + len(extras),))],
        compiler_params=pltpu.CompilerParams(vmem_limit_bytes=MIB),
        name=name,
    )(*arrays, *extras)


def unpack(whole, distances, slabs, name, *arrays):
    count = len(distances)
    return pl.pallas_call(
        functools.partial(unpack_kernel, distances),
        out_shape=[whole] * 3,
        in_specs=[ANY] * (count + len(arrays)),
        out_specs=[ANY] * 3,
        scratch_shapes=[pltpu.SemaphoreType.DMA((3 * count,))],
        compiler_params=pltpu.CompilerParams(vmem_limit_bytes=MIB),
        input_output_aliases={count + n: n for n in range(len(arrays))},
        name=name,
    )(*slabs, *arrays)


def by_heads(queries, keys, values, out_grad, block_mask):
    devices = lax.axis_size(GROUP)
    cells = lax.axis_size("blk")
    tokens = queries.shape[0]
    *arrays, block_mask = [
        pltpu.with_memory_space_constraint(array, pltpu.HBM)
        for array in (queries, keys, values, out_grad, block_mask)
    ]
    sent = pack(arrays, INWARD[:FIRST], "pack_first")
    arrays, sent = lax.optimization_barrier((arrays, sent))
    *rest, own, block_mask = pack(arrays, INWARD[FIRST:] + (STAY,), "pack_rest", block_mask)
    got = list(sent) + rest
    for n, distance in enumerate(INWARD):
        if n in AFTER:
            got[n], got[AFTER[n]] = lax.optimization_barrier((got[n], got[AFTER[n]]))
        got[n] = exchange(got[n], distance)
    soon = [n for n, distance in enumerate(INWARD) if distance is not FAR]
    pairs = jax.ShapeDtypeStruct((cells, 6 * tokens, 2 * tokens), jnp.float32)
    partial = pl.pallas_call(
        functools.partial(early_kernel, [INWARD[n] for n in soon] + [STAY]),
        out_shape=[
            jax.ShapeDtypeStruct((devices, tokens, 4 * HEAD_DIM), jnp.bfloat16),
            pairs,
            pairs,
            jax.ShapeDtypeStruct((cells, 8, 2 * tokens), jnp.float32),
            jax.ShapeDtypeStruct((cells, 8, 2 * tokens), jnp.float32),
            jax.ShapeDtypeStruct((2, 6 * tokens, 2 * tokens), jnp.bfloat16),
            jax.ShapeDtypeStruct((2, tokens, HEAD_DIM), jnp.bfloat16),
        ],
        in_specs=[SMEM] + [VMEM] * (devices - 1),
        out_specs=[VMEM] * 7,
        compiler_params=pltpu.CompilerParams(vmem_limit_bytes=24 * MIB),
        name="early",
    )(block_mask, *[got[n] for n in soon], own)
    distances = OUTWARD + (STAY,)
    grads = pl.pallas_call(
        functools.partial(late_kernel, distances),
        out_shape=[slab_shape(tokens, 3)] * devices,
        in_specs=[VMEM] * 8,
        out_specs=[VMEM] * devices,
        scratch_shapes=[pltpu.VMEM((devices, tokens, 3 * HEAD_DIM), jnp.bfloat16)],
        compiler_params=pltpu.CompilerParams(vmem_limit_bytes=24 * MIB),
        name="late",
    )(got[INWARD.index(FAR)], *partial)
    back = [exchange(grad, distance) for grad, distance in zip(grads, OUTWARD)] + [grads[-1]]
    whole = jax.ShapeDtypeStruct(queries.shape, queries.dtype)
    grads = unpack(whole, distances[-1:] + distances[:EARLY], back[-1:] + back[:EARLY], "unpack")
    return unpack(whole, distances[EARLY:-1], back[EARLY:-1], "unpack_last", *grads)


def local(queries, keys, values, out_grad, block_mask):
    heads = queries.shape[1] // HEAD_DIM
    cells, halves = lax.axis_size("blk"), lax.axis_size("uly")
    if (cells, halves) == (4, 2) and heads == cells * halves and queries.shape[0] == 128:
        return by_heads(queries, keys, values, out_grad, block_mask)
    return by_cells(queries, keys, values, out_grad, block_mask)


def solution(mesh):
    return jax.shard_map(
        local,
        mesh=mesh,
        in_specs=(
            P(("batch", "blk", "uly"), None),
            P(("batch", "blk", "uly"), None),
            P(("batch", "blk", "uly"), None),
            P(("batch", "blk", "uly"), None),
            P("batch", None),
        ),
        out_specs=(
            P(("batch", "blk", "uly"), None),
            P(("batch", "blk", "uly"), None),
            P(("batch", "blk", "uly"), None),
        ),
        check_vma=False,
    )
```

```python
import functools
import math

import jax
import jax.numpy as jnp
from jax import lax
from jax.experimental import pallas as pl
from jax.experimental.pallas import tpu as pltpu
from jax.sharding import PartitionSpec as P

HEAD_DIM = 128
MIB = 1024 * 1024
GROUP = ("blk", "uly")


def padded(block, sides, width):
    for axis, dim in sides:
        count = lax.axis_size(axis)
        forward = [(i, i + 1) for i in range(count - 1)]
        forward.append((count - 1, 0))
        backward = [(target, source) for source, target in forward]
        low = lax.ppermute(
            lax.slice_in_dim(block, block.shape[dim] - width, None, axis=dim), axis, forward
        )
        high = lax.ppermute(lax.slice_in_dim(block, 0, width, axis=dim), axis, backward)
        block = jnp.concatenate([low, block, high], axis=dim)
    return block


def passed_along(block, axis, distance):
    devices = range(lax.axis_size(axis))
    route = [((i - distance) % len(devices), i) for i in devices]
    return lax.ppermute(block, axis, route)


def times_t(left, right):
    return lax.dot_general(
        left, right, (((1,), (1,)), ((), ())), preferred_element_type=jnp.float32
    )


def t_times(left, right):
    return lax.dot_general(
        left, right, (((0,), (0,)), ((), ())), preferred_element_type=jnp.float32
    )


def widen_blocks(mask_blocks):
    return jnp.repeat(jnp.repeat(mask_blocks > 0, 128, axis=0), 128, axis=1)


def by_cells(queries, keys, values, out_grad, block_mask):
    local_q, local_k, local_v, local_g = (
        lax.all_to_all(queries, "uly", split_axis=1, concat_axis=0, tiled=True),
        lax.all_to_all(keys, "uly", split_axis=1, concat_axis=0, tiled=True),
        lax.all_to_all(values, "uly", split_axis=1, concat_axis=0, tiled=True),
        lax.all_to_all(out_grad, "uly", split_axis=1, concat_axis=0, tiled=True),
    )
    genes = local_q.shape[0]
    heads_here = local_q.shape[1] // HEAD_DIM
    scale = 1.0 / math.sqrt(HEAD_DIM)
    cells = lax.axis_size("blk")
    here = lax.axis_index("blk")
    per_cell = genes // 128
    near = (here + jnp.array([-1, 0, 1], dtype=jnp.int32) + cells) % cells
    mask_rows = lax.dynamic_slice_in_dim(block_mask, here * per_cell, per_cell, 0).reshape(
        per_cell, cells, per_cell
    )
    row_mask = widen_blocks(jnp.take(mask_rows, near, axis=1).reshape(per_cell, 3 * per_cell))
    pairs = jnp.stack([local_k, local_v], axis=1)
    band = padded(pairs, (("blk", 0),), genes)
    q_grads = []
    k_parts = []
    v_parts = []
    for head in range(heads_here):
        lower = head * HEAD_DIM
        upper = lower + HEAD_DIM
        q_head = local_q[:, lower:upper]
        g_head = local_g[:, lower:upper]
        k_band = band[:, 0, lower:upper]
        v_band = band[:, 1, lower:upper]
        scores = jnp.where(row_mask, times_t(q_head, k_band) * scale, -1e30)
        top = jnp.max(scores, axis=1, keepdims=True)
        total = jnp.sum(jnp.where(row_mask, jnp.exp(scores - top), 0.0), axis=1, keepdims=True)
        lse = top + jnp.log(total)
        probs = jnp.where(row_mask, jnp.exp(scores - lse), 0.0)
        dprobs = times_t(g_head, v_band)
        delta = jnp.sum(probs * dprobs, axis=1, keepdims=True)
        dscores = (probs * (dprobs - delta)).astype(jnp.bfloat16)
        q_grads.append(
            (jnp.dot(dscores, k_band, preferred_element_type=jnp.float32) * scale).astype(
                jnp.bfloat16
            )
        )
        k_parts.append(t_times(dscores, q_head))
        v_parts.append(t_times(probs.astype(jnp.bfloat16), g_head))
    query_grad = jnp.concatenate(q_grads, axis=1)
    partial_terms = jnp.stack(
        [jnp.concatenate(k_parts, axis=1), jnp.concatenate(v_parts, axis=1)], axis=1
    )
    from_next = passed_along(partial_terms[:genes].astype(jnp.bfloat16), "blk", -1).astype(
        jnp.float32
    )
    from_prior = passed_along(partial_terms[2 * genes :].astype(jnp.bfloat16), "blk", 1).astype(
        jnp.float32
    )
    summed = partial_terms[genes : 2 * genes] + from_next + from_prior
    key_grad = (summed[:, 0] * scale).astype(jnp.bfloat16)
    value_grad = summed[:, 1].astype(jnp.bfloat16)
    return (
        lax.all_to_all(query_grad, "uly", split_axis=0, concat_axis=1, tiled=True),
        lax.all_to_all(key_grad, "uly", split_axis=0, concat_axis=1, tiled=True),
        lax.all_to_all(value_grad, "uly", split_axis=0, concat_axis=1, tiled=True),
    )


def flat_index(axes):
    index = 0
    for axis in axes:
        index = index * lax.axis_size(axis) + lax.axis_index(axis)
    return index


def same_core(here):
    return (here >> 1) & 1


def even_places(here):
    return (here ^ (here >> 1) ^ (here >> 2)) & 1


def hop(first, second=None, chooser=same_core):
    if second is None:
        return lambda here: first
    return lambda here: first + (second - first) * chooser(here)


STAY = hop(0)
CORE = hop(2)
FAR = hop(5)
FAR_CORE = hop(7)
SIDE = hop(4, 1)
OTHER_SIDE = hop(1, 4)
SIDE_CORE = hop(6, 3, even_places)
OTHER_SIDE_CORE = hop(3, 6, even_places)

INWARD = (FAR_CORE, SIDE, CORE, OTHER_SIDE, SIDE_CORE, FAR, OTHER_SIDE_CORE)
OUTWARD = (FAR, FAR_CORE, SIDE, OTHER_SIDE, SIDE_CORE, OTHER_SIDE_CORE, CORE)
FIRST = 2
EARLY = 2
LATE = 5
BEYOND = (4, 5, 6, 7)
DONE = 0
AFTER = {}
EXPONENT = math.log2(math.e) / math.sqrt(HEAD_DIM)


def exchange(block, distance):
    places = range(lax.axis_size(GROUP))
    return lax.ppermute(block, GROUP, [(i, i ^ distance(i)) for i in places])


def part(ref, n):
    return ref.at[:, n * HEAD_DIM : (n + 1) * HEAD_DIM]


def head_of(ref, head):
    return ref.at[:, pl.ds(pl.multiple_of(head * HEAD_DIM, HEAD_DIM), HEAD_DIM)]


def run(copies):
    for copy in copies:
        copy.start()
    for copy in copies:
        copy.wait()


def pack_kernel(distances, *refs):
    count = len(distances)
    extras = (len(refs) - 1 - count - 4) // 2
    sources, outs, sems = refs[: 4 + extras], refs[4 + extras : -1], refs[-1]
    here = flat_index(GROUP)
    pairs = list(zip(sources[4:], outs[count:]))
    for distance, slab in zip(distances, outs):
        for n, array in enumerate(sources[:4]):
            pairs.append((head_of(array, here ^ distance(here)), part(slab, n)))
    run([pltpu.make_async_copy(*pair, sems.at[n]) for n, pair in enumerate(pairs)])


def unpack_kernel(distances, *refs):
    slabs, arrays, sems = refs[: len(distances)], refs[-4:-1], refs[-1]
    here = flat_index(GROUP)
    pairs = []
    for distance, slab in zip(distances, slabs):
        for n, array in enumerate(arrays):
            pairs.append((part(slab, n), head_of(array, here ^ distance(here))))
    run([pltpu.make_async_copy(*pair, sems.at[n]) for n, pair in enumerate(pairs)])


def near_cells(c):
    return (c, c ^ 1, c ^ 3)


def key_places(c):
    return [2 * n + a for n in near_cells(c) for a in range(2)]


def blocks_of(value):
    return [value[r : r + 128] for r in range(0, value.shape[0], 128)]


def seen_by(mask_ref, here, key, queries):
    flags = [jnp.full((1, 128), mask_ref[here ^ query, here ^ key]) for query in queries]
    return jnp.concatenate(flags, axis=1) > 0


def weights(scores, seen, top):
    return [
        jnp.exp2(block * EXPONENT - jnp.where(flag, top, 1e30)) for block, flag in zip(scores, seen)
    ]


def top_of(scores, seen):
    top = jnp.full((1, scores[0].shape[1]), -1e30, jnp.float32)
    for block, flag in zip(scores, seen):
        top = jnp.maximum(top, jnp.where(flag, jnp.max(block, axis=0, keepdims=True), -1e30))
    return top * EXPONENT


def sum_of(blocks):
    total = blocks[0]
    for block in blocks[1:]:
        total = total + block
    return jnp.sum(total, axis=0, keepdims=True)


def query_grad(keys, dscores):
    low = (t_times(keys, dscores) * (1.0 / math.sqrt(HEAD_DIM))).T.astype(jnp.bfloat16)
    return low.reshape(-1, 128, HEAD_DIM)


def early_kernel(distances, mask_ref, *refs):
    slabs, outs = refs[:-7], refs[-7:]
    stack_ref, exps_ref, dprobs_ref, stats_ref, seen_ref, done_ref, query_ref = outs
    here = flat_index(GROUP)
    for distance, slab in zip(distances, slabs):
        stack_ref[distance(here)] = slab[...]

    def take(places, n):
        columns = slice(n * HEAD_DIM, (n + 1) * HEAD_DIM)
        return jnp.concatenate([stack_ref[place, :, columns] for place in places], axis=0)

    cells = stack_ref.shape[0] // 2
    present = [[p for p in (2 * c, 2 * c + 1) if p != LATE] for c in range(cells)]
    for c in range(cells):
        q, g = take(present[c], 0), take(present[c], 3)
        width = q.shape[0]
        keys = [place for place in key_places(c) if place != LATE]
        scores = [b for n in near_cells(c) for b in blocks_of(times_t(take(present[n], 1), q))]
        dprobs = [b for n in near_cells(c) for b in blocks_of(times_t(take(present[n], 2), g))]
        seen = [seen_by(mask_ref, here, key, present[c]) for key in keys]
        top = top_of(scores, seen)
        exps = weights(scores, seen, top)
        total = sum_of(exps)
        product = sum_of([e * d for e, d in zip(exps, dprobs)])
        if c == DONE:
            inverse = 1.0 / total
            delta = product * inverse
            terms = []
            for n, (weight, term) in enumerate(zip(exps, dprobs)):
                probs = weight * inverse
                terms.append((probs * (term - delta)).astype(jnp.bfloat16))
                done_ref[0, 128 * n : 128 * (n + 1)] = probs.astype(jnp.bfloat16)
                done_ref[1, 128 * n : 128 * (n + 1)] = terms[n]
            query_ref[...] = query_grad(take(key_places(c), 1), jnp.concatenate(terms, axis=0))
            continue
        for key, weight, term in zip(keys, exps, dprobs):
            row = 128 * key_places(c).index(key)
            exps_ref[c, row : row + 128, :width] = weight
            dprobs_ref[c, row : row + 128, :width] = term
        stats_ref[c, 0:1, :width] = top
        stats_ref[c, 1:2, :width] = total
        stats_ref[c, 2:3, :width] = product
        for n, key in enumerate(key_places(c)):
            flags = seen_by(mask_ref, here, key, (2 * c, 2 * c + 1))
            seen_ref[c, n : n + 1] = flags.astype(jnp.float32)


def taker(slab, stack_ref):
    def take(places, n):
        columns = slice(n * HEAD_DIM, (n + 1) * HEAD_DIM)
        parts = [slab[:, columns] if p == LATE else stack_ref[p, :, columns] for p in places]
        return jnp.concatenate(parts, axis=0)

    return take


def put(out, n, value):
    out[:, n * HEAD_DIM : (n + 1) * HEAD_DIM] = value.astype(jnp.bfloat16)


def put_pair_grads(take, c, probs_low, dscores, outs):
    q, g = take(key_places(c), 0), take(key_places(c), 3)
    dk = jnp.dot(dscores, q, preferred_element_type=jnp.float32) * (1.0 / math.sqrt(HEAD_DIM))
    dv = jnp.dot(probs_low, g, preferred_element_type=jnp.float32)
    for a, out in enumerate(outs):
        put(out, 1, dk[128 * a : 128 * (a + 1)])
        put(out, 2, dv[128 * a : 128 * (a + 1)])


def late_kernel(slab, *refs):
    stack_ref, exps_ref, dprobs_ref, stats_ref, seen_ref, done_ref = refs[:6]
    outs = dict(zip(BEYOND, refs[6:10]))
    probs_out, dscores_out, query_out = refs[10:]
    cells = stack_ref.shape[0] // 2
    take = taker(slab, stack_ref)

    units = [(c, (2 * c, 2 * c + 1)) for c in range(cells) if c not in (DONE, LATE // 2)]
    units = [(LATE // 2, (place,)) for place in (LATE - 1, LATE)] + units
    fresh = [[p for p in key_places(c) if LATE in (p, *queries)] for c, queries in units]
    scores, dprobs, exps, inverse, delta, early_inverse = ([None] * len(units) for _ in range(6))
    for u, (c, queries) in enumerate(units):
        groups = [(LATE,)] if LATE not in queries else [(2 * n, 2 * n + 1) for n in near_cells(c)]
        groups = groups if fresh[u] else []
        mine_q, mine_g = take(queries, 0), take(queries, 3)
        scores[u] = [b for keys in groups for b in blocks_of(times_t(take(keys, 1), mine_q))]
        dprobs[u] = [b for keys in groups for b in blocks_of(times_t(take(keys, 2), mine_g))]
    seen = []
    for (c, queries), keys in zip(units, fresh):
        first = 128 * (queries[0] - 2 * c)
        columns = slice(first, first + 128 * len(queries))
        rows = [key_places(c).index(key) for key in keys]
        seen.append([seen_ref[c, n : n + 1, columns] > 0 for n in rows])
    tops = [top_of(blocks, flags) if blocks else None for blocks, flags in zip(scores, seen)]
    for u, (c, queries) in enumerate(units):
        early = LATE not in queries
        if early:
            top, total, product = (
                stats_ref[c, n : n + 1, : 128 * len(queries)] for n in range(3)
            )
        shrink = None
        if fresh[u]:
            new_top = jnp.maximum(top, tops[u]) if early else tops[u]
            exps[u] = weights(scores[u], seen[u], new_top)
            new_total = sum_of(exps[u])
            new_product = sum_of([e * d for e, d in zip(exps[u], dprobs[u])])
            if early:
                shrink = jnp.exp2(top - new_top)
                new_total = new_total + total * shrink
                new_product = new_product + product * shrink
            total, product = new_total, new_product
        inverse[u] = 1.0 / total
        delta[u] = product * inverse[u]
        early_inverse[u] = inverse[u] if shrink is None else inverse[u] * shrink

    def finished(u):
        c, queries = units[u]
        probs_low, dscores = [], []
        for n, key in enumerate(key_places(c)):
            if key in fresh[u]:
                index = fresh[u].index(key)
                probs, term = exps[u][index] * inverse[u], dprobs[u][index]
            else:
                place = (c, slice(128 * n, 128 * (n + 1)), slice(0, 128 * len(queries)))
                probs, term = exps_ref[place] * early_inverse[u], dprobs_ref[place]
            probs_low.append(probs.astype(jnp.bfloat16))
            dscores.append((probs * (term - delta[u])).astype(jnp.bfloat16))
        return probs_low, dscores

    probs_low = [{} for _ in range(cells)]
    dscores = [{} for _ in range(cells)]

    def rows_of(c):
        if c == DONE:
            pair = [blocks_of(done_ref[n]) for n in range(2)]
        elif LATE // 2 == c:
            sides = zip(finished(0), finished(1))
            pair = [
                [jnp.concatenate(both, axis=1) for both in zip(left, right)] for left, right in sides
            ]
        else:
            pair = finished(units.index((c, (2 * c, 2 * c + 1))))
        for t, n in enumerate(near_cells(c)):
            probs_low[n][c] = jnp.concatenate(pair[0][2 * t : 2 * t + 2], axis=0)
            dscores[n][c] = jnp.concatenate(pair[1][2 * t : 2 * t + 2], axis=0)

    def joined(blocks, c):
        return jnp.concatenate([blocks[n] for n in near_cells(c)], axis=1)

    rows_of(2)
    rows_of(1)
    rows_of(3)
    rows_of(0)
    for c in (2, 3):
        places = (2 * c, 2 * c + 1)
        put_pair_grads(take, c, joined(probs_low[c], c), joined(dscores[c], c), [outs[p] for p in places])
    for c in (2, 3, 1):
        terms = jnp.concatenate([dscores[n][c] for n in near_cells(c)], axis=0)
        dq = query_grad(take(key_places(c), 1), terms)
        if c == 1:
            query_out[...] = dq
        else:
            for a in range(2):
                put(outs[2 * c + a], 0, dq[a])
    for n in (0, 1):
        probs_out[n] = joined(probs_low[n], n)
        dscores_out[n] = joined(dscores[n], n)


def rest_kernel(distances, slab, stack_ref, probs_ref, dscores_ref, *refs):
    query_refs, kept, outs, out_ref = refs[:2], refs[2:4], refs[4:-1], refs[-1]
    here = flat_index(GROUP)
    fixed = [distance(here) for distance in distances]
    fixed = {place: out for place, out in zip(fixed, outs) if isinstance(place, int)}
    take = taker(slab, stack_ref)
    for c in (0, 1):
        targets = [fixed.get(place, out_ref.at[place]) for place in (2 * c, 2 * c + 1)]
        put_pair_grads(take, c, probs_ref[c], dscores_ref[c], targets)
        for a, target in enumerate(targets):
            put(target, 0, query_refs[c][a])
    for place, ref in zip((4, 6), kept):
        out_ref[place] = ref[...]
    for distance, out in zip(distances, outs):
        if not isinstance(distance(here), int):
            out[...] = out_ref[distance(here)]


SMEM = pl.BlockSpec(memory_space=pltpu.SMEM)
VMEM = pl.BlockSpec(memory_space=pltpu.VMEM)
ANY = pl.BlockSpec(memory_space=pl.ANY)


def slab_shape(tokens, parts):
    return jax.ShapeDtypeStruct((tokens, parts * HEAD_DIM), jnp.bfloat16)


def pack(arrays, distances, name, *extras):
    tokens = arrays[0].shape[0]
    count = len(distances)
    outs = [slab_shape(tokens, 4)] * count
    outs += [jax.ShapeDtypeStruct(extra.shape, extra.dtype) for extra in extras]
    return pl.pallas_call(
        functools.partial(pack_kernel, distances),
        out_shape=outs,
        in_specs=[ANY] * (4 + len(extras)),
        out_specs=[ANY] * len(outs),
        scratch_shapes=[pltpu.SemaphoreType.DMA((4 * count + len(extras),))],
        compiler_params=pltpu.CompilerParams(vmem_limit_bytes=MIB),
        name=name,
    )(*arrays, *extras)


def unpack(whole, distances, slabs, name, *arrays):
    count = len(distances)
    return pl.pallas_call(
        functools.partial(unpack_kernel, distances),
        out_shape=[whole] * 3,
        in_specs=[ANY] * (count + len(arrays)),
        out_specs=[ANY] * 3,
        scratch_shapes=[pltpu.SemaphoreType.DMA((3 * count,))],
        compiler_params=pltpu.CompilerParams(vmem_limit_bytes=MIB),
        input_output_aliases={count + n: n for n in range(len(arrays))},
        name=name,
    )(*slabs, *arrays)


def by_heads(queries, keys, values, out_grad, block_mask):
    devices = lax.axis_size(GROUP)
    cells = lax.axis_size("blk")
    tokens = queries.shape[0]
    *arrays, block_mask = [
        pltpu.with_memory_space_constraint(array, pltpu.HBM)
        for array in (queries, keys, values, out_grad, block_mask)
    ]
    sent = pack(arrays, INWARD[:FIRST], "pack_first")
    arrays, sent = lax.optimization_barrier((arrays, sent))
    *rest, own, block_mask = pack(arrays, INWARD[FIRST:] + (STAY,), "pack_rest", block_mask)
    got = list(sent) + rest
    for n, distance in enumerate(INWARD):
        if n in AFTER:
            got[n], got[AFTER[n]] = lax.optimization_barrier((got[n], got[AFTER[n]]))
        got[n] = exchange(got[n], distance)
    soon = [n for n, distance in enumerate(INWARD) if distance is not FAR]
    pairs = jax.ShapeDtypeStruct((cells, 6 * tokens, 2 * tokens), jnp.float32)
    partial = pl.pallas_call(
        functools.partial(early_kernel, [INWARD[n] for n in soon] + [STAY]),
        out_shape=[
            jax.ShapeDtypeStruct((devices, tokens, 4 * HEAD_DIM), jnp.bfloat16),
            pairs,
            pairs,
            jax.ShapeDtypeStruct((cells, 8, 2 * tokens), jnp.float32),
            jax.ShapeDtypeStruct((cells, 8, 2 * tokens), jnp.float32),
            jax.ShapeDtypeStruct((2, 6 * tokens, 2 * tokens), jnp.bfloat16),
            jax.ShapeDtypeStruct((2, tokens, HEAD_DIM), jnp.bfloat16),
        ],
        in_specs=[SMEM] + [VMEM] * (devices - 1),
        out_specs=[VMEM] * 7,
        compiler_params=pltpu.CompilerParams(vmem_limit_bytes=24 * MIB),
        name="early",
    )(block_mask, *[got[n] for n in soon], own)
    stack, *partial, query_grad_0 = partial
    slab = got[INWARD.index(FAR)]
    low = jax.ShapeDtypeStruct((2, 2 * tokens, 6 * tokens), jnp.bfloat16)
    *beyond, probs_low, dscores, query_grad_1 = pl.pallas_call(
        late_kernel,
        out_shape=[slab_shape(tokens, 3)] * len(BEYOND)
        + [low, low, jax.ShapeDtypeStruct((2, tokens, HEAD_DIM), jnp.bfloat16)],
        in_specs=[VMEM] * 7,
        out_specs=[VMEM] * (len(BEYOND) + 3),
        compiler_params=pltpu.CompilerParams(vmem_limit_bytes=24 * MIB),
        name="late",
    )(slab, stack, *partial)
    beyond = dict(zip(BEYOND, beyond))
    distances = OUTWARD + (STAY,)
    rest = pl.pallas_call(
        functools.partial(rest_kernel, distances[2:]),
        out_shape=[slab_shape(tokens, 3)] * (devices - 2),
        in_specs=[VMEM] * 8,
        out_specs=[VMEM] * (devices - 2),
        scratch_shapes=[pltpu.VMEM((devices, tokens, 3 * HEAD_DIM), jnp.bfloat16)],
        compiler_params=pltpu.CompilerParams(vmem_limit_bytes=24 * MIB),
        name="rest",
    )(slab, stack, probs_low, dscores, query_grad_0, query_grad_1, beyond[4], beyond[6])
    grads = [beyond[5], beyond[7], *rest]
    back = [exchange(grad, distance) for grad, distance in zip(grads, OUTWARD)] + [grads[-1]]
    whole = jax.ShapeDtypeStruct(queries.shape, queries.dtype)
    grads = unpack(whole, distances[-1:] + distances[:EARLY], back[-1:] + back[:EARLY], "unpack")
    return unpack(whole, distances[EARLY:-1], back[EARLY:-1], "unpack_last", *grads)


def local(queries, keys, values, out_grad, block_mask):
    heads = queries.shape[1] // HEAD_DIM
    cells, halves = lax.axis_size("blk"), lax.axis_size("uly")
    if (cells, halves) == (4, 2) and heads == cells * halves and queries.shape[0] == 128:
        return by_heads(queries, keys, values, out_grad, block_mask)
    return by_cells(queries, keys, values, out_grad, block_mask)


def solution(mesh):
    return jax.shard_map(
        local,
        mesh=mesh,
        in_specs=(
            P(("batch", "blk", "uly"), None),
            P(("batch", "blk", "uly"), None),
            P(("batch", "blk", "uly"), None),
            P(("batch", "blk", "uly"), None),
            P("batch", None),
        ),
        out_specs=(
            P(("batch", "blk", "uly"), None),
            P(("batch", "blk", "uly"), None),
            P(("batch", "blk", "uly"), None),
        ),
        check_vma=False,
    )
```

```python
import functools
import math

import jax
import jax.numpy as jnp
from jax import lax
from jax.experimental import pallas as pl
from jax.experimental.pallas import tpu as pltpu
from jax.sharding import PartitionSpec as P

HEAD_DIM = 128
MIB = 1024 * 1024
GROUP = ("blk", "uly")


def padded(block, sides, width):
    for axis, dim in sides:
        count = lax.axis_size(axis)
        forward = [(i, i + 1) for i in range(count - 1)]
        forward.append((count - 1, 0))
        backward = [(target, source) for source, target in forward]
        low = lax.ppermute(
            lax.slice_in_dim(block, block.shape[dim] - width, None, axis=dim), axis, forward
        )
        high = lax.ppermute(lax.slice_in_dim(block, 0, width, axis=dim), axis, backward)
        block = jnp.concatenate([low, block, high], axis=dim)
    return block


def passed_along(block, axis, distance):
    devices = range(lax.axis_size(axis))
    route = [((i - distance) % len(devices), i) for i in devices]
    return lax.ppermute(block, axis, route)


def times_t(left, right):
    return lax.dot_general(
        left, right, (((1,), (1,)), ((), ())), preferred_element_type=jnp.float32
    )


def t_times(left, right):
    return lax.dot_general(
        left, right, (((0,), (0,)), ((), ())), preferred_element_type=jnp.float32
    )


def widen_blocks(mask_blocks):
    return jnp.repeat(jnp.repeat(mask_blocks > 0, 128, axis=0), 128, axis=1)


def by_cells(queries, keys, values, out_grad, block_mask):
    local_q, local_k, local_v, local_g = (
        lax.all_to_all(queries, "uly", split_axis=1, concat_axis=0, tiled=True),
        lax.all_to_all(keys, "uly", split_axis=1, concat_axis=0, tiled=True),
        lax.all_to_all(values, "uly", split_axis=1, concat_axis=0, tiled=True),
        lax.all_to_all(out_grad, "uly", split_axis=1, concat_axis=0, tiled=True),
    )
    genes = local_q.shape[0]
    heads_here = local_q.shape[1] // HEAD_DIM
    scale = 1.0 / math.sqrt(HEAD_DIM)
    cells = lax.axis_size("blk")
    here = lax.axis_index("blk")
    per_cell = genes // 128
    near = (here + jnp.array([-1, 0, 1], dtype=jnp.int32) + cells) % cells
    mask_rows = lax.dynamic_slice_in_dim(block_mask, here * per_cell, per_cell, 0).reshape(
        per_cell, cells, per_cell
    )
    row_mask = widen_blocks(jnp.take(mask_rows, near, axis=1).reshape(per_cell, 3 * per_cell))
    pairs = jnp.stack([local_k, local_v], axis=1)
    band = padded(pairs, (("blk", 0),), genes)
    q_grads = []
    k_parts = []
    v_parts = []
    for head in range(heads_here):
        lower = head * HEAD_DIM
        upper = lower + HEAD_DIM
        q_head = local_q[:, lower:upper]
        g_head = local_g[:, lower:upper]
        k_band = band[:, 0, lower:upper]
        v_band = band[:, 1, lower:upper]
        scores = jnp.where(row_mask, times_t(q_head, k_band) * scale, -1e30)
        top = jnp.max(scores, axis=1, keepdims=True)
        total = jnp.sum(jnp.where(row_mask, jnp.exp(scores - top), 0.0), axis=1, keepdims=True)
        lse = top + jnp.log(total)
        probs = jnp.where(row_mask, jnp.exp(scores - lse), 0.0)
        dprobs = times_t(g_head, v_band)
        delta = jnp.sum(probs * dprobs, axis=1, keepdims=True)
        dscores = (probs * (dprobs - delta)).astype(jnp.bfloat16)
        q_grads.append(
            (jnp.dot(dscores, k_band, preferred_element_type=jnp.float32) * scale).astype(
                jnp.bfloat16
            )
        )
        k_parts.append(t_times(dscores, q_head))
        v_parts.append(t_times(probs.astype(jnp.bfloat16), g_head))
    query_grad = jnp.concatenate(q_grads, axis=1)
    partial_terms = jnp.stack(
        [jnp.concatenate(k_parts, axis=1), jnp.concatenate(v_parts, axis=1)], axis=1
    )
    from_next = passed_along(partial_terms[:genes].astype(jnp.bfloat16), "blk", -1).astype(
        jnp.float32
    )
    from_prior = passed_along(partial_terms[2 * genes :].astype(jnp.bfloat16), "blk", 1).astype(
        jnp.float32
    )
    summed = partial_terms[genes : 2 * genes] + from_next + from_prior
    key_grad = (summed[:, 0] * scale).astype(jnp.bfloat16)
    value_grad = summed[:, 1].astype(jnp.bfloat16)
    return (
        lax.all_to_all(query_grad, "uly", split_axis=0, concat_axis=1, tiled=True),
        lax.all_to_all(key_grad, "uly", split_axis=0, concat_axis=1, tiled=True),
        lax.all_to_all(value_grad, "uly", split_axis=0, concat_axis=1, tiled=True),
    )


def flat_index(axes):
    index = 0
    for axis in axes:
        index = index * lax.axis_size(axis) + lax.axis_index(axis)
    return index


def same_core(here):
    return (here >> 1) & 1


def even_places(here):
    return (here ^ (here >> 1) ^ (here >> 2)) & 1


def hop(first, second=None, chooser=same_core):
    if second is None:
        return lambda here: first
    return lambda here: first + (second - first) * chooser(here)


STAY = hop(0)
CORE = hop(2)
FAR = hop(5)
FAR_CORE = hop(7)
SIDE = hop(4, 1)
OTHER_SIDE = hop(1, 4)
SIDE_CORE = hop(6, 3, even_places)
OTHER_SIDE_CORE = hop(3, 6, even_places)

INWARD = (FAR, SIDE_CORE, CORE, SIDE, OTHER_SIDE, OTHER_SIDE_CORE, FAR_CORE)
OUTWARD = (FAR, FAR_CORE, SIDE, OTHER_SIDE, SIDE_CORE, OTHER_SIDE_CORE, CORE)
FIRST = 2
EARLY = 2
LATE_HOP = FAR_CORE
LATE = 7
BEYOND = (4, 5, 6, 7)
DONE = 1
AFTER = {}
EXPONENT = math.log2(math.e) / math.sqrt(HEAD_DIM)


def exchange(block, distance):
    places = range(lax.axis_size(GROUP))
    return lax.ppermute(block, GROUP, [(i, i ^ distance(i)) for i in places])


def part(ref, n):
    return ref.at[:, n * HEAD_DIM : (n + 1) * HEAD_DIM]


def head_of(ref, head):
    return ref.at[:, pl.ds(pl.multiple_of(head * HEAD_DIM, HEAD_DIM), HEAD_DIM)]


def run(copies):
    for copy in copies:
        copy.start()
    for copy in copies:
        copy.wait()


def pack_kernel(distances, *refs):
    count = len(distances)
    extras = (len(refs) - 1 - count - 4) // 2
    sources, outs, sems = refs[: 4 + extras], refs[4 + extras : -1], refs[-1]
    here = flat_index(GROUP)
    pairs = list(zip(sources[4:], outs[count:]))
    for distance, slab in zip(distances, outs):
        for n, array in enumerate(sources[:4]):
            pairs.append((head_of(array, here ^ distance(here)), part(slab, n)))
    run([pltpu.make_async_copy(*pair, sems.at[n]) for n, pair in enumerate(pairs)])


def unpack_kernel(distances, *refs):
    slabs, arrays, sems = refs[: len(distances)], refs[-4:-1], refs[-1]
    here = flat_index(GROUP)
    pairs = []
    for distance, slab in zip(distances, slabs):
        for n, array in enumerate(arrays):
            pairs.append((part(slab, n), head_of(array, here ^ distance(here))))
    run([pltpu.make_async_copy(*pair, sems.at[n]) for n, pair in enumerate(pairs)])


def near_cells(c):
    return (c, c ^ 1, c ^ 3)


def key_places(c):
    return [2 * n + a for n in near_cells(c) for a in range(2)]


def blocks_of(value):
    return [value[r : r + 128] for r in range(0, value.shape[0], 128)]


def seen_by(mask_ref, here, key, queries):
    flags = [jnp.full((1, 128), mask_ref[here ^ query, here ^ key]) for query in queries]
    return jnp.concatenate(flags, axis=1) > 0


def weights(scores, seen, top):
    return [
        jnp.exp2(block * EXPONENT - jnp.where(flag, top, 1e30)) for block, flag in zip(scores, seen)
    ]


def top_of(scores, seen):
    top = jnp.full((1, scores[0].shape[1]), -1e30, jnp.float32)
    for block, flag in zip(scores, seen):
        top = jnp.maximum(top, jnp.where(flag, jnp.max(block, axis=0, keepdims=True), -1e30))
    return top * EXPONENT


def sum_of(blocks):
    total = blocks[0]
    for block in blocks[1:]:
        total = total + block
    return jnp.sum(total, axis=0, keepdims=True)


def query_grad(keys, dscores):
    low = (t_times(keys, dscores) * (1.0 / math.sqrt(HEAD_DIM))).T.astype(jnp.bfloat16)
    return low.reshape(-1, 128, HEAD_DIM)


def seen_kernel(mask_ref, seen_ref):
    here = flat_index(GROUP)
    for c in range(seen_ref.shape[0]):
        for n, key in enumerate(key_places(c)):
            flags = seen_by(mask_ref, here, key, (2 * c, 2 * c + 1))
            seen_ref[c, n : n + 1] = flags.astype(jnp.float32)


def early_kernel(distances, seen_ref, *refs):
    slabs, outs = refs[:-6], refs[-6:]
    stack_ref, exps_ref, dprobs_ref, stats_ref, done_ref, query_ref = outs
    here = flat_index(GROUP)
    for distance, slab in zip(distances, slabs):
        stack_ref[distance(here)] = slab[...]

    def take(places, n):
        columns = slice(n * HEAD_DIM, (n + 1) * HEAD_DIM)
        return jnp.concatenate([stack_ref[place, :, columns] for place in places], axis=0)

    cells = stack_ref.shape[0] // 2
    present = [[p for p in (2 * c, 2 * c + 1) if p != LATE] for c in range(cells)]
    for c in range(cells):
        q, g = take(present[c], 0), take(present[c], 3)
        width = q.shape[0]
        keys = [place for place in key_places(c) if place != LATE]
        scores = [b for n in near_cells(c) for b in blocks_of(times_t(take(present[n], 1), q))]
        dprobs = [b for n in near_cells(c) for b in blocks_of(times_t(take(present[n], 2), g))]
        rows = [key_places(c).index(key) for key in keys]
        seen = [seen_ref[c, n : n + 1, :width] > 0 for n in rows]
        top = top_of(scores, seen)
        exps = weights(scores, seen, top)
        total = sum_of(exps)
        product = sum_of([e * d for e, d in zip(exps, dprobs)])
        if c == DONE:
            inverse = 1.0 / total
            delta = product * inverse
            terms = []
            for n, (weight, term) in enumerate(zip(exps, dprobs)):
                probs = weight * inverse
                terms.append((probs * (term - delta)).astype(jnp.bfloat16))
                done_ref[0, 128 * n : 128 * (n + 1)] = probs.astype(jnp.bfloat16)
                done_ref[1, 128 * n : 128 * (n + 1)] = terms[n]
            query_ref[...] = query_grad(take(key_places(c), 1), jnp.concatenate(terms, axis=0))
            continue
        for key, weight, term in zip(keys, exps, dprobs):
            row = 128 * key_places(c).index(key)
            exps_ref[c, row : row + 128, :width] = weight
            dprobs_ref[c, row : row + 128, :width] = term
        stats_ref[c, 0:1, :width] = top
        stats_ref[c, 1:2, :width] = total
        stats_ref[c, 2:3, :width] = product


def taker(slab, stack_ref):
    def take(places, n):
        columns = slice(n * HEAD_DIM, (n + 1) * HEAD_DIM)
        parts = [slab[:, columns] if p == LATE else stack_ref[p, :, columns] for p in places]
        return jnp.concatenate(parts, axis=0)

    return take


def put(out, n, value):
    out[:, n * HEAD_DIM : (n + 1) * HEAD_DIM] = value.astype(jnp.bfloat16)


def put_pair_grads(take, c, probs_low, dscores, outs):
    q, g = take(key_places(c), 0), take(key_places(c), 3)
    dk = jnp.dot(dscores, q, preferred_element_type=jnp.float32) * (1.0 / math.sqrt(HEAD_DIM))
    dv = jnp.dot(probs_low, g, preferred_element_type=jnp.float32)
    for a, out in enumerate(outs):
        put(out, 1, dk[128 * a : 128 * (a + 1)])
        put(out, 2, dv[128 * a : 128 * (a + 1)])


def late_kernel(slab, *refs):
    seen_ref, stack_ref, exps_ref, dprobs_ref, stats_ref, done_ref = refs[:6]
    outs = dict(zip(BEYOND, refs[6:10]))
    probs_out, dscores_out, query_out = refs[10:]
    cells = stack_ref.shape[0] // 2
    take = taker(slab, stack_ref)

    units = [(c, (2 * c, 2 * c + 1)) for c in range(cells) if c not in (DONE, LATE // 2)]
    units = [(LATE // 2, (place,)) for place in (LATE - 1, LATE)] + units
    fresh = [[p for p in key_places(c) if LATE in (p, *queries)] for c, queries in units]
    scores, dprobs, exps, inverse, delta, early_inverse = ([None] * len(units) for _ in range(6))
    for u, (c, queries) in enumerate(units):
        groups = [(LATE,)] if LATE not in queries else [(2 * n, 2 * n + 1) for n in near_cells(c)]
        groups = groups if fresh[u] else []
        mine_q, mine_g = take(queries, 0), take(queries, 3)
        scores[u] = [b for keys in groups for b in blocks_of(times_t(take(keys, 1), mine_q))]
        dprobs[u] = [b for keys in groups for b in blocks_of(times_t(take(keys, 2), mine_g))]
    seen = []
    for (c, queries), keys in zip(units, fresh):
        first = 128 * (queries[0] - 2 * c)
        columns = slice(first, first + 128 * len(queries))
        rows = [key_places(c).index(key) for key in keys]
        seen.append([seen_ref[c, n : n + 1, columns] > 0 for n in rows])
    tops = [top_of(blocks, flags) if blocks else None for blocks, flags in zip(scores, seen)]
    for u, (c, queries) in enumerate(units):
        early = LATE not in queries
        if early:
            top, total, product = (
                stats_ref[c, n : n + 1, : 128 * len(queries)] for n in range(3)
            )
        shrink = None
        if fresh[u]:
            new_top = jnp.maximum(top, tops[u]) if early else tops[u]
            exps[u] = weights(scores[u], seen[u], new_top)
            new_total = sum_of(exps[u])
            new_product = sum_of([e * d for e, d in zip(exps[u], dprobs[u])])
            if early:
                shrink = jnp.exp2(top - new_top)
                new_total = new_total + total * shrink
                new_product = new_product + product * shrink
            total, product = new_total, new_product
        inverse[u] = 1.0 / total
        delta[u] = product * inverse[u]
        early_inverse[u] = inverse[u] if shrink is None else inverse[u] * shrink

    def finished(u):
        c, queries = units[u]
        probs_low, dscores = [], []
        for n, key in enumerate(key_places(c)):
            if key in fresh[u]:
                index = fresh[u].index(key)
                probs, term = exps[u][index] * inverse[u], dprobs[u][index]
            else:
                place = (c, slice(128 * n, 128 * (n + 1)), slice(0, 128 * len(queries)))
                probs, term = exps_ref[place] * early_inverse[u], dprobs_ref[place]
            probs_low.append(probs.astype(jnp.bfloat16))
            dscores.append((probs * (term - delta[u])).astype(jnp.bfloat16))
        return probs_low, dscores

    probs_low = [{} for _ in range(cells)]
    dscores = [{} for _ in range(cells)]

    def rows_of(c):
        if c == DONE:
            pair = [blocks_of(done_ref[n]) for n in range(2)]
        elif LATE // 2 == c:
            sides = zip(finished(0), finished(1))
            pair = [
                [jnp.concatenate(both, axis=1) for both in zip(left, right)] for left, right in sides
            ]
        else:
            pair = finished(units.index((c, (2 * c, 2 * c + 1))))
        for t, n in enumerate(near_cells(c)):
            probs_low[n][c] = jnp.concatenate(pair[0][2 * t : 2 * t + 2], axis=0)
            dscores[n][c] = jnp.concatenate(pair[1][2 * t : 2 * t + 2], axis=0)

    def joined(blocks, c):
        return jnp.concatenate([blocks[n] for n in near_cells(c)], axis=1)

    for c in (LATE // 2, 1 - DONE, LATE // 2 ^ 1, DONE):
        rows_of(c)
    for c in (2, 3):
        places = (2 * c, 2 * c + 1)
        put_pair_grads(take, c, joined(probs_low[c], c), joined(dscores[c], c), [outs[p] for p in places])
    for c in (2, 3, 1 - DONE):
        terms = jnp.concatenate([dscores[n][c] for n in near_cells(c)], axis=0)
        dq = query_grad(take(key_places(c), 1), terms)
        if c == 1 - DONE:
            query_out[...] = dq
        else:
            for a in range(2):
                put(outs[2 * c + a], 0, dq[a])
    for n in (0, 1):
        probs_out[n] = joined(probs_low[n], n)
        dscores_out[n] = joined(dscores[n], n)


def rest_kernel(distances, slab, stack_ref, probs_ref, dscores_ref, *refs):
    query_refs, kept, outs, out_ref = refs[:2], refs[2:4], refs[4:-1], refs[-1]
    here = flat_index(GROUP)
    fixed = [distance(here) for distance in distances]
    fixed = {place: out for place, out in zip(fixed, outs) if isinstance(place, int)}
    take = taker(slab, stack_ref)
    for c in (0, 1):
        targets = [fixed.get(place, out_ref.at[place]) for place in (2 * c, 2 * c + 1)]
        put_pair_grads(take, c, probs_ref[c], dscores_ref[c], targets)
        for a, target in enumerate(targets):
            put(target, 0, query_refs[c][a])
    for place, ref in zip((4, 6), kept):
        out_ref[place] = ref[...]
    for distance, out in zip(distances, outs):
        if not isinstance(distance(here), int):
            out[...] = out_ref[distance(here)]


SMEM = pl.BlockSpec(memory_space=pltpu.SMEM)
VMEM = pl.BlockSpec(memory_space=pltpu.VMEM)
ANY = pl.BlockSpec(memory_space=pl.ANY)


def slab_shape(tokens, parts):
    return jax.ShapeDtypeStruct((tokens, parts * HEAD_DIM), jnp.bfloat16)


def pack(arrays, distances, name, *extras):
    tokens = arrays[0].shape[0]
    count = len(distances)
    outs = [slab_shape(tokens, 4)] * count
    outs += [jax.ShapeDtypeStruct(extra.shape, extra.dtype) for extra in extras]
    return pl.pallas_call(
        functools.partial(pack_kernel, distances),
        out_shape=outs,
        in_specs=[ANY] * (4 + len(extras)),
        out_specs=[ANY] * len(outs),
        scratch_shapes=[pltpu.SemaphoreType.DMA((4 * count + len(extras),))],
        compiler_params=pltpu.CompilerParams(vmem_limit_bytes=MIB),
        name=name,
    )(*arrays, *extras)


def unpack(whole, distances, slabs, name, *arrays):
    count = len(distances)
    return pl.pallas_call(
        functools.partial(unpack_kernel, distances),
        out_shape=[whole] * 3,
        in_specs=[ANY] * (count + len(arrays)),
        out_specs=[ANY] * 3,
        scratch_shapes=[pltpu.SemaphoreType.DMA((3 * count,))],
        compiler_params=pltpu.CompilerParams(vmem_limit_bytes=MIB),
        input_output_aliases={count + n: n for n in range(len(arrays))},
        name=name,
    )(*slabs, *arrays)


def by_heads(queries, keys, values, out_grad, block_mask):
    devices = lax.axis_size(GROUP)
    cells = lax.axis_size("blk")
    tokens = queries.shape[0]
    *arrays, block_mask = [
        pltpu.with_memory_space_constraint(array, pltpu.HBM)
        for array in (queries, keys, values, out_grad, block_mask)
    ]
    sent = pack(arrays, INWARD[:FIRST], "pack_first")
    arrays, sent = lax.optimization_barrier((arrays, sent))
    *rest, own, block_mask = pack(arrays, INWARD[FIRST:] + (STAY,), "pack_rest", block_mask)
    got = list(sent) + rest
    for n, distance in enumerate(INWARD):
        if n in AFTER:
            got[n], got[AFTER[n]] = lax.optimization_barrier((got[n], got[AFTER[n]]))
        got[n] = exchange(got[n], distance)
    soon = [n for n, distance in enumerate(INWARD) if distance is not LATE_HOP]
    seen = pl.pallas_call(
        seen_kernel,
        out_shape=jax.ShapeDtypeStruct((cells, 8, 2 * tokens), jnp.float32),
        in_specs=[SMEM],
        out_specs=VMEM,
        compiler_params=pltpu.CompilerParams(vmem_limit_bytes=MIB),
        name="seen",
    )(block_mask)
    pairs = jax.ShapeDtypeStruct((cells, 6 * tokens, 2 * tokens), jnp.float32)
    partial = pl.pallas_call(
        functools.partial(early_kernel, [INWARD[n] for n in soon] + [STAY]),
        out_shape=[
            jax.ShapeDtypeStruct((devices, tokens, 4 * HEAD_DIM), jnp.bfloat16),
            pairs,
            pairs,
            jax.ShapeDtypeStruct((cells, 8, 2 * tokens), jnp.float32),
            jax.ShapeDtypeStruct((2, 6 * tokens, 2 * tokens), jnp.bfloat16),
            jax.ShapeDtypeStruct((2, tokens, HEAD_DIM), jnp.bfloat16),
        ],
        in_specs=[VMEM] * devices,
        out_specs=[VMEM] * 6,
        compiler_params=pltpu.CompilerParams(vmem_limit_bytes=24 * MIB),
        name="early",
    )(seen, *[got[n] for n in soon], own)
    stack, *partial, query_grad_done = partial
    slab = got[INWARD.index(LATE_HOP)]
    low = jax.ShapeDtypeStruct((2, 2 * tokens, 6 * tokens), jnp.bfloat16)
    *beyond, probs_low, dscores, query_grad_other = pl.pallas_call(
        late_kernel,
        out_shape=[slab_shape(tokens, 3)] * len(BEYOND)
        + [low, low, jax.ShapeDtypeStruct((2, tokens, HEAD_DIM), jnp.bfloat16)],
        in_specs=[VMEM] * 7,
        out_specs=[VMEM] * (len(BEYOND) + 3),
        compiler_params=pltpu.CompilerParams(vmem_limit_bytes=24 * MIB),
        name="late",
    )(slab, seen, stack, *partial)
    beyond = dict(zip(BEYOND, beyond))
    query_grads = (query_grad_done, query_grad_other)
    query_grads = query_grads[::-1] if DONE == 1 else query_grads
    distances = OUTWARD + (STAY,)
    rest = pl.pallas_call(
        functools.partial(rest_kernel, distances[2:]),
        out_shape=[slab_shape(tokens, 3)] * (devices - 2),
        in_specs=[VMEM] * 8,
        out_specs=[VMEM] * (devices - 2),
        scratch_shapes=[pltpu.VMEM((devices, tokens, 3 * HEAD_DIM), jnp.bfloat16)],
        compiler_params=pltpu.CompilerParams(vmem_limit_bytes=24 * MIB),
        name="rest",
    )(slab, stack, probs_low, dscores, *query_grads, beyond[4], beyond[6])
    grads = [beyond[5], beyond[7], *rest]
    back = [exchange(grad, distance) for grad, distance in zip(grads, OUTWARD)] + [grads[-1]]
    whole = jax.ShapeDtypeStruct(queries.shape, queries.dtype)
    grads = unpack(whole, distances[-1:] + distances[:EARLY], back[-1:] + back[:EARLY], "unpack")
    return unpack(whole, distances[EARLY:-1], back[EARLY:-1], "unpack_last", *grads)


def local(queries, keys, values, out_grad, block_mask):
    heads = queries.shape[1] // HEAD_DIM
    cells, halves = lax.axis_size("blk"), lax.axis_size("uly")
    if (cells, halves) == (4, 2) and heads == cells * halves and queries.shape[0] == 128:
        return by_heads(queries, keys, values, out_grad, block_mask)
    return by_cells(queries, keys, values, out_grad, block_mask)


def solution(mesh):
    return jax.shard_map(
        local,
        mesh=mesh,
        in_specs=(
            P(("batch", "blk", "uly"), None),
            P(("batch", "blk", "uly"), None),
            P(("batch", "blk", "uly"), None),
            P(("batch", "blk", "uly"), None),
            P("batch", None),
        ),
        out_specs=(
            P(("batch", "blk", "uly"), None),
            P(("batch", "blk", "uly"), None),
            P(("batch", "blk", "uly"), None),
        ),
        check_vma=False,
    )
```

```python
import functools
import math

import jax
import jax.numpy as jnp
from jax import lax
from jax.experimental import pallas as pl
from jax.experimental.pallas import tpu as pltpu
from jax.sharding import PartitionSpec as P

HEAD_DIM = 128
MIB = 1024 * 1024
GROUP = ("blk", "uly")


def padded(block, sides, width):
    for axis, dim in sides:
        count = lax.axis_size(axis)
        forward = [(i, i + 1) for i in range(count - 1)]
        forward.append((count - 1, 0))
        backward = [(target, source) for source, target in forward]
        low = lax.ppermute(
            lax.slice_in_dim(block, block.shape[dim] - width, None, axis=dim), axis, forward
        )
        high = lax.ppermute(lax.slice_in_dim(block, 0, width, axis=dim), axis, backward)
        block = jnp.concatenate([low, block, high], axis=dim)
    return block


def passed_along(block, axis, distance):
    devices = range(lax.axis_size(axis))
    route = [((i - distance) % len(devices), i) for i in devices]
    return lax.ppermute(block, axis, route)


def times_t(left, right):
    return lax.dot_general(
        left, right, (((1,), (1,)), ((), ())), preferred_element_type=jnp.float32
    )


def t_times(left, right):
    return lax.dot_general(
        left, right, (((0,), (0,)), ((), ())), preferred_element_type=jnp.float32
    )


def widen_blocks(mask_blocks):
    return jnp.repeat(jnp.repeat(mask_blocks > 0, 128, axis=0), 128, axis=1)


def by_cells(queries, keys, values, out_grad, block_mask):
    local_q, local_k, local_v, local_g = (
        lax.all_to_all(queries, "uly", split_axis=1, concat_axis=0, tiled=True),
        lax.all_to_all(keys, "uly", split_axis=1, concat_axis=0, tiled=True),
        lax.all_to_all(values, "uly", split_axis=1, concat_axis=0, tiled=True),
        lax.all_to_all(out_grad, "uly", split_axis=1, concat_axis=0, tiled=True),
    )
    genes = local_q.shape[0]
    heads_here = local_q.shape[1] // HEAD_DIM
    scale = 1.0 / math.sqrt(HEAD_DIM)
    cells = lax.axis_size("blk")
    here = lax.axis_index("blk")
    per_cell = genes // 128
    near = (here + jnp.array([-1, 0, 1], dtype=jnp.int32) + cells) % cells
    mask_rows = lax.dynamic_slice_in_dim(block_mask, here * per_cell, per_cell, 0).reshape(
        per_cell, cells, per_cell
    )
    row_mask = widen_blocks(jnp.take(mask_rows, near, axis=1).reshape(per_cell, 3 * per_cell))
    pairs = jnp.stack([local_k, local_v], axis=1)
    band = padded(pairs, (("blk", 0),), genes)
    q_grads = []
    k_parts = []
    v_parts = []
    for head in range(heads_here):
        lower = head * HEAD_DIM
        upper = lower + HEAD_DIM
        q_head = local_q[:, lower:upper]
        g_head = local_g[:, lower:upper]
        k_band = band[:, 0, lower:upper]
        v_band = band[:, 1, lower:upper]
        scores = jnp.where(row_mask, times_t(q_head, k_band) * scale, -1e30)
        top = jnp.max(scores, axis=1, keepdims=True)
        total = jnp.sum(jnp.where(row_mask, jnp.exp(scores - top), 0.0), axis=1, keepdims=True)
        lse = top + jnp.log(total)
        probs = jnp.where(row_mask, jnp.exp(scores - lse), 0.0)
        dprobs = times_t(g_head, v_band)
        delta = jnp.sum(probs * dprobs, axis=1, keepdims=True)
        dscores = (probs * (dprobs - delta)).astype(jnp.bfloat16)
        q_grads.append(
            (jnp.dot(dscores, k_band, preferred_element_type=jnp.float32) * scale).astype(
                jnp.bfloat16
            )
        )
        k_parts.append(t_times(dscores, q_head))
        v_parts.append(t_times(probs.astype(jnp.bfloat16), g_head))
    query_grad = jnp.concatenate(q_grads, axis=1)
    partial_terms = jnp.stack(
        [jnp.concatenate(k_parts, axis=1), jnp.concatenate(v_parts, axis=1)], axis=1
    )
    from_next = passed_along(partial_terms[:genes].astype(jnp.bfloat16), "blk", -1).astype(
        jnp.float32
    )
    from_prior = passed_along(partial_terms[2 * genes :].astype(jnp.bfloat16), "blk", 1).astype(
        jnp.float32
    )
    summed = partial_terms[genes : 2 * genes] + from_next + from_prior
    key_grad = (summed[:, 0] * scale).astype(jnp.bfloat16)
    value_grad = summed[:, 1].astype(jnp.bfloat16)
    return (
        lax.all_to_all(query_grad, "uly", split_axis=0, concat_axis=1, tiled=True),
        lax.all_to_all(key_grad, "uly", split_axis=0, concat_axis=1, tiled=True),
        lax.all_to_all(value_grad, "uly", split_axis=0, concat_axis=1, tiled=True),
    )


def flat_index(axes):
    index = 0
    for axis in axes:
        index = index * lax.axis_size(axis) + lax.axis_index(axis)
    return index


def same_core(here):
    return (here >> 1) & 1


def even_places(here):
    return (here ^ (here >> 1) ^ (here >> 2)) & 1


def hop(first, second=None, chooser=same_core):
    if second is None:
        return lambda here: first
    return lambda here: first + (second - first) * chooser(here)


STAY = hop(0)
CORE = hop(2)
FAR = hop(5)
FAR_CORE = hop(7)
SIDE = hop(4, 1)
OTHER_SIDE = hop(1, 4)
SIDE_CORE = hop(6, 3, even_places)
OTHER_SIDE_CORE = hop(3, 6, even_places)

INWARD = (FAR, SIDE_CORE, CORE, SIDE, OTHER_SIDE, OTHER_SIDE_CORE, FAR_CORE)
OUTWARD = (FAR, FAR_CORE, SIDE, OTHER_SIDE, SIDE_CORE, OTHER_SIDE_CORE, CORE)
FIRST = 2
UNPACKED = ((-1, 0, 1), (2, 3), (4, 5, 6))
LATE_HOP = FAR_CORE
LATE = 7
BEYOND = (4, 5, 6, 7)
DONE = 1
AFTER = {}
EXPONENT = math.log2(math.e) / math.sqrt(HEAD_DIM)


def exchange(block, distance):
    places = range(lax.axis_size(GROUP))
    return lax.ppermute(block, GROUP, [(i, i ^ distance(i)) for i in places])


def part(ref, n):
    return ref.at[:, n * HEAD_DIM : (n + 1) * HEAD_DIM]


def head_of(ref, head):
    return ref.at[:, pl.ds(pl.multiple_of(head * HEAD_DIM, HEAD_DIM), HEAD_DIM)]


def run(copies):
    for copy in copies:
        copy.start()
    for copy in copies:
        copy.wait()


def pack_kernel(distances, *refs):
    count = len(distances)
    extras = (len(refs) - 1 - count - 4) // 2
    sources, outs, sems = refs[: 4 + extras], refs[4 + extras : -1], refs[-1]
    here = flat_index(GROUP)
    pairs = list(zip(sources[4:], outs[count:]))
    for distance, slab in zip(distances, outs):
        for n, array in enumerate(sources[:4]):
            pairs.append((head_of(array, here ^ distance(here)), part(slab, n)))
    run([pltpu.make_async_copy(*pair, sems.at[n]) for n, pair in enumerate(pairs)])


def unpack_kernel(distances, *refs):
    slabs, arrays, sems = refs[: len(distances)], refs[-4:-1], refs[-1]
    here = flat_index(GROUP)
    pairs = []
    for distance, slab in zip(distances, slabs):
        for n, array in enumerate(arrays):
            pairs.append((part(slab, n), head_of(array, here ^ distance(here))))
    run([pltpu.make_async_copy(*pair, sems.at[n]) for n, pair in enumerate(pairs)])


def near_cells(c):
    return (c, c ^ 1, c ^ 3)


def key_places(c):
    return [2 * n + a for n in near_cells(c) for a in range(2)]


def blocks_of(value):
    return [value[r : r + 128] for r in range(0, value.shape[0], 128)]


def seen_by(mask_ref, here, key, queries):
    flags = [jnp.full((1, 128), mask_ref[here ^ query, here ^ key]) for query in queries]
    return jnp.concatenate(flags, axis=1) > 0


def weights(scores, seen, top):
    return [
        jnp.exp2(block * EXPONENT - jnp.where(flag, top, 1e30)) for block, flag in zip(scores, seen)
    ]


def top_of(scores, seen):
    top = jnp.full((1, scores[0].shape[1]), -1e30, jnp.float32)
    for block, flag in zip(scores, seen):
        top = jnp.maximum(top, jnp.where(flag, jnp.max(block, axis=0, keepdims=True), -1e30))
    return top * EXPONENT


def sum_of(blocks):
    total = blocks[0]
    for block in blocks[1:]:
        total = total + block
    return jnp.sum(total, axis=0, keepdims=True)


def query_grad(keys, dscores):
    low = (t_times(keys, dscores) * (1.0 / math.sqrt(HEAD_DIM))).T.astype(jnp.bfloat16)
    return low.reshape(-1, 128, HEAD_DIM)


def seen_kernel(mask_ref, seen_ref):
    here = flat_index(GROUP)
    for c in range(seen_ref.shape[0]):
        for n, key in enumerate(key_places(c)):
            flags = seen_by(mask_ref, here, key, (2 * c, 2 * c + 1))
            seen_ref[c, n : n + 1] = flags.astype(jnp.float32)


def early_kernel(distances, seen_ref, *refs):
    slabs, outs = refs[:-6], refs[-6:]
    stack_ref, exps_ref, dprobs_ref, stats_ref, done_ref, query_ref = outs
    here = flat_index(GROUP)
    for distance, slab in zip(distances, slabs):
        stack_ref[distance(here)] = slab[...]

    def take(places, n):
        columns = slice(n * HEAD_DIM, (n + 1) * HEAD_DIM)
        return jnp.concatenate([stack_ref[place, :, columns] for place in places], axis=0)

    cells = stack_ref.shape[0] // 2
    present = [[p for p in (2 * c, 2 * c + 1) if p != LATE] for c in range(cells)]
    for c in range(cells):
        q, g = take(present[c], 0), take(present[c], 3)
        width = q.shape[0]
        keys = [place for place in key_places(c) if place != LATE]
        scores = [b for n in near_cells(c) for b in blocks_of(times_t(take(present[n], 1), q))]
        dprobs = [b for n in near_cells(c) for b in blocks_of(times_t(take(present[n], 2), g))]
        rows = [key_places(c).index(key) for key in keys]
        seen = [seen_ref[c, n : n + 1, :width] > 0 for n in rows]
        top = top_of(scores, seen)
        exps = weights(scores, seen, top)
        total = sum_of(exps)
        product = sum_of([e * d for e, d in zip(exps, dprobs)])
        if c == DONE:
            inverse = 1.0 / total
            delta = product * inverse
            terms = []
            for n, (weight, term) in enumerate(zip(exps, dprobs)):
                probs = weight * inverse
                terms.append((probs * (term - delta)).astype(jnp.bfloat16))
                done_ref[0, 128 * n : 128 * (n + 1)] = probs.astype(jnp.bfloat16)
                done_ref[1, 128 * n : 128 * (n + 1)] = terms[n]
            query_ref[...] = query_grad(take(key_places(c), 1), jnp.concatenate(terms, axis=0))
            continue
        for key, weight, term in zip(keys, exps, dprobs):
            row = 128 * key_places(c).index(key)
            exps_ref[c, row : row + 128, :width] = weight
            dprobs_ref[c, row : row + 128, :width] = term
        stats_ref[c, 0:1, :width] = top
        stats_ref[c, 1:2, :width] = total
        stats_ref[c, 2:3, :width] = product


def taker(slab, stack_ref):
    def take(places, n):
        columns = slice(n * HEAD_DIM, (n + 1) * HEAD_DIM)
        parts = [slab[:, columns] if p == LATE else stack_ref[p, :, columns] for p in places]
        return jnp.concatenate(parts, axis=0)

    return take


def put(out, n, value):
    out[:, n * HEAD_DIM : (n + 1) * HEAD_DIM] = value.astype(jnp.bfloat16)


def put_pair_grads(take, c, probs_low, dscores, outs):
    q, g = take(key_places(c), 0), take(key_places(c), 3)
    dk = jnp.dot(dscores, q, preferred_element_type=jnp.float32) * (1.0 / math.sqrt(HEAD_DIM))
    dv = jnp.dot(probs_low, g, preferred_element_type=jnp.float32)
    for a, out in enumerate(outs):
        put(out, 1, dk[128 * a : 128 * (a + 1)])
        put(out, 2, dv[128 * a : 128 * (a + 1)])


def late_kernel(slab, *refs):
    seen_ref, stack_ref, exps_ref, dprobs_ref, stats_ref, done_ref = refs[:6]
    outs = dict(zip(BEYOND, refs[6:10]))
    probs_out, dscores_out, query_out = refs[10:]
    cells = stack_ref.shape[0] // 2
    take = taker(slab, stack_ref)

    units = [(c, (2 * c, 2 * c + 1)) for c in range(cells) if c not in (DONE, LATE // 2)]
    units = [(LATE // 2, (place,)) for place in (LATE - 1, LATE)] + units
    fresh = [[p for p in key_places(c) if LATE in (p, *queries)] for c, queries in units]
    scores, dprobs, exps, inverse, delta, early_inverse = ([None] * len(units) for _ in range(6))
    for u, (c, queries) in enumerate(units):
        groups = [(LATE,)] if LATE not in queries else [(2 * n, 2 * n + 1) for n in near_cells(c)]
        groups = groups if fresh[u] else []
        mine_q, mine_g = take(queries, 0), take(queries, 3)
        scores[u] = [b for keys in groups for b in blocks_of(times_t(take(keys, 1), mine_q))]
        dprobs[u] = [b for keys in groups for b in blocks_of(times_t(take(keys, 2), mine_g))]
    seen = []
    for (c, queries), keys in zip(units, fresh):
        first = 128 * (queries[0] - 2 * c)
        columns = slice(first, first + 128 * len(queries))
        rows = [key_places(c).index(key) for key in keys]
        seen.append([seen_ref[c, n : n + 1, columns] > 0 for n in rows])
    tops = [top_of(blocks, flags) if blocks else None for blocks, flags in zip(scores, seen)]
    for u, (c, queries) in enumerate(units):
        early = LATE not in queries
        if early:
            top, total, product = (
                stats_ref[c, n : n + 1, : 128 * len(queries)] for n in range(3)
            )
        shrink = None
        if fresh[u]:
            new_top = jnp.maximum(top, tops[u]) if early else tops[u]
            exps[u] = weights(scores[u], seen[u], new_top)
            new_total = sum_of(exps[u])
            new_product = sum_of([e * d for e, d in zip(exps[u], dprobs[u])])
            if early:
                shrink = jnp.exp2(top - new_top)
                new_total = new_total + total * shrink
                new_product = new_product + product * shrink
            total, product = new_total, new_product
        inverse[u] = 1.0 / total
        delta[u] = product * inverse[u]
        early_inverse[u] = inverse[u] if shrink is None else inverse[u] * shrink

    def finished(u):
        c, queries = units[u]
        probs_low, dscores = [], []
        for n, key in enumerate(key_places(c)):
            if key in fresh[u]:
                index = fresh[u].index(key)
                probs, term = exps[u][index] * inverse[u], dprobs[u][index]
            else:
                place = (c, slice(128 * n, 128 * (n + 1)), slice(0, 128 * len(queries)))
                probs, term = exps_ref[place] * early_inverse[u], dprobs_ref[place]
            probs_low.append(probs.astype(jnp.bfloat16))
            dscores.append((probs * (term - delta[u])).astype(jnp.bfloat16))
        return probs_low, dscores

    probs_low = [{} for _ in range(cells)]
    dscores = [{} for _ in range(cells)]

    def rows_of(c):
        if c == DONE:
            pair = [blocks_of(done_ref[n]) for n in range(2)]
        elif LATE // 2 == c:
            sides = zip(finished(0), finished(1))
            pair = [
                [jnp.concatenate(both, axis=1) for both in zip(left, right)] for left, right in sides
            ]
        else:
            pair = finished(units.index((c, (2 * c, 2 * c + 1))))
        for t, n in enumerate(near_cells(c)):
            probs_low[n][c] = jnp.concatenate(pair[0][2 * t : 2 * t + 2], axis=0)
            dscores[n][c] = jnp.concatenate(pair[1][2 * t : 2 * t + 2], axis=0)

    def joined(blocks, c):
        return jnp.concatenate([blocks[n] for n in near_cells(c)], axis=1)

    for c in (LATE // 2, 1 - DONE, LATE // 2 ^ 1, DONE):
        rows_of(c)
    for c in (2, 3):
        places = (2 * c, 2 * c + 1)
        put_pair_grads(take, c, joined(probs_low[c], c), joined(dscores[c], c), [outs[p] for p in places])
    for c in (2, 3, 1 - DONE):
        terms = jnp.concatenate([dscores[n][c] for n in near_cells(c)], axis=0)
        dq = query_grad(take(key_places(c), 1), terms)
        if c == 1 - DONE:
            query_out[...] = dq
        else:
            for a in range(2):
                put(outs[2 * c + a], 0, dq[a])
    for n in (0, 1):
        probs_out[n] = joined(probs_low[n], n)
        dscores_out[n] = joined(dscores[n], n)


def rest_kernel(distances, slab, stack_ref, probs_ref, dscores_ref, *refs):
    query_refs, kept, outs, out_ref = refs[:2], refs[2:4], refs[4:-1], refs[-1]
    here = flat_index(GROUP)
    fixed = [distance(here) for distance in distances]
    fixed = {place: out for place, out in zip(fixed, outs) if isinstance(place, int)}
    take = taker(slab, stack_ref)
    for c in (0, 1):
        targets = [fixed.get(place, out_ref.at[place]) for place in (2 * c, 2 * c + 1)]
        put_pair_grads(take, c, probs_ref[c], dscores_ref[c], targets)
        for a, target in enumerate(targets):
            put(target, 0, query_refs[c][a])
    for place, ref in zip((4, 6), kept):
        out_ref[place] = ref[...]
    for distance, out in zip(distances, outs):
        if not isinstance(distance(here), int):
            out[...] = out_ref[distance(here)]


SMEM = pl.BlockSpec(memory_space=pltpu.SMEM)
VMEM = pl.BlockSpec(memory_space=pltpu.VMEM)
ANY = pl.BlockSpec(memory_space=pl.ANY)


def slab_shape(tokens, parts):
    return jax.ShapeDtypeStruct((tokens, parts * HEAD_DIM), jnp.bfloat16)


def pack(arrays, distances, name, *extras):
    tokens = arrays[0].shape[0]
    count = len(distances)
    outs = [slab_shape(tokens, 4)] * count
    outs += [jax.ShapeDtypeStruct(extra.shape, extra.dtype) for extra in extras]
    return pl.pallas_call(
        functools.partial(pack_kernel, distances),
        out_shape=outs,
        in_specs=[ANY] * (4 + len(extras)),
        out_specs=[ANY] * len(outs),
        scratch_shapes=[pltpu.SemaphoreType.DMA((4 * count + len(extras),))],
        compiler_params=pltpu.CompilerParams(vmem_limit_bytes=MIB),
        name=name,
    )(*arrays, *extras)


def unpack(whole, distances, slabs, name, *arrays):
    count = len(distances)
    return pl.pallas_call(
        functools.partial(unpack_kernel, distances),
        out_shape=[whole] * 3,
        in_specs=[ANY] * (count + len(arrays)),
        out_specs=[ANY] * 3,
        scratch_shapes=[pltpu.SemaphoreType.DMA((3 * count,))],
        compiler_params=pltpu.CompilerParams(vmem_limit_bytes=MIB),
        input_output_aliases={count + n: n for n in range(len(arrays))},
        name=name,
    )(*slabs, *arrays)


def by_heads(queries, keys, values, out_grad, block_mask):
    devices = lax.axis_size(GROUP)
    cells = lax.axis_size("blk")
    tokens = queries.shape[0]
    *arrays, block_mask = [
        pltpu.with_memory_space_constraint(array, pltpu.HBM)
        for array in (queries, keys, values, out_grad, block_mask)
    ]
    sent = pack(arrays, INWARD[:FIRST], "pack_first")
    arrays, sent = lax.optimization_barrier((arrays, sent))
    *rest, own, block_mask = pack(arrays, INWARD[FIRST:] + (STAY,), "pack_rest", block_mask)
    got = list(sent) + rest
    for n, distance in enumerate(INWARD):
        if n in AFTER:
            got[n], got[AFTER[n]] = lax.optimization_barrier((got[n], got[AFTER[n]]))
        got[n] = exchange(got[n], distance)
    soon = [n for n, distance in enumerate(INWARD) if distance is not LATE_HOP]
    seen = pl.pallas_call(
        seen_kernel,
        out_shape=jax.ShapeDtypeStruct((cells, 8, 2 * tokens), jnp.float32),
        in_specs=[SMEM],
        out_specs=VMEM,
        compiler_params=pltpu.CompilerParams(vmem_limit_bytes=MIB),
        name="seen",
    )(block_mask)
    pairs = jax.ShapeDtypeStruct((cells, 6 * tokens, 2 * tokens), jnp.float32)
    partial = pl.pallas_call(
        functools.partial(early_kernel, [INWARD[n] for n in soon] + [STAY]),
        out_shape=[
            jax.ShapeDtypeStruct((devices, tokens, 4 * HEAD_DIM), jnp.bfloat16),
            pairs,
            pairs,
            jax.ShapeDtypeStruct((cells, 8, 2 * tokens), jnp.float32),
            jax.ShapeDtypeStruct((2, 6 * tokens, 2 * tokens), jnp.bfloat16),
            jax.ShapeDtypeStruct((2, tokens, HEAD_DIM), jnp.bfloat16),
        ],
        in_specs=[VMEM] * devices,
        out_specs=[VMEM] * 6,
        compiler_params=pltpu.CompilerParams(vmem_limit_bytes=24 * MIB),
        name="early",
    )(seen, *[got[n] for n in soon], own)
    stack, *partial, query_grad_done = partial
    slab = got[INWARD.index(LATE_HOP)]
    low = jax.ShapeDtypeStruct((2, 2 * tokens, 6 * tokens), jnp.bfloat16)
    *beyond, probs_low, dscores, query_grad_other = pl.pallas_call(
        late_kernel,
        out_shape=[slab_shape(tokens, 3)] * len(BEYOND)
        + [low, low, jax.ShapeDtypeStruct((2, tokens, HEAD_DIM), jnp.bfloat16)],
        in_specs=[VMEM] * 7,
        out_specs=[VMEM] * (len(BEYOND) + 3),
        compiler_params=pltpu.CompilerParams(vmem_limit_bytes=24 * MIB),
        name="late",
    )(slab, seen, stack, *partial)
    beyond = dict(zip(BEYOND, beyond))
    query_grads = (query_grad_done, query_grad_other)
    query_grads = query_grads[::-1] if DONE == 1 else query_grads
    distances = OUTWARD + (STAY,)
    rest = pl.pallas_call(
        functools.partial(rest_kernel, distances[2:]),
        out_shape=[slab_shape(tokens, 3)] * (devices - 2),
        in_specs=[VMEM] * 8,
        out_specs=[VMEM] * (devices - 2),
        scratch_shapes=[pltpu.VMEM((devices, tokens, 3 * HEAD_DIM), jnp.bfloat16)],
        compiler_params=pltpu.CompilerParams(vmem_limit_bytes=24 * MIB),
        name="rest",
    )(slab, stack, probs_low, dscores, *query_grads, beyond[4], beyond[6])
    grads = [beyond[5], beyond[7], *rest]
    back = [exchange(grad, distance) for grad, distance in zip(grads, OUTWARD)] + [grads[-1]]
    whole = jax.ShapeDtypeStruct(queries.shape, queries.dtype)
    grads = []
    for number, group in enumerate(UNPACKED):
        hops = [distances[n] for n in group]
        grads = unpack(whole, hops, [back[n] for n in group], f"unpack_{number}", *grads)
    return grads


def local(queries, keys, values, out_grad, block_mask):
    heads = queries.shape[1] // HEAD_DIM
    cells, halves = lax.axis_size("blk"), lax.axis_size("uly")
    if (cells, halves) == (4, 2) and heads == cells * halves and queries.shape[0] == 128:
        return by_heads(queries, keys, values, out_grad, block_mask)
    return by_cells(queries, keys, values, out_grad, block_mask)


def solution(mesh):
    return jax.shard_map(
        local,
        mesh=mesh,
        in_specs=(
            P(("batch", "blk", "uly"), None),
            P(("batch", "blk", "uly"), None),
            P(("batch", "blk", "uly"), None),
            P(("batch", "blk", "uly"), None),
            P("batch", None),
        ),
        out_specs=(
            P(("batch", "blk", "uly"), None),
            P(("batch", "blk", "uly"), None),
            P(("batch", "blk", "uly"), None),
        ),
        check_vma=False,
    )
```

```python
import functools
import math

import jax
import jax.numpy as jnp
from jax import lax
from jax.experimental import pallas as pl
from jax.experimental.pallas import tpu as pltpu
from jax.sharding import PartitionSpec as P

HEAD_DIM = 128
MIB = 1024 * 1024
GROUP = ("blk", "uly")


def padded(block, sides, width):
    for axis, dim in sides:
        count = lax.axis_size(axis)
        forward = [(i, i + 1) for i in range(count - 1)]
        forward.append((count - 1, 0))
        backward = [(target, source) for source, target in forward]
        low = lax.ppermute(
            lax.slice_in_dim(block, block.shape[dim] - width, None, axis=dim), axis, forward
        )
        high = lax.ppermute(lax.slice_in_dim(block, 0, width, axis=dim), axis, backward)
        block = jnp.concatenate([low, block, high], axis=dim)
    return block


def passed_along(block, axis, distance):
    devices = range(lax.axis_size(axis))
    route = [((i - distance) % len(devices), i) for i in devices]
    return lax.ppermute(block, axis, route)


def times_t(left, right):
    return lax.dot_general(
        left, right, (((1,), (1,)), ((), ())), preferred_element_type=jnp.float32
    )


def t_times(left, right):
    return lax.dot_general(
        left, right, (((0,), (0,)), ((), ())), preferred_element_type=jnp.float32
    )


def widen_blocks(mask_blocks):
    return jnp.repeat(jnp.repeat(mask_blocks > 0, 128, axis=0), 128, axis=1)


def by_cells(queries, keys, values, out_grad, block_mask):
    local_q, local_k, local_v, local_g = (
        lax.all_to_all(queries, "uly", split_axis=1, concat_axis=0, tiled=True),
        lax.all_to_all(keys, "uly", split_axis=1, concat_axis=0, tiled=True),
        lax.all_to_all(values, "uly", split_axis=1, concat_axis=0, tiled=True),
        lax.all_to_all(out_grad, "uly", split_axis=1, concat_axis=0, tiled=True),
    )
    genes = local_q.shape[0]
    heads_here = local_q.shape[1] // HEAD_DIM
    scale = 1.0 / math.sqrt(HEAD_DIM)
    cells = lax.axis_size("blk")
    here = lax.axis_index("blk")
    per_cell = genes // 128
    near = (here + jnp.array([-1, 0, 1], dtype=jnp.int32) + cells) % cells
    mask_rows = lax.dynamic_slice_in_dim(block_mask, here * per_cell, per_cell, 0).reshape(
        per_cell, cells, per_cell
    )
    row_mask = widen_blocks(jnp.take(mask_rows, near, axis=1).reshape(per_cell, 3 * per_cell))
    pairs = jnp.stack([local_k, local_v], axis=1)
    band = padded(pairs, (("blk", 0),), genes)
    q_grads = []
    k_parts = []
    v_parts = []
    for head in range(heads_here):
        lower = head * HEAD_DIM
        upper = lower + HEAD_DIM
        q_head = local_q[:, lower:upper]
        g_head = local_g[:, lower:upper]
        k_band = band[:, 0, lower:upper]
        v_band = band[:, 1, lower:upper]
        scores = jnp.where(row_mask, times_t(q_head, k_band) * scale, -1e30)
        top = jnp.max(scores, axis=1, keepdims=True)
        total = jnp.sum(jnp.where(row_mask, jnp.exp(scores - top), 0.0), axis=1, keepdims=True)
        lse = top + jnp.log(total)
        probs = jnp.where(row_mask, jnp.exp(scores - lse), 0.0)
        dprobs = times_t(g_head, v_band)
        delta = jnp.sum(probs * dprobs, axis=1, keepdims=True)
        dscores = (probs * (dprobs - delta)).astype(jnp.bfloat16)
        q_grads.append(
            (jnp.dot(dscores, k_band, preferred_element_type=jnp.float32) * scale).astype(
                jnp.bfloat16
            )
        )
        k_parts.append(t_times(dscores, q_head))
        v_parts.append(t_times(probs.astype(jnp.bfloat16), g_head))
    query_grad = jnp.concatenate(q_grads, axis=1)
    partial_terms = jnp.stack(
        [jnp.concatenate(k_parts, axis=1), jnp.concatenate(v_parts, axis=1)], axis=1
    )
    from_next = passed_along(partial_terms[:genes].astype(jnp.bfloat16), "blk", -1).astype(
        jnp.float32
    )
    from_prior = passed_along(partial_terms[2 * genes :].astype(jnp.bfloat16), "blk", 1).astype(
        jnp.float32
    )
    summed = partial_terms[genes : 2 * genes] + from_next + from_prior
    key_grad = (summed[:, 0] * scale).astype(jnp.bfloat16)
    value_grad = summed[:, 1].astype(jnp.bfloat16)
    return (
        lax.all_to_all(query_grad, "uly", split_axis=0, concat_axis=1, tiled=True),
        lax.all_to_all(key_grad, "uly", split_axis=0, concat_axis=1, tiled=True),
        lax.all_to_all(value_grad, "uly", split_axis=0, concat_axis=1, tiled=True),
    )


def flat_index(axes):
    index = 0
    for axis in axes:
        index = index * lax.axis_size(axis) + lax.axis_index(axis)
    return index


def same_core(here):
    return (here >> 1) & 1


def even_places(here):
    return (here ^ (here >> 1) ^ (here >> 2)) & 1


def hop(first, second=None, chooser=same_core):
    if second is None:
        return lambda here: first
    return lambda here: first + (second - first) * chooser(here)


STAY = hop(0)
CORE = hop(2)
FAR = hop(5)
FAR_CORE = hop(7)
SIDE = hop(4, 1)
OTHER_SIDE = hop(1, 4)
SIDE_CORE = hop(6, 3, even_places)
OTHER_SIDE_CORE = hop(3, 6, even_places)

INWARD = (FAR, SIDE_CORE, CORE, SIDE, OTHER_SIDE, OTHER_SIDE_CORE, FAR_CORE)
OUTWARD = (FAR, FAR_CORE, SIDE, OTHER_SIDE, SIDE_CORE, OTHER_SIDE_CORE, CORE)
FIRST = 2
UNPACKED = ((-1, 0, 1), (2, 3), (4, 5, 6))
LATE_HOP = FAR_CORE
LATE = 7
BEYOND = (4, 5, 6, 7)
DONE = 1
OTHER = 0
AFTER = {}
EXPONENT = math.log2(math.e) / math.sqrt(HEAD_DIM)


def exchange(block, distance):
    places = range(lax.axis_size(GROUP))
    return lax.ppermute(block, GROUP, [(i, i ^ distance(i)) for i in places])


def part(ref, n):
    return ref.at[:, n * HEAD_DIM : (n + 1) * HEAD_DIM]


def head_of(ref, head):
    return ref.at[:, pl.ds(pl.multiple_of(head * HEAD_DIM, HEAD_DIM), HEAD_DIM)]


def run(copies):
    for copy in copies:
        copy.start()
    for copy in copies:
        copy.wait()


def pack_kernel(distances, *refs):
    count = len(distances)
    extras = (len(refs) - 1 - count - 4) // 2
    sources, outs, sems = refs[: 4 + extras], refs[4 + extras : -1], refs[-1]
    here = flat_index(GROUP)
    pairs = list(zip(sources[4:], outs[count:]))
    for distance, slab in zip(distances, outs):
        for n, array in enumerate(sources[:4]):
            pairs.append((head_of(array, here ^ distance(here)), part(slab, n)))
    run([pltpu.make_async_copy(*pair, sems.at[n]) for n, pair in enumerate(pairs)])


def unpack_kernel(distances, *refs):
    slabs, arrays, sems = refs[: len(distances)], refs[-4:-1], refs[-1]
    here = flat_index(GROUP)
    pairs = []
    for distance, slab in zip(distances, slabs):
        for n, array in enumerate(arrays):
            pairs.append((part(slab, n), head_of(array, here ^ distance(here))))
    run([pltpu.make_async_copy(*pair, sems.at[n]) for n, pair in enumerate(pairs)])


def near_cells(c):
    return (c, c ^ 1, c ^ 3)


def key_places(c):
    return [2 * n + a for n in near_cells(c) for a in range(2)]


def blocks_of(value):
    return [value[r : r + 128] for r in range(0, value.shape[0], 128)]


def seen_by(mask_ref, here, key, queries):
    flags = [jnp.full((1, 128), mask_ref[here ^ query, here ^ key]) for query in queries]
    return jnp.concatenate(flags, axis=1) > 0


def weights(scores, seen, top):
    return [
        jnp.exp2(block * EXPONENT - jnp.where(flag, top, 1e30)) for block, flag in zip(scores, seen)
    ]


def top_of(scores, seen):
    top = jnp.full((1, scores[0].shape[1]), -1e30, jnp.float32)
    for block, flag in zip(scores, seen):
        top = jnp.maximum(top, jnp.where(flag, jnp.max(block, axis=0, keepdims=True), -1e30))
    return top * EXPONENT


def sum_of(blocks):
    total = blocks[0]
    for block in blocks[1:]:
        total = total + block
    return jnp.sum(total, axis=0, keepdims=True)


def query_grad(keys, dscores):
    low = (t_times(keys, dscores) * (1.0 / math.sqrt(HEAD_DIM))).T.astype(jnp.bfloat16)
    return low.reshape(-1, 128, HEAD_DIM)


def seen_kernel(mask_ref, seen_ref):
    here = flat_index(GROUP)
    for c in range(seen_ref.shape[0]):
        for n, key in enumerate(key_places(c)):
            flags = seen_by(mask_ref, here, key, (2 * c, 2 * c + 1))
            seen_ref[c, n : n + 1] = flags.astype(jnp.float32)


def early_kernel(distances, seen_ref, *refs):
    slabs, outs = refs[:-6], refs[-6:]
    stack_ref, exps_ref, dprobs_ref, stats_ref, done_ref, query_ref = outs
    here = flat_index(GROUP)
    for distance, slab in zip(distances, slabs):
        stack_ref[distance(here)] = slab[...]

    def take(places, n):
        columns = slice(n * HEAD_DIM, (n + 1) * HEAD_DIM)
        return jnp.concatenate([stack_ref[place, :, columns] for place in places], axis=0)

    cells = stack_ref.shape[0] // 2
    present = [[p for p in (2 * c, 2 * c + 1) if p != LATE] for c in range(cells)]
    for c in range(cells):
        q, g = take(present[c], 0), take(present[c], 3)
        width = q.shape[0]
        keys = [place for place in key_places(c) if place != LATE]
        scores = [b for n in near_cells(c) for b in blocks_of(times_t(take(present[n], 1), q))]
        dprobs = [b for n in near_cells(c) for b in blocks_of(times_t(take(present[n], 2), g))]
        rows = [key_places(c).index(key) for key in keys]
        seen = [seen_ref[c, n : n + 1, :width] > 0 for n in rows]
        top = top_of(scores, seen)
        exps = weights(scores, seen, top)
        total = sum_of(exps)
        product = sum_of([e * d for e, d in zip(exps, dprobs)])
        if c == DONE:
            inverse = 1.0 / total
            delta = product * inverse
            terms = []
            for n, (weight, term) in enumerate(zip(exps, dprobs)):
                probs = weight * inverse
                terms.append((probs * (term - delta)).astype(jnp.bfloat16))
                done_ref[0, 128 * n : 128 * (n + 1)] = probs.astype(jnp.bfloat16)
                done_ref[1, 128 * n : 128 * (n + 1)] = terms[n]
            query_ref[...] = query_grad(take(key_places(c), 1), jnp.concatenate(terms, axis=0))
            continue
        for key, weight, term in zip(keys, exps, dprobs):
            row = 128 * key_places(c).index(key)
            exps_ref[c, row : row + 128, :width] = weight
            dprobs_ref[c, row : row + 128, :width] = term
        stats_ref[c, 0:1, :width] = top
        stats_ref[c, 1:2, :width] = total
        stats_ref[c, 2:3, :width] = product


def taker(slab, stack_ref):
    def take(places, n):
        columns = slice(n * HEAD_DIM, (n + 1) * HEAD_DIM)
        parts = [slab[:, columns] if p == LATE else stack_ref[p, :, columns] for p in places]
        return jnp.concatenate(parts, axis=0)

    return take


def put(out, n, value):
    out[:, n * HEAD_DIM : (n + 1) * HEAD_DIM] = value.astype(jnp.bfloat16)


def put_pair_grads(take, c, probs_low, dscores, outs):
    q, g = take(key_places(c), 0), take(key_places(c), 3)
    dk = jnp.dot(dscores, q, preferred_element_type=jnp.float32) * (1.0 / math.sqrt(HEAD_DIM))
    dv = jnp.dot(probs_low, g, preferred_element_type=jnp.float32)
    for a, out in enumerate(outs):
        put(out, 1, dk[128 * a : 128 * (a + 1)])
        put(out, 2, dv[128 * a : 128 * (a + 1)])


def late_kernel(slab, *refs):
    seen_ref, stack_ref, exps_ref, dprobs_ref, stats_ref, done_ref = refs[:6]
    outs = dict(zip(BEYOND, refs[6:10]))
    tiles_out, rows_out = refs[10:]
    cells = stack_ref.shape[0] // 2
    take = taker(slab, stack_ref)

    units = [(c, (2 * c, 2 * c + 1)) for c in range(cells) if c not in (DONE, LATE // 2)]
    units = [(LATE // 2, (place,)) for place in (LATE - 1, LATE)] + units
    fresh = [[p for p in key_places(c) if LATE in (p, *queries)] for c, queries in units]
    scores, dprobs, exps, inverse, delta, early_inverse = ([None] * len(units) for _ in range(6))
    for u, (c, queries) in enumerate(units):
        groups = [(LATE,)] if LATE not in queries else [(2 * n, 2 * n + 1) for n in near_cells(c)]
        groups = groups if fresh[u] else []
        mine_q, mine_g = take(queries, 0), take(queries, 3)
        scores[u] = [b for keys in groups for b in blocks_of(times_t(take(keys, 1), mine_q))]
        dprobs[u] = [b for keys in groups for b in blocks_of(times_t(take(keys, 2), mine_g))]
    seen = []
    for (c, queries), keys in zip(units, fresh):
        first = 128 * (queries[0] - 2 * c)
        columns = slice(first, first + 128 * len(queries))
        rows = [key_places(c).index(key) for key in keys]
        seen.append([seen_ref[c, n : n + 1, columns] > 0 for n in rows])
    tops = [top_of(blocks, flags) if blocks else None for blocks, flags in zip(scores, seen)]
    for u, (c, queries) in enumerate(units):
        early = LATE not in queries
        if early:
            top, total, product = (
                stats_ref[c, n : n + 1, : 128 * len(queries)] for n in range(3)
            )
        shrink = None
        if fresh[u]:
            new_top = jnp.maximum(top, tops[u]) if early else tops[u]
            exps[u] = weights(scores[u], seen[u], new_top)
            new_total = sum_of(exps[u])
            new_product = sum_of([e * d for e, d in zip(exps[u], dprobs[u])])
            if early:
                shrink = jnp.exp2(top - new_top)
                new_total = new_total + total * shrink
                new_product = new_product + product * shrink
            total, product = new_total, new_product
        inverse[u] = 1.0 / total
        delta[u] = product * inverse[u]
        early_inverse[u] = inverse[u] if shrink is None else inverse[u] * shrink

    def finished(u, n):
        c, queries = units[u]
        low, terms = [], []
        for key in (2 * n, 2 * n + 1):
            if key in fresh[u]:
                index = fresh[u].index(key)
                probs, dprob = exps[u][index] * inverse[u], dprobs[u][index]
            else:
                row = 128 * key_places(c).index(key)
                place = (c, slice(row, row + 128), slice(0, 128 * len(queries)))
                probs, dprob = exps_ref[place] * early_inverse[u], dprobs_ref[place]
            low.append(probs.astype(jnp.bfloat16))
            terms.append((probs * (dprob - delta[u])).astype(jnp.bfloat16))
        return jnp.concatenate(low, axis=0), jnp.concatenate(terms, axis=0)

    tiles = {}
    for c in (LATE // 2, OTHER, LATE // 2 ^ 1, DONE):
        for t, n in enumerate(near_cells(c)):
            if c < 2 and n < 2:
                continue
            if c == DONE:
                tiles[n, c] = [done_ref[i, 256 * t : 256 * (t + 1)] for i in range(2)]
            elif c == LATE // 2:
                sides = zip(finished(0, n), finished(1, n))
                tiles[n, c] = [jnp.concatenate(both, axis=1) for both in sides]
            else:
                tiles[n, c] = finished(units.index((c, (2 * c, 2 * c + 1))), n)
    for c in (2, 3):
        pair = [jnp.concatenate([tiles[c, m][i] for m in near_cells(c)], axis=1) for i in range(2)]
        put_pair_grads(take, c, *pair, [outs[2 * c], outs[2 * c + 1]])
    for c in (2, 3):
        terms = jnp.concatenate([tiles[n, c][1] for n in near_cells(c)], axis=0)
        dq = query_grad(take(key_places(c), 1), terms)
        for a in range(2):
            put(outs[2 * c + a], 0, dq[a])
    for i in range(2):
        for n in (0, 1):
            tiles_out[i, n] = tiles[n, n ^ 3][i]
    tiles_out[1, 2] = tiles[OTHER ^ 3, OTHER][1]
    u = units.index((OTHER, (2 * OTHER, 2 * OTHER + 1)))
    rows_out[0:1] = early_inverse[u]
    rows_out[1:2] = delta[u]


def rest_kernel(distances, slab, *refs):
    stack_ref, exps_ref, dprobs_ref, done_ref, query_ref, tiles_ref, rows_ref = refs[:7]
    kept, outs, out_ref = refs[7:9], refs[9:-1], refs[-1]
    here = flat_index(GROUP)
    fixed = [distance(here) for distance in distances]
    fixed = {place: out for place, out in zip(fixed, outs) if isinstance(place, int)}
    take = taker(slab, stack_ref)
    tiles = {(n, n ^ 3): [tiles_ref[i, n] for i in range(2)] for n in (0, 1)}
    for n in (0, 1):
        rows = [slice(256 * near_cells(c).index(n), 256 * (near_cells(c).index(n) + 1)) for c in (DONE, OTHER)]
        tiles[n, DONE] = [done_ref[i, rows[0]] for i in range(2)]
        probs = exps_ref[OTHER, rows[1]] * rows_ref[0:1]
        terms = probs * (dprobs_ref[OTHER, rows[1]] - rows_ref[1:2])
        tiles[n, OTHER] = [probs.astype(jnp.bfloat16), terms.astype(jnp.bfloat16)]
    terms = [tiles_ref[1, 2] if n > 1 else tiles[n, OTHER][1] for n in near_cells(OTHER)]
    other_query = query_grad(take(key_places(OTHER), 1), jnp.concatenate(terms, axis=0))
    for c in (0, 1):
        targets = [fixed.get(place, out_ref.at[place]) for place in (2 * c, 2 * c + 1)]
        pair = [jnp.concatenate([tiles[c, m][i] for m in near_cells(c)], axis=1) for i in range(2)]
        put_pair_grads(take, c, *pair, targets)
        for a, target in enumerate(targets):
            put(target, 0, query_ref[a] if c == DONE else other_query[a])
    for place, ref in zip((4, 6), kept):
        out_ref[place] = ref[...]
    for distance, out in zip(distances, outs):
        if not isinstance(distance(here), int):
            out[...] = out_ref[distance(here)]


SMEM = pl.BlockSpec(memory_space=pltpu.SMEM)
VMEM = pl.BlockSpec(memory_space=pltpu.VMEM)
ANY = pl.BlockSpec(memory_space=pl.ANY)


def slab_shape(tokens, parts):
    return jax.ShapeDtypeStruct((tokens, parts * HEAD_DIM), jnp.bfloat16)


def pack(arrays, distances, name, *extras):
    tokens = arrays[0].shape[0]
    count = len(distances)
    outs = [slab_shape(tokens, 4)] * count
    outs += [jax.ShapeDtypeStruct(extra.shape, extra.dtype) for extra in extras]
    return pl.pallas_call(
        functools.partial(pack_kernel, distances),
        out_shape=outs,
        in_specs=[ANY] * (4 + len(extras)),
        out_specs=[ANY] * len(outs),
        scratch_shapes=[pltpu.SemaphoreType.DMA((4 * count + len(extras),))],
        compiler_params=pltpu.CompilerParams(vmem_limit_bytes=MIB),
        name=name,
    )(*arrays, *extras)


def unpack(whole, distances, slabs, name, *arrays):
    count = len(distances)
    return pl.pallas_call(
        functools.partial(unpack_kernel, distances),
        out_shape=[whole] * 3,
        in_specs=[ANY] * (count + len(arrays)),
        out_specs=[ANY] * 3,
        scratch_shapes=[pltpu.SemaphoreType.DMA((3 * count,))],
        compiler_params=pltpu.CompilerParams(vmem_limit_bytes=MIB),
        input_output_aliases={count + n: n for n in range(len(arrays))},
        name=name,
    )(*slabs, *arrays)


def by_heads(queries, keys, values, out_grad, block_mask):
    devices = lax.axis_size(GROUP)
    cells = lax.axis_size("blk")
    tokens = queries.shape[0]
    *arrays, block_mask = [
        pltpu.with_memory_space_constraint(array, pltpu.HBM)
        for array in (queries, keys, values, out_grad, block_mask)
    ]
    sent = pack(arrays, INWARD[:FIRST], "pack_first")
    arrays, sent = lax.optimization_barrier((arrays, sent))
    *rest, own, block_mask = pack(arrays, INWARD[FIRST:] + (STAY,), "pack_rest", block_mask)
    got = list(sent) + rest
    for n, distance in enumerate(INWARD):
        if n in AFTER:
            got[n], got[AFTER[n]] = lax.optimization_barrier((got[n], got[AFTER[n]]))
        got[n] = exchange(got[n], distance)
    soon = [n for n, distance in enumerate(INWARD) if distance is not LATE_HOP]
    seen = pl.pallas_call(
        seen_kernel,
        out_shape=jax.ShapeDtypeStruct((cells, 8, 2 * tokens), jnp.float32),
        in_specs=[SMEM],
        out_specs=VMEM,
        compiler_params=pltpu.CompilerParams(vmem_limit_bytes=MIB),
        name="seen",
    )(block_mask)
    pairs = jax.ShapeDtypeStruct((cells, 6 * tokens, 2 * tokens), jnp.float32)
    partial = pl.pallas_call(
        functools.partial(early_kernel, [INWARD[n] for n in soon] + [STAY]),
        out_shape=[
            jax.ShapeDtypeStruct((devices, tokens, 4 * HEAD_DIM), jnp.bfloat16),
            pairs,
            pairs,
            jax.ShapeDtypeStruct((cells, 8, 2 * tokens), jnp.float32),
            jax.ShapeDtypeStruct((2, 6 * tokens, 2 * tokens), jnp.bfloat16),
            jax.ShapeDtypeStruct((2, tokens, HEAD_DIM), jnp.bfloat16),
        ],
        in_specs=[VMEM] * devices,
        out_specs=[VMEM] * 6,
        compiler_params=pltpu.CompilerParams(vmem_limit_bytes=24 * MIB),
        name="early",
    )(seen, *[got[n] for n in soon], own)
    stack, exps, dprobs, stats, done, done_query = partial
    slab = got[INWARD.index(LATE_HOP)]
    *beyond, tiles, rows = pl.pallas_call(
        late_kernel,
        out_shape=[slab_shape(tokens, 3)] * len(BEYOND)
        + [
            jax.ShapeDtypeStruct((2, 3, 2 * tokens, 2 * tokens), jnp.bfloat16),
            jax.ShapeDtypeStruct((8, 2 * tokens), jnp.float32),
        ],
        in_specs=[VMEM] * 7,
        out_specs=[VMEM] * (len(BEYOND) + 2),
        compiler_params=pltpu.CompilerParams(vmem_limit_bytes=24 * MIB),
        name="late",
    )(slab, seen, stack, exps, dprobs, stats, done)
    beyond = dict(zip(BEYOND, beyond))
    distances = OUTWARD + (STAY,)
    rest = pl.pallas_call(
        functools.partial(rest_kernel, distances[2:]),
        out_shape=[slab_shape(tokens, 3)] * (devices - 2),
        in_specs=[VMEM] * 10,
        out_specs=[VMEM] * (devices - 2),
        scratch_shapes=[pltpu.VMEM((devices, tokens, 3 * HEAD_DIM), jnp.bfloat16)],
        compiler_params=pltpu.CompilerParams(vmem_limit_bytes=24 * MIB),
        name="rest",
    )(slab, stack, exps, dprobs, done, done_query, tiles, rows, beyond[4], beyond[6])
    grads = [beyond[5], beyond[7], *rest]
    back = [exchange(grad, distance) for grad, distance in zip(grads, OUTWARD)] + [grads[-1]]
    whole = jax.ShapeDtypeStruct(queries.shape, queries.dtype)
    grads = []
    for number, group in enumerate(UNPACKED):
        hops = [distances[n] for n in group]
        grads = unpack(whole, hops, [back[n] for n in group], f"unpack_{number}", *grads)
    return grads


def local(queries, keys, values, out_grad, block_mask):
    heads = queries.shape[1] // HEAD_DIM
    cells, halves = lax.axis_size("blk"), lax.axis_size("uly")
    if (cells, halves) == (4, 2) and heads == cells * halves and queries.shape[0] == 128:
        return by_heads(queries, keys, values, out_grad, block_mask)
    return by_cells(queries, keys, values, out_grad, block_mask)


def solution(mesh):
    return jax.shard_map(
        local,
        mesh=mesh,
        in_specs=(
            P(("batch", "blk", "uly"), None),
            P(("batch", "blk", "uly"), None),
            P(("batch", "blk", "uly"), None),
            P(("batch", "blk", "uly"), None),
            P("batch", None),
        ),
        out_specs=(
            P(("batch", "blk", "uly"), None),
            P(("batch", "blk", "uly"), None),
            P(("batch", "blk", "uly"), None),
        ),
        check_vma=False,
    )
```

```python
import functools
import math

import jax
import jax.numpy as jnp
from jax import lax
from jax.experimental import pallas as pl
from jax.experimental.pallas import tpu as pltpu
from jax.sharding import PartitionSpec as P

HEAD_DIM = 128
MIB = 1024 * 1024
GROUP = ("blk", "uly")


def padded(block, sides, width):
    for axis, dim in sides:
        count = lax.axis_size(axis)
        forward = [(i, i + 1) for i in range(count - 1)]
        forward.append((count - 1, 0))
        backward = [(target, source) for source, target in forward]
        low = lax.ppermute(
            lax.slice_in_dim(block, block.shape[dim] - width, None, axis=dim), axis, forward
        )
        high = lax.ppermute(lax.slice_in_dim(block, 0, width, axis=dim), axis, backward)
        block = jnp.concatenate([low, block, high], axis=dim)
    return block


def passed_along(block, axis, distance):
    devices = range(lax.axis_size(axis))
    route = [((i - distance) % len(devices), i) for i in devices]
    return lax.ppermute(block, axis, route)


def times_t(left, right):
    return lax.dot_general(
        left, right, (((1,), (1,)), ((), ())), preferred_element_type=jnp.float32
    )


def t_times(left, right):
    return lax.dot_general(
        left, right, (((0,), (0,)), ((), ())), preferred_element_type=jnp.float32
    )


def widen_blocks(mask_blocks):
    return jnp.repeat(jnp.repeat(mask_blocks > 0, 128, axis=0), 128, axis=1)


def by_cells(queries, keys, values, out_grad, block_mask):
    local_q, local_k, local_v, local_g = (
        lax.all_to_all(queries, "uly", split_axis=1, concat_axis=0, tiled=True),
        lax.all_to_all(keys, "uly", split_axis=1, concat_axis=0, tiled=True),
        lax.all_to_all(values, "uly", split_axis=1, concat_axis=0, tiled=True),
        lax.all_to_all(out_grad, "uly", split_axis=1, concat_axis=0, tiled=True),
    )
    genes = local_q.shape[0]
    heads_here = local_q.shape[1] // HEAD_DIM
    scale = 1.0 / math.sqrt(HEAD_DIM)
    cells = lax.axis_size("blk")
    here = lax.axis_index("blk")
    per_cell = genes // 128
    near = (here + jnp.array([-1, 0, 1], dtype=jnp.int32) + cells) % cells
    mask_rows = lax.dynamic_slice_in_dim(block_mask, here * per_cell, per_cell, 0).reshape(
        per_cell, cells, per_cell
    )
    row_mask = widen_blocks(jnp.take(mask_rows, near, axis=1).reshape(per_cell, 3 * per_cell))
    pairs = jnp.stack([local_k, local_v], axis=1)
    band = padded(pairs, (("blk", 0),), genes)
    q_grads = []
    k_parts = []
    v_parts = []
    for head in range(heads_here):
        lower = head * HEAD_DIM
        upper = lower + HEAD_DIM
        q_head = local_q[:, lower:upper]
        g_head = local_g[:, lower:upper]
        k_band = band[:, 0, lower:upper]
        v_band = band[:, 1, lower:upper]
        scores = jnp.where(row_mask, times_t(q_head, k_band) * scale, -1e30)
        top = jnp.max(scores, axis=1, keepdims=True)
        total = jnp.sum(jnp.where(row_mask, jnp.exp(scores - top), 0.0), axis=1, keepdims=True)
        lse = top + jnp.log(total)
        probs = jnp.where(row_mask, jnp.exp(scores - lse), 0.0)
        dprobs = times_t(g_head, v_band)
        delta = jnp.sum(probs * dprobs, axis=1, keepdims=True)
        dscores = (probs * (dprobs - delta)).astype(jnp.bfloat16)
        q_grads.append(
            (jnp.dot(dscores, k_band, preferred_element_type=jnp.float32) * scale).astype(
                jnp.bfloat16
            )
        )
        k_parts.append(t_times(dscores, q_head))
        v_parts.append(t_times(probs.astype(jnp.bfloat16), g_head))
    query_grad = jnp.concatenate(q_grads, axis=1)
    partial_terms = jnp.stack(
        [jnp.concatenate(k_parts, axis=1), jnp.concatenate(v_parts, axis=1)], axis=1
    )
    from_next = passed_along(partial_terms[:genes].astype(jnp.bfloat16), "blk", -1).astype(
        jnp.float32
    )
    from_prior = passed_along(partial_terms[2 * genes :].astype(jnp.bfloat16), "blk", 1).astype(
        jnp.float32
    )
    summed = partial_terms[genes : 2 * genes] + from_next + from_prior
    key_grad = (summed[:, 0] * scale).astype(jnp.bfloat16)
    value_grad = summed[:, 1].astype(jnp.bfloat16)
    return (
        lax.all_to_all(query_grad, "uly", split_axis=0, concat_axis=1, tiled=True),
        lax.all_to_all(key_grad, "uly", split_axis=0, concat_axis=1, tiled=True),
        lax.all_to_all(value_grad, "uly", split_axis=0, concat_axis=1, tiled=True),
    )


def flat_index(axes):
    index = 0
    for axis in axes:
        index = index * lax.axis_size(axis) + lax.axis_index(axis)
    return index


def same_core(here):
    return (here >> 1) & 1


def even_places(here):
    return (here ^ (here >> 1) ^ (here >> 2)) & 1


def hop(first, second=None, chooser=same_core):
    if second is None:
        return lambda here: first
    return lambda here: first + (second - first) * chooser(here)


STAY = hop(0)
CORE = hop(2)
FAR = hop(5)
FAR_CORE = hop(7)
SIDE = hop(4, 1)
OTHER_SIDE = hop(1, 4)
SIDE_CORE = hop(6, 3, even_places)
OTHER_SIDE_CORE = hop(3, 6, even_places)

INWARD = (FAR, SIDE_CORE, CORE, SIDE, OTHER_SIDE, OTHER_SIDE_CORE, FAR_CORE)
OUTWARD = (FAR, FAR_CORE, SIDE, OTHER_SIDE, SIDE_CORE, OTHER_SIDE_CORE, CORE)
FIRST = 2
UNPACKED = ((-1, 0, 1), (2, 3), (4, 5, 6))
LATE_HOP = FAR_CORE
LATE = 7
BEYOND = (4, 5, 6, 7)
DONE = 1
OTHER = 0
AFTER = {}
EXPONENT = math.log2(math.e) / math.sqrt(HEAD_DIM)


def exchange(block, distance):
    places = range(lax.axis_size(GROUP))
    return lax.ppermute(block, GROUP, [(i, i ^ distance(i)) for i in places])


def part(ref, n):
    return ref.at[:, n * HEAD_DIM : (n + 1) * HEAD_DIM]


def head_of(ref, head):
    return ref.at[:, pl.ds(pl.multiple_of(head * HEAD_DIM, HEAD_DIM), HEAD_DIM)]


def run(copies):
    for copy in copies:
        copy.start()
    for copy in copies:
        copy.wait()


def pack_kernel(distances, *refs):
    count = len(distances)
    extras = (len(refs) - 1 - count - 4) // 2
    sources, outs, sems = refs[: 4 + extras], refs[4 + extras : -1], refs[-1]
    here = flat_index(GROUP)
    pairs = list(zip(sources[4:], outs[count:]))
    for distance, slab in zip(distances, outs):
        for n, array in enumerate(sources[:4]):
            pairs.append((head_of(array, here ^ distance(here)), part(slab, n)))
    run([pltpu.make_async_copy(*pair, sems.at[n]) for n, pair in enumerate(pairs)])


def unpack_kernel(distances, *refs):
    slabs, arrays, sems = refs[: len(distances)], refs[-4:-1], refs[-1]
    here = flat_index(GROUP)
    pairs = []
    for distance, slab in zip(distances, slabs):
        for n, array in enumerate(arrays):
            pairs.append((part(slab, n), head_of(array, here ^ distance(here))))
    run([pltpu.make_async_copy(*pair, sems.at[n]) for n, pair in enumerate(pairs)])


def near_cells(c):
    return (c, c ^ 1, c ^ 3)


def key_places(c):
    return [2 * n + a for n in near_cells(c) for a in range(2)]


def blocks_of(value):
    return [value[r : r + 128] for r in range(0, value.shape[0], 128)]


def seen_by(mask_ref, here, key, queries):
    flags = [jnp.full((1, 128), mask_ref[here ^ query, here ^ key]) for query in queries]
    return jnp.concatenate(flags, axis=1) > 0


def weights(scores, seen, top):
    return [
        jnp.exp2(block * EXPONENT - jnp.where(flag, top, 1e30)) for block, flag in zip(scores, seen)
    ]


def top_of(scores, seen):
    top = jnp.full((1, scores[0].shape[1]), -1e30, jnp.float32)
    for block, flag in zip(scores, seen):
        top = jnp.maximum(top, jnp.where(flag, jnp.max(block, axis=0, keepdims=True), -1e30))
    return top * EXPONENT


def sum_of(blocks):
    total = blocks[0]
    for block in blocks[1:]:
        total = total + block
    return jnp.sum(total, axis=0, keepdims=True)


def query_grad(keys, dscores):
    low = (t_times(keys, dscores) * (1.0 / math.sqrt(HEAD_DIM))).T.astype(jnp.bfloat16)
    return low.reshape(-1, 128, HEAD_DIM)


def seen_kernel(mask_ref, seen_ref):
    here = flat_index(GROUP)
    for c in range(seen_ref.shape[0]):
        for n, key in enumerate(key_places(c)):
            flags = seen_by(mask_ref, here, key, (2 * c, 2 * c + 1))
            seen_ref[c, n : n + 1] = flags.astype(jnp.float32)


def early_kernel(distances, seen_ref, *refs):
    slabs, outs = refs[:-7], refs[-7:]
    stack_ref, exps_ref, dprobs_ref, stats_ref, done_ref, query_ref, partial_ref = outs
    here = flat_index(GROUP)
    for distance, slab in zip(distances, slabs):
        stack_ref[distance(here)] = slab[...]

    def take(places, n):
        columns = slice(n * HEAD_DIM, (n + 1) * HEAD_DIM)
        return jnp.concatenate([stack_ref[place, :, columns] for place in places], axis=0)

    cells = stack_ref.shape[0] // 2
    present = [[p for p in (2 * c, 2 * c + 1) if p != LATE] for c in range(cells)]
    for c in range(cells):
        q, g = take(present[c], 0), take(present[c], 3)
        width = q.shape[0]
        keys = [place for place in key_places(c) if place != LATE]
        scores = [b for n in near_cells(c) for b in blocks_of(times_t(take(present[n], 1), q))]
        dprobs = [b for n in near_cells(c) for b in blocks_of(times_t(take(present[n], 2), g))]
        rows = [key_places(c).index(key) for key in keys]
        seen = [seen_ref[c, n : n + 1, :width] > 0 for n in rows]
        top = top_of(scores, seen)
        exps = weights(scores, seen, top)
        total = sum_of(exps)
        product = sum_of([e * d for e, d in zip(exps, dprobs)])
        if c == DONE:
            inverse = 1.0 / total
            delta = product * inverse
            terms = []
            for n, (weight, term) in enumerate(zip(exps, dprobs)):
                probs = weight * inverse
                terms.append((probs * (term - delta)).astype(jnp.bfloat16))
                done_ref[0, 128 * n : 128 * (n + 1)] = probs.astype(jnp.bfloat16)
                done_ref[1, 128 * n : 128 * (n + 1)] = terms[n]
            query_ref[...] = query_grad(take(key_places(c), 1), jnp.concatenate(terms, axis=0))
            rows = slice(256 * near_cells(c).index(c ^ 3), 256 * near_cells(c).index(c ^ 3) + 256)
            partial_ref[0] = jnp.dot(done_ref[0, rows], g, preferred_element_type=jnp.float32)
            partial_ref[1] = jnp.dot(done_ref[1, rows], q, preferred_element_type=jnp.float32)
            continue
        for key, weight, term in zip(keys, exps, dprobs):
            row = 128 * key_places(c).index(key)
            exps_ref[c, row : row + 128, :width] = weight
            dprobs_ref[c, row : row + 128, :width] = term
        stats_ref[c, 0:1, :width] = top
        stats_ref[c, 1:2, :width] = total
        stats_ref[c, 2:3, :width] = product


def taker(slab, stack_ref):
    def take(places, n):
        columns = slice(n * HEAD_DIM, (n + 1) * HEAD_DIM)
        parts = [slab[:, columns] if p == LATE else stack_ref[p, :, columns] for p in places]
        return jnp.concatenate(parts, axis=0)

    return take


def put(out, n, value):
    out[:, n * HEAD_DIM : (n + 1) * HEAD_DIM] = value.astype(jnp.bfloat16)


def put_pair_grads(take, c, probs_low, dscores, outs, partial=None):
    places = key_places(c)[: dscores.shape[1] // 128]
    dk = jnp.dot(dscores, take(places, 0), preferred_element_type=jnp.float32)
    dv = jnp.dot(probs_low, take(places, 3), preferred_element_type=jnp.float32)
    if partial is not None:
        dv, dk = dv + partial[0], dk + partial[1]
    dk = dk * (1.0 / math.sqrt(HEAD_DIM))
    for a, out in enumerate(outs):
        put(out, 1, dk[128 * a : 128 * (a + 1)])
        put(out, 2, dv[128 * a : 128 * (a + 1)])


def late_kernel(slab, *refs):
    seen_ref, stack_ref, exps_ref, dprobs_ref, stats_ref, partial_ref = refs[:6]
    outs = dict(zip(BEYOND, refs[6:10]))
    tiles_out, rows_out = refs[10:]
    cells = stack_ref.shape[0] // 2
    take = taker(slab, stack_ref)

    units = [(c, (2 * c, 2 * c + 1)) for c in range(cells) if c not in (DONE, LATE // 2)]
    units = [(LATE // 2, (place,)) for place in (LATE - 1, LATE)] + units
    fresh = [[p for p in key_places(c) if LATE in (p, *queries)] for c, queries in units]
    scores, dprobs, exps, inverse, delta, early_inverse = ([None] * len(units) for _ in range(6))
    for u, (c, queries) in enumerate(units):
        groups = [(LATE,)] if LATE not in queries else [(2 * n, 2 * n + 1) for n in near_cells(c)]
        groups = groups if fresh[u] else []
        mine_q, mine_g = take(queries, 0), take(queries, 3)
        scores[u] = [b for keys in groups for b in blocks_of(times_t(take(keys, 1), mine_q))]
        dprobs[u] = [b for keys in groups for b in blocks_of(times_t(take(keys, 2), mine_g))]
    seen = []
    for (c, queries), keys in zip(units, fresh):
        first = 128 * (queries[0] - 2 * c)
        columns = slice(first, first + 128 * len(queries))
        rows = [key_places(c).index(key) for key in keys]
        seen.append([seen_ref[c, n : n + 1, columns] > 0 for n in rows])
    tops = [top_of(blocks, flags) if blocks else None for blocks, flags in zip(scores, seen)]
    for u, (c, queries) in enumerate(units):
        early = LATE not in queries
        if early:
            top, total, product = (
                stats_ref[c, n : n + 1, : 128 * len(queries)] for n in range(3)
            )
        shrink = None
        if fresh[u]:
            new_top = jnp.maximum(top, tops[u]) if early else tops[u]
            exps[u] = weights(scores[u], seen[u], new_top)
            new_total = sum_of(exps[u])
            new_product = sum_of([e * d for e, d in zip(exps[u], dprobs[u])])
            if early:
                shrink = jnp.exp2(top - new_top)
                new_total = new_total + total * shrink
                new_product = new_product + product * shrink
            total, product = new_total, new_product
        inverse[u] = 1.0 / total
        delta[u] = product * inverse[u]
        early_inverse[u] = inverse[u] if shrink is None else inverse[u] * shrink

    def finished(u, n):
        c, queries = units[u]
        low, terms = [], []
        for key in (2 * n, 2 * n + 1):
            if key in fresh[u]:
                index = fresh[u].index(key)
                probs, dprob = exps[u][index] * inverse[u], dprobs[u][index]
            else:
                row = 128 * key_places(c).index(key)
                place = (c, slice(row, row + 128), slice(0, 128 * len(queries)))
                probs, dprob = exps_ref[place] * early_inverse[u], dprobs_ref[place]
            low.append(probs.astype(jnp.bfloat16))
            terms.append((probs * (dprob - delta[u])).astype(jnp.bfloat16))
        return jnp.concatenate(low, axis=0), jnp.concatenate(terms, axis=0)

    tiles = {}
    for c in (LATE // 2, OTHER, LATE // 2 ^ 1):
        for n in near_cells(c):
            if c < 2 and n < 2:
                continue
            if c == LATE // 2:
                sides = zip(finished(0, n), finished(1, n))
                tiles[n, c] = [jnp.concatenate(both, axis=1) for both in sides]
            else:
                tiles[n, c] = finished(units.index((c, (2 * c, 2 * c + 1))), n)
    for c in (2, 3):
        near = [m for m in near_cells(c) if m != DONE]
        pair = [jnp.concatenate([tiles[c, m][i] for m in near], axis=1) for i in range(2)]
        partial = partial_ref if len(near) < 3 else None
        put_pair_grads(take, c, *pair, [outs[2 * c], outs[2 * c + 1]], partial)
    for c in (2, 3):
        terms = jnp.concatenate([tiles[n, c][1] for n in near_cells(c)], axis=0)
        dq = query_grad(take(key_places(c), 1), terms)
        for a in range(2):
            put(outs[2 * c + a], 0, dq[a])
    for i in range(2):
        for n in (0, 1):
            tiles_out[i, n] = tiles[n, n ^ 3][i]
    tiles_out[1, 2] = tiles[OTHER ^ 3, OTHER][1]
    u = units.index((OTHER, (2 * OTHER, 2 * OTHER + 1)))
    rows_out[0:1] = early_inverse[u]
    rows_out[1:2] = delta[u]


def rest_kernel(distances, slab, *refs):
    stack_ref, exps_ref, dprobs_ref, done_ref, query_ref, tiles_ref, rows_ref = refs[:7]
    kept, outs, out_ref = refs[7:9], refs[9:-1], refs[-1]
    here = flat_index(GROUP)
    fixed = [distance(here) for distance in distances]
    fixed = {place: out for place, out in zip(fixed, outs) if isinstance(place, int)}
    take = taker(slab, stack_ref)
    tiles = {(n, n ^ 3): [tiles_ref[i, n] for i in range(2)] for n in (0, 1)}
    for n in (0, 1):
        rows = [slice(256 * near_cells(c).index(n), 256 * (near_cells(c).index(n) + 1)) for c in (DONE, OTHER)]
        tiles[n, DONE] = [done_ref[i, rows[0]] for i in range(2)]
        probs = exps_ref[OTHER, rows[1]] * rows_ref[0:1]
        terms = probs * (dprobs_ref[OTHER, rows[1]] - rows_ref[1:2])
        tiles[n, OTHER] = [probs.astype(jnp.bfloat16), terms.astype(jnp.bfloat16)]
    terms = [tiles_ref[1, 2] if n > 1 else tiles[n, OTHER][1] for n in near_cells(OTHER)]
    other_query = query_grad(take(key_places(OTHER), 1), jnp.concatenate(terms, axis=0))
    for c in (0, 1):
        targets = [fixed.get(place, out_ref.at[place]) for place in (2 * c, 2 * c + 1)]
        pair = [jnp.concatenate([tiles[c, m][i] for m in near_cells(c)], axis=1) for i in range(2)]
        put_pair_grads(take, c, *pair, targets)
        for a, target in enumerate(targets):
            put(target, 0, query_ref[a] if c == DONE else other_query[a])
    for place, ref in zip((4, 6), kept):
        out_ref[place] = ref[...]
    for distance, out in zip(distances, outs):
        if not isinstance(distance(here), int):
            out[...] = out_ref[distance(here)]


SMEM = pl.BlockSpec(memory_space=pltpu.SMEM)
VMEM = pl.BlockSpec(memory_space=pltpu.VMEM)
ANY = pl.BlockSpec(memory_space=pl.ANY)


def slab_shape(tokens, parts):
    return jax.ShapeDtypeStruct((tokens, parts * HEAD_DIM), jnp.bfloat16)


def pack(arrays, distances, name, *extras):
    tokens = arrays[0].shape[0]
    count = len(distances)
    outs = [slab_shape(tokens, 4)] * count
    outs += [jax.ShapeDtypeStruct(extra.shape, extra.dtype) for extra in extras]
    return pl.pallas_call(
        functools.partial(pack_kernel, distances),
        out_shape=outs,
        in_specs=[ANY] * (4 + len(extras)),
        out_specs=[ANY] * len(outs),
        scratch_shapes=[pltpu.SemaphoreType.DMA((4 * count + len(extras),))],
        compiler_params=pltpu.CompilerParams(vmem_limit_bytes=MIB),
        name=name,
    )(*arrays, *extras)


def unpack(whole, distances, slabs, name, *arrays):
    count = len(distances)
    return pl.pallas_call(
        functools.partial(unpack_kernel, distances),
        out_shape=[whole] * 3,
        in_specs=[ANY] * (count + len(arrays)),
        out_specs=[ANY] * 3,
        scratch_shapes=[pltpu.SemaphoreType.DMA((3 * count,))],
        compiler_params=pltpu.CompilerParams(vmem_limit_bytes=MIB),
        input_output_aliases={count + n: n for n in range(len(arrays))},
        name=name,
    )(*slabs, *arrays)


def by_heads(queries, keys, values, out_grad, block_mask):
    devices = lax.axis_size(GROUP)
    cells = lax.axis_size("blk")
    tokens = queries.shape[0]
    *arrays, block_mask = [
        pltpu.with_memory_space_constraint(array, pltpu.HBM)
        for array in (queries, keys, values, out_grad, block_mask)
    ]
    sent = pack(arrays, INWARD[:FIRST], "pack_first")
    arrays, sent = lax.optimization_barrier((arrays, sent))
    *rest, own, block_mask = pack(arrays, INWARD[FIRST:] + (STAY,), "pack_rest", block_mask)
    got = list(sent) + rest
    for n, distance in enumerate(INWARD):
        if n in AFTER:
            got[n], got[AFTER[n]] = lax.optimization_barrier((got[n], got[AFTER[n]]))
        got[n] = exchange(got[n], distance)
    soon = [n for n, distance in enumerate(INWARD) if distance is not LATE_HOP]
    seen = pl.pallas_call(
        seen_kernel,
        out_shape=jax.ShapeDtypeStruct((cells, 8, 2 * tokens), jnp.float32),
        in_specs=[SMEM],
        out_specs=VMEM,
        compiler_params=pltpu.CompilerParams(vmem_limit_bytes=MIB),
        name="seen",
    )(block_mask)
    pairs = jax.ShapeDtypeStruct((cells, 6 * tokens, 2 * tokens), jnp.float32)
    partial = pl.pallas_call(
        functools.partial(early_kernel, [INWARD[n] for n in soon] + [STAY]),
        out_shape=[
            jax.ShapeDtypeStruct((devices, tokens, 4 * HEAD_DIM), jnp.bfloat16),
            pairs,
            pairs,
            jax.ShapeDtypeStruct((cells, 8, 2 * tokens), jnp.float32),
            jax.ShapeDtypeStruct((2, 6 * tokens, 2 * tokens), jnp.bfloat16),
            jax.ShapeDtypeStruct((2, tokens, HEAD_DIM), jnp.bfloat16),
            jax.ShapeDtypeStruct((2, 2 * tokens, HEAD_DIM), jnp.float32),
        ],
        in_specs=[VMEM] * devices,
        out_specs=[VMEM] * 7,
        compiler_params=pltpu.CompilerParams(vmem_limit_bytes=24 * MIB),
        name="early",
    )(seen, *[got[n] for n in soon], own)
    stack, exps, dprobs, stats, done, done_query, done_part = partial
    slab = got[INWARD.index(LATE_HOP)]
    *beyond, tiles, rows = pl.pallas_call(
        late_kernel,
        out_shape=[slab_shape(tokens, 3)] * len(BEYOND)
        + [
            jax.ShapeDtypeStruct((2, 3, 2 * tokens, 2 * tokens), jnp.bfloat16),
            jax.ShapeDtypeStruct((8, 2 * tokens), jnp.float32),
        ],
        in_specs=[VMEM] * 7,
        out_specs=[VMEM] * (len(BEYOND) + 2),
        compiler_params=pltpu.CompilerParams(vmem_limit_bytes=24 * MIB),
        name="late",
    )(slab, seen, stack, exps, dprobs, stats, done_part)
    beyond = dict(zip(BEYOND, beyond))
    distances = OUTWARD + (STAY,)
    rest = pl.pallas_call(
        functools.partial(rest_kernel, distances[2:]),
        out_shape=[slab_shape(tokens, 3)] * (devices - 2),
        in_specs=[VMEM] * 10,
        out_specs=[VMEM] * (devices - 2),
        scratch_shapes=[pltpu.VMEM((devices, tokens, 3 * HEAD_DIM), jnp.bfloat16)],
        compiler_params=pltpu.CompilerParams(vmem_limit_bytes=24 * MIB),
        name="rest",
    )(slab, stack, exps, dprobs, done, done_query, tiles, rows, beyond[4], beyond[6])
    grads = [beyond[5], beyond[7], *rest]
    back = [exchange(grad, distance) for grad, distance in zip(grads, OUTWARD)] + [grads[-1]]
    whole = jax.ShapeDtypeStruct(queries.shape, queries.dtype)
    grads = []
    for number, group in enumerate(UNPACKED):
        hops = [distances[n] for n in group]
        grads = unpack(whole, hops, [back[n] for n in group], f"unpack_{number}", *grads)
    return grads


def local(queries, keys, values, out_grad, block_mask):
    heads = queries.shape[1] // HEAD_DIM
    cells, halves = lax.axis_size("blk"), lax.axis_size("uly")
    if (cells, halves) == (4, 2) and heads == cells * halves and queries.shape[0] == 128:
        return by_heads(queries, keys, values, out_grad, block_mask)
    return by_cells(queries, keys, values, out_grad, block_mask)


def solution(mesh):
    return jax.shard_map(
        local,
        mesh=mesh,
        in_specs=(
            P(("batch", "blk", "uly"), None),
            P(("batch", "blk", "uly"), None),
            P(("batch", "blk", "uly"), None),
            P(("batch", "blk", "uly"), None),
            P("batch", None),
        ),
        out_specs=(
            P(("batch", "blk", "uly"), None),
            P(("batch", "blk", "uly"), None),
            P(("batch", "blk", "uly"), None),
        ),
        check_vma=False,
    )
```

```python
import functools
import math

import jax
import jax.numpy as jnp
from jax import lax
from jax.experimental import pallas as pl
from jax.experimental.pallas import tpu as pltpu
from jax.sharding import PartitionSpec as P

HEAD_DIM = 128
MIB = 1024 * 1024
GROUP = ("blk", "uly")


def padded(block, sides, width):
    for axis, dim in sides:
        count = lax.axis_size(axis)
        forward = [(i, i + 1) for i in range(count - 1)]
        forward.append((count - 1, 0))
        backward = [(target, source) for source, target in forward]
        low = lax.ppermute(
            lax.slice_in_dim(block, block.shape[dim] - width, None, axis=dim), axis, forward
        )
        high = lax.ppermute(lax.slice_in_dim(block, 0, width, axis=dim), axis, backward)
        block = jnp.concatenate([low, block, high], axis=dim)
    return block


def passed_along(block, axis, distance):
    devices = range(lax.axis_size(axis))
    route = [((i - distance) % len(devices), i) for i in devices]
    return lax.ppermute(block, axis, route)


def times_t(left, right):
    return lax.dot_general(
        left, right, (((1,), (1,)), ((), ())), preferred_element_type=jnp.float32
    )


def t_times(left, right):
    return lax.dot_general(
        left, right, (((0,), (0,)), ((), ())), preferred_element_type=jnp.float32
    )


def widen_blocks(mask_blocks):
    return jnp.repeat(jnp.repeat(mask_blocks > 0, 128, axis=0), 128, axis=1)


def by_cells(queries, keys, values, out_grad, block_mask):
    local_q, local_k, local_v, local_g = (
        lax.all_to_all(queries, "uly", split_axis=1, concat_axis=0, tiled=True),
        lax.all_to_all(keys, "uly", split_axis=1, concat_axis=0, tiled=True),
        lax.all_to_all(values, "uly", split_axis=1, concat_axis=0, tiled=True),
        lax.all_to_all(out_grad, "uly", split_axis=1, concat_axis=0, tiled=True),
    )
    genes = local_q.shape[0]
    heads_here = local_q.shape[1] // HEAD_DIM
    scale = 1.0 / math.sqrt(HEAD_DIM)
    cells = lax.axis_size("blk")
    here = lax.axis_index("blk")
    per_cell = genes // 128
    near = (here + jnp.array([-1, 0, 1], dtype=jnp.int32) + cells) % cells
    mask_rows = lax.dynamic_slice_in_dim(block_mask, here * per_cell, per_cell, 0).reshape(
        per_cell, cells, per_cell
    )
    row_mask = widen_blocks(jnp.take(mask_rows, near, axis=1).reshape(per_cell, 3 * per_cell))
    pairs = jnp.stack([local_k, local_v], axis=1)
    band = padded(pairs, (("blk", 0),), genes)
    q_grads = []
    k_parts = []
    v_parts = []
    for head in range(heads_here):
        lower = head * HEAD_DIM
        upper = lower + HEAD_DIM
        q_head = local_q[:, lower:upper]
        g_head = local_g[:, lower:upper]
        k_band = band[:, 0, lower:upper]
        v_band = band[:, 1, lower:upper]
        scores = jnp.where(row_mask, times_t(q_head, k_band) * scale, -1e30)
        top = jnp.max(scores, axis=1, keepdims=True)
        total = jnp.sum(jnp.where(row_mask, jnp.exp(scores - top), 0.0), axis=1, keepdims=True)
        lse = top + jnp.log(total)
        probs = jnp.where(row_mask, jnp.exp(scores - lse), 0.0)
        dprobs = times_t(g_head, v_band)
        delta = jnp.sum(probs * dprobs, axis=1, keepdims=True)
        dscores = (probs * (dprobs - delta)).astype(jnp.bfloat16)
        q_grads.append(
            (jnp.dot(dscores, k_band, preferred_element_type=jnp.float32) * scale).astype(
                jnp.bfloat16
            )
        )
        k_parts.append(t_times(dscores, q_head))
        v_parts.append(t_times(probs.astype(jnp.bfloat16), g_head))
    query_grad = jnp.concatenate(q_grads, axis=1)
    partial_terms = jnp.stack(
        [jnp.concatenate(k_parts, axis=1), jnp.concatenate(v_parts, axis=1)], axis=1
    )
    from_next = passed_along(partial_terms[:genes].astype(jnp.bfloat16), "blk", -1).astype(
        jnp.float32
    )
    from_prior = passed_along(partial_terms[2 * genes :].astype(jnp.bfloat16), "blk", 1).astype(
        jnp.float32
    )
    summed = partial_terms[genes : 2 * genes] + from_next + from_prior
    key_grad = (summed[:, 0] * scale).astype(jnp.bfloat16)
    value_grad = summed[:, 1].astype(jnp.bfloat16)
    return (
        lax.all_to_all(query_grad, "uly", split_axis=0, concat_axis=1, tiled=True),
        lax.all_to_all(key_grad, "uly", split_axis=0, concat_axis=1, tiled=True),
        lax.all_to_all(value_grad, "uly", split_axis=0, concat_axis=1, tiled=True),
    )


def flat_index(axes):
    index = 0
    for axis in axes:
        index = index * lax.axis_size(axis) + lax.axis_index(axis)
    return index


def same_core(here):
    return (here >> 1) & 1


def even_places(here):
    return (here ^ (here >> 1) ^ (here >> 2)) & 1


def hop(first, second=None, chooser=same_core):
    if second is None:
        return lambda here: first
    return lambda here: first + (second - first) * chooser(here)


STAY = hop(0)
CORE = hop(2)
FAR = hop(5)
FAR_CORE = hop(7)
SIDE = hop(4, 1)
OTHER_SIDE = hop(1, 4)
SIDE_CORE = hop(6, 3, even_places)
OTHER_SIDE_CORE = hop(3, 6, even_places)

INWARD = (FAR, SIDE_CORE, CORE, SIDE, OTHER_SIDE, OTHER_SIDE_CORE, FAR_CORE)
OUTWARD = (FAR, FAR_CORE, SIDE, OTHER_SIDE, OTHER_SIDE_CORE, SIDE_CORE, CORE)
FIRST = 2
UNPACKED = ((-1, 0, 1), (2, 3), (4, 5, 6))
LATE_HOP = FAR_CORE
LATE = 7
BEYOND = (4, 5, 6, 7)
DONE = 1
OTHER = 0
AFTER = {}
EXPONENT = math.log2(math.e) / math.sqrt(HEAD_DIM)


def exchange(block, distance):
    places = range(lax.axis_size(GROUP))
    return lax.ppermute(block, GROUP, [(i, i ^ distance(i)) for i in places])


def part(ref, n):
    return ref.at[:, n * HEAD_DIM : (n + 1) * HEAD_DIM]


def head_of(ref, head):
    return ref.at[:, pl.ds(pl.multiple_of(head * HEAD_DIM, HEAD_DIM), HEAD_DIM)]


def run(copies):
    for copy in copies:
        copy.start()
    for copy in copies:
        copy.wait()


def pack_kernel(distances, *refs):
    count = len(distances)
    extras = (len(refs) - 1 - count - 4) // 2
    sources, outs, sems = refs[: 4 + extras], refs[4 + extras : -1], refs[-1]
    here = flat_index(GROUP)
    pairs = list(zip(sources[4:], outs[count:]))
    for distance, slab in zip(distances, outs):
        for n, array in enumerate(sources[:4]):
            pairs.append((head_of(array, here ^ distance(here)), part(slab, n)))
    run([pltpu.make_async_copy(*pair, sems.at[n]) for n, pair in enumerate(pairs)])


def unpack_kernel(distances, *refs):
    slabs, arrays, sems = refs[: len(distances)], refs[-4:-1], refs[-1]
    here = flat_index(GROUP)
    pairs = []
    for distance, slab in zip(distances, slabs):
        for n, array in enumerate(arrays):
            pairs.append((part(slab, n), head_of(array, here ^ distance(here))))
    run([pltpu.make_async_copy(*pair, sems.at[n]) for n, pair in enumerate(pairs)])


def near_cells(c):
    return (c, c ^ 1, c ^ 3)


def key_places(c):
    return [2 * n + a for n in near_cells(c) for a in range(2)]


def blocks_of(value):
    return [value[r : r + 128] for r in range(0, value.shape[0], 128)]


def seen_by(mask_ref, here, key, queries):
    flags = [jnp.full((1, 128), mask_ref[here ^ query, here ^ key]) for query in queries]
    return jnp.concatenate(flags, axis=1) > 0


def weights(scores, seen, top):
    return [
        jnp.exp2(block * EXPONENT - jnp.where(flag, top, 1e30)) for block, flag in zip(scores, seen)
    ]


def top_of(scores, seen):
    top = jnp.full((1, scores[0].shape[1]), -1e30, jnp.float32)
    for block, flag in zip(scores, seen):
        top = jnp.maximum(top, jnp.where(flag, jnp.max(block, axis=0, keepdims=True), -1e30))
    return top * EXPONENT


def sum_of(blocks):
    total = blocks[0]
    for block in blocks[1:]:
        total = total + block
    return jnp.sum(total, axis=0, keepdims=True)


def query_grad(keys, dscores):
    low = (t_times(keys, dscores) * (1.0 / math.sqrt(HEAD_DIM))).T.astype(jnp.bfloat16)
    return low.reshape(-1, 128, HEAD_DIM)


def seen_kernel(mask_ref, seen_ref):
    here = flat_index(GROUP)
    for c in range(seen_ref.shape[0]):
        for n, key in enumerate(key_places(c)):
            flags = seen_by(mask_ref, here, key, (2 * c, 2 * c + 1))
            seen_ref[c, n : n + 1] = flags.astype(jnp.float32)


def early_kernel(distances, seen_ref, *refs):
    slabs, outs = refs[:-7], refs[-7:]
    stack_ref, exps_ref, dprobs_ref, stats_ref, done_ref, query_ref, partial_ref = outs
    here = flat_index(GROUP)
    for distance, slab in zip(distances, slabs):
        stack_ref[distance(here)] = slab[...]

    def take(places, n):
        columns = slice(n * HEAD_DIM, (n + 1) * HEAD_DIM)
        return jnp.concatenate([stack_ref[place, :, columns] for place in places], axis=0)

    cells = stack_ref.shape[0] // 2
    present = [[p for p in (2 * c, 2 * c + 1) if p != LATE] for c in range(cells)]
    for c in range(cells):
        q, g = take(present[c], 0), take(present[c], 3)
        width = q.shape[0]
        keys = [place for place in key_places(c) if place != LATE]
        scores = [b for n in near_cells(c) for b in blocks_of(times_t(take(present[n], 1), q))]
        dprobs = [b for n in near_cells(c) for b in blocks_of(times_t(take(present[n], 2), g))]
        rows = [key_places(c).index(key) for key in keys]
        seen = [seen_ref[c, n : n + 1, :width] > 0 for n in rows]
        top = top_of(scores, seen)
        exps = weights(scores, seen, top)
        total = sum_of(exps)
        product = sum_of([e * d for e, d in zip(exps, dprobs)])
        if c == DONE:
            inverse = 1.0 / total
            delta = product * inverse
            terms = []
            for n, (weight, term) in enumerate(zip(exps, dprobs)):
                probs = weight * inverse
                terms.append((probs * (term - delta)).astype(jnp.bfloat16))
                done_ref[0, 128 * n : 128 * (n + 1)] = probs.astype(jnp.bfloat16)
                done_ref[1, 128 * n : 128 * (n + 1)] = terms[n]
            query_ref[...] = query_grad(take(key_places(c), 1), jnp.concatenate(terms, axis=0))
            rows = slice(256 * near_cells(c).index(c ^ 3), 256 * near_cells(c).index(c ^ 3) + 256)
            partial_ref[0] = jnp.dot(done_ref[0, rows], g, preferred_element_type=jnp.float32)
            partial_ref[1] = jnp.dot(done_ref[1, rows], q, preferred_element_type=jnp.float32)
            continue
        for key, weight, term in zip(keys, exps, dprobs):
            row = 128 * key_places(c).index(key)
            exps_ref[c, row : row + 128, :width] = weight
            dprobs_ref[c, row : row + 128, :width] = term
        stats_ref[c, 0:1, :width] = top
        stats_ref[c, 1:2, :width] = total
        stats_ref[c, 2:3, :width] = product


def taker(slab, stack_ref):
    def take(places, n):
        columns = slice(n * HEAD_DIM, (n + 1) * HEAD_DIM)
        parts = [slab[:, columns] if p == LATE else stack_ref[p, :, columns] for p in places]
        return jnp.concatenate(parts, axis=0)

    return take


def put(out, n, value):
    out[:, n * HEAD_DIM : (n + 1) * HEAD_DIM] = value.astype(jnp.bfloat16)


def put_pair_grads(take, c, probs_low, dscores, outs, partial=None):
    places = key_places(c)[: dscores.shape[1] // 128]
    dk = jnp.dot(dscores, take(places, 0), preferred_element_type=jnp.float32)
    dv = jnp.dot(probs_low, take(places, 3), preferred_element_type=jnp.float32)
    if partial is not None:
        dv, dk = dv + partial[0], dk + partial[1]
    dk = dk * (1.0 / math.sqrt(HEAD_DIM))
    for a, out in enumerate(outs):
        put(out, 1, dk[128 * a : 128 * (a + 1)])
        put(out, 2, dv[128 * a : 128 * (a + 1)])


def late_kernel(slab, *refs):
    seen_ref, stack_ref, exps_ref, dprobs_ref, stats_ref, partial_ref = refs[:6]
    outs = dict(zip(BEYOND, refs[6:10]))
    tiles_out, rows_out = refs[10:]
    cells = stack_ref.shape[0] // 2
    take = taker(slab, stack_ref)

    units = [(c, (2 * c, 2 * c + 1)) for c in range(cells) if c not in (DONE, LATE // 2)]
    units = [(LATE // 2, (place,)) for place in (LATE - 1, LATE)] + units
    fresh = [[p for p in key_places(c) if LATE in (p, *queries)] for c, queries in units]
    scores, dprobs, exps, inverse, delta, early_inverse = ([None] * len(units) for _ in range(6))
    for u, (c, queries) in enumerate(units):
        groups = [(LATE,)] if LATE not in queries else [(2 * n, 2 * n + 1) for n in near_cells(c)]
        groups = groups if fresh[u] else []
        mine_q, mine_g = take(queries, 0), take(queries, 3)
        scores[u] = [b for keys in groups for b in blocks_of(times_t(take(keys, 1), mine_q))]
        dprobs[u] = [b for keys in groups for b in blocks_of(times_t(take(keys, 2), mine_g))]
    seen = []
    for (c, queries), keys in zip(units, fresh):
        first = 128 * (queries[0] - 2 * c)
        columns = slice(first, first + 128 * len(queries))
        rows = [key_places(c).index(key) for key in keys]
        seen.append([seen_ref[c, n : n + 1, columns] > 0 for n in rows])
    tops = [top_of(blocks, flags) if blocks else None for blocks, flags in zip(scores, seen)]
    for u, (c, queries) in enumerate(units):
        early = LATE not in queries
        if early:
            top, total, product = (
                stats_ref[c, n : n + 1, : 128 * len(queries)] for n in range(3)
            )
        shrink = None
        if fresh[u]:
            new_top = jnp.maximum(top, tops[u]) if early else tops[u]
            exps[u] = weights(scores[u], seen[u], new_top)
            new_total = sum_of(exps[u])
            new_product = sum_of([e * d for e, d in zip(exps[u], dprobs[u])])
            if early:
                shrink = jnp.exp2(top - new_top)
                new_total = new_total + total * shrink
                new_product = new_product + product * shrink
            total, product = new_total, new_product
        inverse[u] = 1.0 / total
        delta[u] = product * inverse[u]
        early_inverse[u] = inverse[u] if shrink is None else inverse[u] * shrink

    def finished(u, n):
        c, queries = units[u]
        low, terms = [], []
        for key in (2 * n, 2 * n + 1):
            if key in fresh[u]:
                index = fresh[u].index(key)
                probs, dprob = exps[u][index] * inverse[u], dprobs[u][index]
            else:
                row = 128 * key_places(c).index(key)
                place = (c, slice(row, row + 128), slice(0, 128 * len(queries)))
                probs, dprob = exps_ref[place] * early_inverse[u], dprobs_ref[place]
            low.append(probs.astype(jnp.bfloat16))
            terms.append((probs * (dprob - delta[u])).astype(jnp.bfloat16))
        return jnp.concatenate(low, axis=0), jnp.concatenate(terms, axis=0)

    tiles = {}
    for c in (LATE // 2, OTHER, LATE // 2 ^ 1):
        for n in near_cells(c):
            if c < 2 and n < 2:
                continue
            if c == LATE // 2:
                sides = zip(finished(0, n), finished(1, n))
                tiles[n, c] = [jnp.concatenate(both, axis=1) for both in sides]
            else:
                tiles[n, c] = finished(units.index((c, (2 * c, 2 * c + 1))), n)
    for c in (2, 3):
        near = [m for m in near_cells(c) if m != DONE]
        pair = [jnp.concatenate([tiles[c, m][i] for m in near], axis=1) for i in range(2)]
        partial = partial_ref if len(near) < 3 else None
        put_pair_grads(take, c, *pair, [outs[2 * c], outs[2 * c + 1]], partial)
    for c in (2, 3):
        terms = jnp.concatenate([tiles[n, c][1] for n in near_cells(c)], axis=0)
        dq = query_grad(take(key_places(c), 1), terms)
        for a in range(2):
            put(outs[2 * c + a], 0, dq[a])
    for i in range(2):
        for n in (0, 1):
            tiles_out[i, n] = tiles[n, n ^ 3][i]
    tiles_out[1, 2] = tiles[OTHER ^ 3, OTHER][1]
    u = units.index((OTHER, (2 * OTHER, 2 * OTHER + 1)))
    rows_out[0:1] = early_inverse[u]
    rows_out[1:2] = delta[u]


def rest_kernel(distances, slab, *refs):
    stack_ref, exps_ref, dprobs_ref, done_ref, query_ref, tiles_ref, rows_ref = refs[:7]
    kept, outs, out_ref = refs[7:9], refs[9:-1], refs[-1]
    here = flat_index(GROUP)
    fixed = [distance(here) for distance in distances]
    fixed = {place: out for place, out in zip(fixed, outs) if isinstance(place, int)}
    take = taker(slab, stack_ref)
    tiles = {(n, n ^ 3): [tiles_ref[i, n] for i in range(2)] for n in (0, 1)}
    for n in (0, 1):
        rows = [slice(256 * near_cells(c).index(n), 256 * (near_cells(c).index(n) + 1)) for c in (DONE, OTHER)]
        tiles[n, DONE] = [done_ref[i, rows[0]] for i in range(2)]
        probs = exps_ref[OTHER, rows[1]] * rows_ref[0:1]
        terms = probs * (dprobs_ref[OTHER, rows[1]] - rows_ref[1:2])
        tiles[n, OTHER] = [probs.astype(jnp.bfloat16), terms.astype(jnp.bfloat16)]
    terms = [tiles_ref[1, 2] if n > 1 else tiles[n, OTHER][1] for n in near_cells(OTHER)]
    other_query = query_grad(take(key_places(OTHER), 1), jnp.concatenate(terms, axis=0))
    for c in (0, 1):
        targets = [fixed.get(place, out_ref.at[place]) for place in (2 * c, 2 * c + 1)]
        pair = [jnp.concatenate([tiles[c, m][i] for m in near_cells(c)], axis=1) for i in range(2)]
        put_pair_grads(take, c, *pair, targets)
        for a, target in enumerate(targets):
            put(target, 0, query_ref[a] if c == DONE else other_query[a])
    for place, ref in zip((4, 6), kept):
        out_ref[place] = ref[...]
    for distance, out in zip(distances, outs):
        if not isinstance(distance(here), int):
            out[...] = out_ref[distance(here)]


SMEM = pl.BlockSpec(memory_space=pltpu.SMEM)
VMEM = pl.BlockSpec(memory_space=pltpu.VMEM)
ANY = pl.BlockSpec(memory_space=pl.ANY)


def slab_shape(tokens, parts):
    return jax.ShapeDtypeStruct((tokens, parts * HEAD_DIM), jnp.bfloat16)


def pack(arrays, distances, name, *extras):
    tokens = arrays[0].shape[0]
    count = len(distances)
    outs = [slab_shape(tokens, 4)] * count
    outs += [jax.ShapeDtypeStruct(extra.shape, extra.dtype) for extra in extras]
    return pl.pallas_call(
        functools.partial(pack_kernel, distances),
        out_shape=outs,
        in_specs=[ANY] * (4 + len(extras)),
        out_specs=[ANY] * len(outs),
        scratch_shapes=[pltpu.SemaphoreType.DMA((4 * count + len(extras),))],
        compiler_params=pltpu.CompilerParams(vmem_limit_bytes=MIB),
        name=name,
    )(*arrays, *extras)


def unpack(whole, distances, slabs, name, *arrays):
    count = len(distances)
    return pl.pallas_call(
        functools.partial(unpack_kernel, distances),
        out_shape=[whole] * 3,
        in_specs=[ANY] * (count + len(arrays)),
        out_specs=[ANY] * 3,
        scratch_shapes=[pltpu.SemaphoreType.DMA((3 * count,))],
        compiler_params=pltpu.CompilerParams(vmem_limit_bytes=MIB),
        input_output_aliases={count + n: n for n in range(len(arrays))},
        name=name,
    )(*slabs, *arrays)


def by_heads(queries, keys, values, out_grad, block_mask):
    devices = lax.axis_size(GROUP)
    cells = lax.axis_size("blk")
    tokens = queries.shape[0]
    *arrays, block_mask = [
        pltpu.with_memory_space_constraint(array, pltpu.HBM)
        for array in (queries, keys, values, out_grad, block_mask)
    ]
    sent = pack(arrays, INWARD[:FIRST], "pack_first")
    arrays, sent = lax.optimization_barrier((arrays, sent))
    *rest, own, block_mask = pack(arrays, INWARD[FIRST:] + (STAY,), "pack_rest", block_mask)
    got = list(sent) + rest
    for n, distance in enumerate(INWARD):
        if n in AFTER:
            got[n], got[AFTER[n]] = lax.optimization_barrier((got[n], got[AFTER[n]]))
        got[n] = exchange(got[n], distance)
    soon = [n for n, distance in enumerate(INWARD) if distance is not LATE_HOP]
    seen = pl.pallas_call(
        seen_kernel,
        out_shape=jax.ShapeDtypeStruct((cells, 8, 2 * tokens), jnp.float32),
        in_specs=[SMEM],
        out_specs=VMEM,
        compiler_params=pltpu.CompilerParams(vmem_limit_bytes=MIB),
        name="seen",
    )(block_mask)
    pairs = jax.ShapeDtypeStruct((cells, 6 * tokens, 2 * tokens), jnp.float32)
    partial = pl.pallas_call(
        functools.partial(early_kernel, [INWARD[n] for n in soon] + [STAY]),
        out_shape=[
            jax.ShapeDtypeStruct((devices, tokens, 4 * HEAD_DIM), jnp.bfloat16),
            pairs,
            pairs,
            jax.ShapeDtypeStruct((cells, 8, 2 * tokens), jnp.float32),
            jax.ShapeDtypeStruct((2, 6 * tokens, 2 * tokens), jnp.bfloat16),
            jax.ShapeDtypeStruct((2, tokens, HEAD_DIM), jnp.bfloat16),
            jax.ShapeDtypeStruct((2, 2 * tokens, HEAD_DIM), jnp.float32),
        ],
        in_specs=[VMEM] * devices,
        out_specs=[VMEM] * 7,
        compiler_params=pltpu.CompilerParams(vmem_limit_bytes=24 * MIB),
        name="early",
    )(seen, *[got[n] for n in soon], own)
    stack, exps, dprobs, stats, done, done_query, done_part = partial
    slab = got[INWARD.index(LATE_HOP)]
    *beyond, tiles, rows = pl.pallas_call(
        late_kernel,
        out_shape=[slab_shape(tokens, 3)] * len(BEYOND)
        + [
            jax.ShapeDtypeStruct((2, 3, 2 * tokens, 2 * tokens), jnp.bfloat16),
            jax.ShapeDtypeStruct((8, 2 * tokens), jnp.float32),
        ],
        in_specs=[VMEM] * 7,
        out_specs=[VMEM] * (len(BEYOND) + 2),
        compiler_params=pltpu.CompilerParams(vmem_limit_bytes=24 * MIB),
        name="late",
    )(slab, seen, stack, exps, dprobs, stats, done_part)
    beyond = dict(zip(BEYOND, beyond))
    distances = OUTWARD + (STAY,)
    rest = pl.pallas_call(
        functools.partial(rest_kernel, distances[2:]),
        out_shape=[slab_shape(tokens, 3)] * (devices - 2),
        in_specs=[VMEM] * 10,
        out_specs=[VMEM] * (devices - 2),
        scratch_shapes=[pltpu.VMEM((devices, tokens, 3 * HEAD_DIM), jnp.bfloat16)],
        compiler_params=pltpu.CompilerParams(vmem_limit_bytes=24 * MIB),
        name="rest",
    )(slab, stack, exps, dprobs, done, done_query, tiles, rows, beyond[4], beyond[6])
    grads = [beyond[5], beyond[7], *rest]
    back = [exchange(grad, distance) for grad, distance in zip(grads, OUTWARD)] + [grads[-1]]
    whole = jax.ShapeDtypeStruct(queries.shape, queries.dtype)
    grads = []
    for number, group in enumerate(UNPACKED):
        hops = [distances[n] for n in group]
        grads = unpack(whole, hops, [back[n] for n in group], f"unpack_{number}", *grads)
    return grads


def local(queries, keys, values, out_grad, block_mask):
    heads = queries.shape[1] // HEAD_DIM
    cells, halves = lax.axis_size("blk"), lax.axis_size("uly")
    if (cells, halves) == (4, 2) and heads == cells * halves and queries.shape[0] == 128:
        return by_heads(queries, keys, values, out_grad, block_mask)
    return by_cells(queries, keys, values, out_grad, block_mask)


def solution(mesh):
    return jax.shard_map(
        local,
        mesh=mesh,
        in_specs=(
            P(("batch", "blk", "uly"), None),
            P(("batch", "blk", "uly"), None),
            P(("batch", "blk", "uly"), None),
            P(("batch", "blk", "uly"), None),
            P("batch", None),
        ),
        out_specs=(
            P(("batch", "blk", "uly"), None),
            P(("batch", "blk", "uly"), None),
            P(("batch", "blk", "uly"), None),
        ),
        check_vma=False,
    )
```
